128 devices in a mesh: dp: 4 (over x), frame: 4 (over z), expert: 8 (over y, core).
Axes of the slice: x: 4, y: 4, z: 4, core: 2. Of those that a mesh axis runs over, the one named last changes fastest.
Arguments:
- queries: bfloat16 [16384, 2048], P(('dp', 'frame'), 'expert'), parts along dimension 0, may hold values from -8 to 8
- keys: bfloat16 [16384, 2048], P(('dp', 'frame'), 'expert'), parts along dimension 0, may hold values from -8 to 8
- values: bfloat16 [16384, 2048], P(('dp', 'frame'), 'expert'), parts along dimension 0, may hold values from -6 to 6
- hidden_state: bfloat16 [16384, 4096], P(('dp', 'frame', 'expert')), parts along dimension 0, may hold values from -60 to 60
- out_grad: bfloat16 [16384, 4096], P(('dp', 'frame', 'expert')), parts along dimension 0, may hold values from -6 to 6
- stored_pre: bfloat16 [16384, 2, 2, 2048], P(('dp', 'frame', 'expert')), parts along dimension 0, may hold values from -6 to 6
- expert_ids: int32 [16384, 2], P(('dp', 'frame', 'expert')), parts along dimension 0, may hold values from 0 to 7, as said below
- gate_weights: float32 [16384, 2], P(('dp', 'frame', 'expert')), parts along dimension 0, may hold values from 0.25 to 1
- w_gate: bfloat16 [8, 4096, 2048], P('expert', None, 'frame'), may hold values from -0.09375 to 0.09375
- w_up: bfloat16 [8, 4096, 2048], P('expert', None, 'frame'), may hold values from -0.09375 to 0.09375
- w_down: bfloat16 [8, 2048, 4096], P('expert', 'frame'), may hold values from -0.125 to 0.125
Outputs:
- residual_grad: bfloat16 [16384, 4096], P(('dp', 'frame', 'expert')), parts along dimension 0
- query_grad: bfloat16 [16384, 2048], P(('dp', 'frame'), 'expert'), parts along dimension 0
- key_grad: bfloat16 [16384, 2048], P(('dp', 'frame'), 'expert'), parts along dimension 0
- value_grad: bfloat16 [16384, 2048], P(('dp', 'frame'), 'expert'), parts along dimension 0
The draws below stay inside these ranges and needn't reach their ends.
There are 4 independent parts, one for each index of `dp`. The reference program is written for one: setup_inputs(seed, part) draws one part's arguments, and reference() takes and returns one part's arrays. A program takes and returns all parts, laid end to end along the dimension named above; an argument that names none is the same for every part. Nothing has to cross between parts.
Inputs may be any that keep to these rules, and one draw needn't show every extreme that they name: `expert_ids`: each token names 2 different experts. In the tokens of one device (aligned blocks of 128 rows) no expert is named more than 36 times; in each span one expert is named exactly 36 times in every block of that span.
All inputs are finite; a program needn't handle non-finite values.
Results may differ from the reference program's by a relative error of at most 0.015.
Values may be sent and summed in bfloat16 or wider, within the bound.
A program may use at most 192 MiB of HBM per device.

```python
import jax
import jax.numpy as jnp
from jax import lax

D = 4096
HEADS = 16
HD = 128
FF = 2048
EXPERTS = 8
TOP = 2
TOK_DEV = 128
CAP = 36
SPAN_TOK = 1024
TOKENS = 4096
ATT = 2048
N_FRAME = 4


def draw_queries(key, part):
    own_key = jax.random.fold_in(key, 21)
    drawn = jax.random.truncated_normal(own_key, -6.0, 6.0, (TOKENS, ATT), jnp.float32)
    return drawn.astype(jnp.bfloat16)


def draw_keys(key, part):
    own_key = jax.random.fold_in(key, 22)
    drawn = jax.random.truncated_normal(own_key, -6.0, 6.0, (TOKENS, ATT), jnp.float32)
    return drawn.astype(jnp.bfloat16)


def draw_hidden_state(key, part):
    own_key = jax.random.fold_in(key, 31)
    row_key, column_key, bulk_key = jax.random.split(own_key, 3)
    row_scale = jnp.exp(jax.random.uniform(row_key, (TOKENS, 1), jnp.float32, -1.2, 1.2))
    column_scale = jnp.exp(jax.random.uniform(column_key, (1, D), jnp.float32, -1.2, 1.2))
    bulk = jax.random.truncated_normal(bulk_key, -5.0, 5.0, (TOKENS, D), jnp.float32)
    return (bulk * row_scale * column_scale).astype(jnp.bfloat16)


def draw_expert_ids(key, part):
    own_key = jax.random.fold_in(key, 11)
    block_count = TOKENS // TOK_DEV
    per_span = SPAN_TOK // TOK_DEV
    mean_load = TOP * TOK_DEV // EXPERTS
    load_step = mean_load // 8

    def one_block(block_index):
        block_key = jax.random.fold_in(own_key, block_index)
        span_key = jax.random.fold_in(own_key, 100000 + block_index // per_span)
        full_expert = jax.random.randint(span_key, (), 0, EXPERTS)
        offset_key, order_key, rank_key = jax.random.split(block_key, 3)
        offsets = jax.random.randint(offset_key, (3,), 0, load_step + 1)
        head_counts = jnp.stack([mean_load + load_step, mean_load - load_step]).astype(jnp.int32)
        pair_counts = jnp.stack([mean_load + offsets, mean_load - offsets], axis=1).reshape(-1).astype(jnp.int32)
        load_counts = jnp.concatenate([head_counts, pair_counts])
        expert_order = jnp.concatenate([jnp.zeros((1,), jnp.int32), 1 + jax.random.permutation(order_key, EXPERTS - 1).astype(jnp.int32)])
        order_ids = (full_expert + expert_order) % EXPERTS
        run_bounds = jnp.cumsum(load_counts)
        slot_index = jnp.arange(TOP * TOK_DEV, dtype=jnp.int32)
        run_index = jnp.sum((slot_index[:, None] >= run_bounds[None, :]).astype(jnp.int32), axis=1)
        slot_expert = jnp.sum(jnp.where(run_index[:, None] == jnp.arange(EXPERTS, dtype=jnp.int32)[None, :], order_ids[None, :], 0), axis=1)
        token_rank = jax.random.permutation(rank_key, TOK_DEV).astype(jnp.int32)
        return jnp.stack([slot_expert[token_rank], slot_expert[TOK_DEV + token_rank]], axis=1)
    blocks = jax.vmap(one_block)(jnp.arange(block_count, dtype=jnp.int32))
    return blocks.reshape(TOKENS, TOP).astype(jnp.int32)


def block_levels(key, shape, pieces, least, top_value):
    def one(axis_at, blocks):
        draws = jax.random.uniform(jax.random.fold_in(jax.random.fold_in(key, 6), axis_at), (blocks,), jnp.float32, least / len(pieces), top_value / len(pieces))
        return jnp.repeat(jnp.exp(draws), shape[axis_at] // blocks).reshape((-1,) + (1,) * (len(shape) - axis_at - 1))

    level = one(*pieces[0])
    for cut in pieces[1:]:
        level = level * one(*cut)
    return level


def scatter_about(key, shape, spread, limit, shards=(), held_as=jnp.bfloat16):
    values = jax.random.normal(key, shape, jnp.float32) * spread
    if len(shards) > 0:
        values = block_levels(key, shape, shards, -0.22, 0.18) * values
    return jnp.clip(values, min=-limit, max=limit).astype(held_as)


def setup_inputs(seed: int = 0, part: int = 0) -> dict:
    streams_of = jax.random.split(jax.random.key(seed), 12)
    own_keys = jax.random.split(jax.random.fold_in(streams_of[11], part), 12)
    return {
        "queries": draw_queries(jax.random.fold_in(jax.random.fold_in(streams_of[11], part), 71), part),
        "keys": draw_keys(jax.random.fold_in(jax.random.fold_in(streams_of[11], part), 71), part),
        "values": scatter_about(own_keys[2], (TOKENS, ATT), 1.0, 6.0, ((0, 4), (1, 8))),
        "hidden_state": draw_hidden_state(jax.random.fold_in(jax.random.fold_in(streams_of[11], part), 71), part),
        "out_grad": scatter_about(own_keys[4], (TOKENS, D), 1.0, 6.0, ((0, 32),)),
        "stored_pre": scatter_about(own_keys[5], (TOKENS, TOP, 2, FF), 1.0, 6.0, ((0, 32),)),
        "expert_ids": draw_expert_ids(jax.random.fold_in(jax.random.fold_in(streams_of[11], part), 71), part),
        "gate_weights": jnp.clip(0.25 + 0.75 * jax.random.uniform(own_keys[7], (TOKENS, TOP), jnp.float32) ** block_levels(own_keys[7], (TOKENS, TOP), ((0, 32),), -0.2, 0.2), 0.25, 1.0),
        "w_gate": scatter_about(streams_of[8], (EXPERTS, D, FF), D ** -0.5, 0.09375, ((0, 8), (2, 4))),
        "w_up": scatter_about(streams_of[9], (EXPERTS, D, FF), D ** -0.5, 0.09375, ((0, 8), (2, 4))),
        "w_down": scatter_about(streams_of[10], (EXPERTS, FF, D), FF ** -0.5, 0.125, ((0, 8), (1, 4))),
    }


masked_score = -1e+30

def head_backward(query_rows, key_rows, value_rows, grad_rows):
    score_scale = HD ** (-0.5)
    scores = jnp.dot(query_rows, key_rows.T, preferred_element_type=jnp.float32) * score_scale
    largest = lax.optimization_barrier(jnp.max(scores, axis=-1, keepdims=True))
    exponent = jnp.exp(scores - largest)
    softmax = exponent / lax.optimization_barrier(jnp.sum(exponent, axis=-1, keepdims=True))
    softmax_grad = jnp.dot(grad_rows, value_rows.T, preferred_element_type=jnp.float32)
    centre = lax.optimization_barrier(jnp.sum(softmax * softmax_grad, axis=-1, keepdims=True))
    score_grads = (softmax * (softmax_grad - centre) * score_scale).astype(jnp.bfloat16)
    softmax_low = softmax.astype(jnp.bfloat16)
    query_part = jnp.dot(score_grads, key_rows, preferred_element_type=jnp.float32)
    key_part = jnp.dot(score_grads.T, query_rows, preferred_element_type=jnp.float32)
    value_part = jnp.dot(softmax_low.T, grad_rows, preferred_element_type=jnp.float32)
    return (query_part.astype(jnp.bfloat16), key_part, value_part)

def reference(queries, keys, values, hidden_state, out_grad, stored_pre, expert_ids, gate_weights, w_gate, w_up, w_down):
    pair_count = TOKENS * TOP
    ff_group = FF // N_FRAME
    pair_grad = (gate_weights[:, :, None] * out_grad[:, None, :].astype(jnp.float32)).astype(jnp.bfloat16).reshape(pair_count, D)
    stored_rows = stored_pre.reshape(pair_count, 2, FF)
    flat_ids = expert_ids.reshape(pair_count)
    row_limit = TOKENS // TOK_DEV * CAP

    def per_expert(expert_index):
        chosen = jnp.nonzero(flat_ids == expert_index, size=row_limit, fill_value=pair_count)[0].astype(jnp.int32)
        grad_rows = jnp.take(pair_grad, chosen, axis=0, mode='fill', fill_value=0)
        stored_here = jnp.take(stored_rows, chosen, axis=0, mode='fill', fill_value=0)
        gate_matrix = w_gate[expert_index]
        up_matrix = w_up[expert_index]
        down_matrix = w_down[expert_index]
        hidden = jnp.dot(grad_rows, down_matrix.T, preferred_element_type=jnp.float32)
        gate_value = stored_here[:, 0, :].astype(jnp.float32)
        up_value = stored_here[:, 1, :].astype(jnp.float32)
        gate_sigmoid = jax.nn.sigmoid(gate_value)
        gate_grad = (hidden * up_value * gate_sigmoid * (1.0 + gate_value * (1.0 - gate_sigmoid))).astype(jnp.bfloat16)
        up_grad = (hidden * gate_value * gate_sigmoid).astype(jnp.bfloat16)
        total = jnp.zeros((row_limit, D), jnp.float32)
        for group_index in range(N_FRAME):
            low_col = group_index * ff_group
            high_col = low_col + ff_group
            group_sum = jnp.dot(gate_grad[:, low_col:high_col], gate_matrix[:, low_col:high_col].T, preferred_element_type=jnp.float32)
            group_sum = group_sum + jnp.dot(up_grad[:, low_col:high_col], up_matrix[:, low_col:high_col].T, preferred_element_type=jnp.float32)
            group_low = lax.optimization_barrier(group_sum.astype(jnp.bfloat16))
            total = total + group_low.astype(jnp.float32)
        return (chosen, total.astype(jnp.bfloat16))
    chosen_all, inputs_all = lax.map(per_expert, jnp.arange(EXPERTS, dtype=jnp.int32))
    collected = jnp.zeros((pair_count + 1, D), jnp.float32).at[chosen_all.reshape(-1)].add(inputs_all.reshape(-1, D).astype(jnp.float32))
    moe_grad = lax.optimization_barrier(jnp.sum(collected[:pair_count].reshape(TOKENS, TOP, D), axis=1))
    state = hidden_state.astype(jnp.float32)
    inverse_rms = lax.rsqrt(lax.optimization_barrier(jnp.mean(state * state, axis=-1, keepdims=True)) + 1e-06)
    normed = state * inverse_rms
    residual = out_grad.astype(jnp.float32) + inverse_rms * (moe_grad - normed * lax.optimization_barrier(jnp.mean(moe_grad * normed, axis=-1, keepdims=True)))
    residual_grad = residual.astype(jnp.bfloat16)
    grad_out = residual_grad[:, :ATT]

    def split_heads(matrix):
        return matrix.reshape(TOKENS, HEADS, HD).transpose(1, 0, 2)

    def one_head(operands):
        query_head, key_head, value_head, grad_head = operands
        query_pieces = []
        key_total = jnp.zeros((TOKENS, HD), jnp.float32)
        value_total = jnp.zeros((TOKENS, HD), jnp.float32)
        for span_index in range(N_FRAME):
            start_row = span_index * SPAN_TOK
            end_row = start_row + SPAN_TOK
            query_piece, key_piece, value_piece = head_backward(query_head[start_row:end_row], key_head[:end_row], value_head[:end_row], grad_head[start_row:end_row])
            query_pieces.append(query_piece)
            key_total = key_total.at[:end_row].add(key_piece)
            value_total = value_total.at[:end_row].add(value_piece)
        return (jnp.concatenate(query_pieces, axis=0), key_total.astype(jnp.bfloat16), value_total.astype(jnp.bfloat16))
    query_heads, key_heads, value_heads = lax.map(one_head, (split_heads(queries), split_heads(keys), split_heads(values), split_heads(grad_out)))

    def join_heads(stacked):
        return stacked.transpose(1, 0, 2).reshape(TOKENS, ATT)
    return (residual_grad, join_heads(query_heads), join_heads(key_heads), join_heads(value_heads))
```

```python
import functools

import jax
import jax.numpy as jnp
from jax import lax
from jax.experimental import pallas as pl
from jax.experimental.pallas import tpu as pltpu
from jax.sharding import PartitionSpec as P

HD = 128
N_EXP = 8
N_FRAME = 4
MAIN = 16
BF = jnp.bfloat16
F32 = jnp.float32
MESH = pl.DeviceIdType.MESH
VMEM_LIMIT = 63 * 1024 * 1024


def dot_nn(a, b):
    return lax.dot_general(a, b, (((1,), (0,)), ((), ())), preferred_element_type=F32)


def dot_nt(a, b):
    return lax.dot_general(a, b, (((1,), (1,)), ((), ())), preferred_element_type=F32)


def moe_kernel(
    ids_ref, gw_ref, og_ref, st_ref, hs_ref, wd_hbm, wg_hbm, wu_hbm,
    resid_ref, gout_ref,
    wd, wg, wu, rows, stored, hid, grads, ysend, yrecv, zrecv,
    half_in, full_in, moe, amat, emat, atmat, etmat,
    w_sem, ys_sem, yr_sem, zs_sem, zr_sem, ag_s, ag_r, fw_s, fw_r, st_s, st_r,
    ha_s, ha_r, fu_s, fu_r, go_s, go_r,
):
    me = lax.axis_index("expert")
    fr = lax.axis_index("frame")
    left = lax.rem(fr + 3, 4)
    right = lax.rem(fr + 1, 4)
    opposite = lax.rem(fr + 2, 4)
    toks, width = og_ref.shape
    cw = width // 4
    ext = cw // 4
    ff = hid.shape[2]
    n_rows = rows.shape[2]
    half = n_rows // 2

    def to_frame(src, dst, ss, rs, dest):
        return pltpu.make_async_remote_copy(
            src_ref=src, dst_ref=dst, send_sem=ss, recv_sem=rs,
            device_id={"frame": dest}, device_id_type=MESH)

    def to_expert(src, dst, ss, rs, dest):
        return pltpu.make_async_remote_copy(
            src_ref=src, dst_ref=dst, send_sem=ss, recv_sem=rs,
            device_id={"expert": dest}, device_id_type=MESH)

    barrier = pltpu.get_barrier_semaphore()
    for d in range(1, N_EXP):
        pl.semaphore_signal(barrier, inc=1, device_id={"expert": lax.rem(me + d, N_EXP)}, device_id_type=MESH)
    for dest in (left, right, opposite):
        pl.semaphore_signal(barrier, inc=1, device_id={"frame": dest}, device_id_type=MESH)

    w_copies = [pltpu.make_async_copy(wd_hbm.at[:, pl.ds(c * cw, cw)], wd.at[c], w_sem.at[c]) for c in range(4)]
    w_copies += [pltpu.make_async_copy(wg_hbm, wg, w_sem.at[4]), pltpu.make_async_copy(wu_hbm, wu, w_sem.at[5])]
    for copy in w_copies:
        copy.start()

    earlier_mask = (
        lax.broadcasted_iota(jnp.int32, (toks, toks), 0) < lax.broadcasted_iota(jnp.int32, (toks, toks), 1)
    ).astype(F32).astype(BF)
    expert_iota = lax.broadcasted_iota(jnp.int32, (N_EXP, toks), 0)
    base = jnp.zeros((N_EXP, 1), F32)
    main_iota = lax.broadcasted_iota(jnp.int32, (2 * N_EXP * MAIN, toks), 0)
    ext_iota = lax.broadcasted_iota(jnp.int32, (N_EXP * MAIN, toks), 0)
    main_sum = jnp.zeros(main_iota.shape, F32)
    ext_sum = [jnp.zeros(ext_iota.shape, F32) for _ in range(4)]
    for k in range(2):
        rel = (ids_ref[pl.ds(k, 1), :] - me + N_EXP) & (N_EXP - 1)
        hit = (expert_iota == rel).astype(F32)
        earlier = dot_nn(hit.astype(BF), earlier_mask) + base
        slot = jnp.sum(hit * earlier, axis=0, keepdims=True).astype(jnp.int32)
        base = base + jnp.sum(hit, axis=1, keepdims=True)
        main_at = jnp.where(slot < 32, (slot >> 4) * (N_EXP * MAIN) + rel * MAIN + (slot & 15), -1)
        ext_at = jnp.where(slot < 32, -1000, rel * MAIN + slot - 32)
        main_k = (main_iota == main_at).astype(F32)
        amat[:, pl.ds(k * toks, toks)] = main_k.astype(BF)
        main_sum = main_sum + main_k
        for j in range(4):
            ext_k = (ext_iota == ext_at + 4 * j).astype(F32)
            emat[j, :, pl.ds(k * toks, toks)] = ext_k.astype(BF)
            ext_sum[j] = ext_sum[j] + ext_k
    atmat[...] = main_sum.T.astype(BF)
    for j in range(4):
        etmat[j] = ext_sum[j].T.astype(BF)

    def pack_pairs(chunk, pairs):
        main = dot_nn(amat[...], pairs).astype(BF)
        ysend[chunk, :, pl.ds(0, cw)] = main[: N_EXP * MAIN]
        ysend[chunk, :, pl.ds(cw, cw)] = main[N_EXP * MAIN:]
        extra = dot_nn(emat[0], pairs[:, :ext])
        for j in range(1, 4):
            extra = extra + dot_nn(emat[j], pairs[:, j * ext:(j + 1) * ext])
        ysend[chunk, :, pl.ds(2 * cw, ext)] = extra.astype(BF)

    def y_copy(chunk, d):
        return to_expert(
            ysend.at[chunk, pl.ds(MAIN * d, MAIN)], yrecv.at[chunk, pl.ds(MAIN * d, MAIN)],
            ys_sem.at[chunk, d], yr_sem.at[chunk, d], lax.rem(me + d, N_EXP))

    pl.semaphore_wait(barrier, N_EXP + 2)

    def build_rows(c, carry):
        x = og_ref[:, pl.ds(pl.multiple_of(c * cw, cw), cw)].astype(F32)
        pairs = jnp.concatenate(
            [(gw_ref[:, 0:1] * x).astype(BF), (gw_ref[:, 1:2] * x).astype(BF)], axis=0)
        pack_pairs(c, pairs)
        for d in range(1, N_EXP):
            y_copy(c, d).start()
        return carry

    lax.fori_loop(0, 4, build_rows, 0)

    def build_stored(c, carry):
        f = lax.rem(fr + c, 4)
        parts = []
        for k in range(2):
            parts.append(jnp.concatenate(
                [st_ref[:, pl.ds(pl.multiple_of((k * 2 + kind) * 4 * ff + f * ff, ff), ff)] for kind in range(2)], axis=1))
        pack_pairs(4 + c, jnp.concatenate(parts, axis=0))
        for d in range(1, N_EXP):
            y_copy(4 + c, d).start()
        return carry

    lax.fori_loop(0, 4, build_stored, 0)

    sel_r = lax.broadcasted_iota(jnp.int32, (4 * N_EXP, N_EXP * MAIN), 0)
    sel_c = lax.broadcasted_iota(jnp.int32, (4 * N_EXP, N_EXP * MAIN), 1)
    selt_r = lax.broadcasted_iota(jnp.int32, (N_EXP * MAIN, 4 * N_EXP), 1)
    selt_c = lax.broadcasted_iota(jnp.int32, (N_EXP * MAIN, 4 * N_EXP), 0)

    def unpack(chunk, dst):
        for d in range(1, N_EXP):
            y_copy(chunk, d).wait_recv()
        yrecv[chunk, pl.ds(0, MAIN)] = ysend[chunk, pl.ds(0, MAIN)]
        dst[pl.ds(0, N_EXP * MAIN), :] = yrecv[chunk, :, pl.ds(0, cw)]
        dst[pl.ds(N_EXP * MAIN, N_EXP * MAIN), :] = yrecv[chunk, :, pl.ds(cw, cw)]
        extra = yrecv[chunk, :, pl.ds(2 * cw, ext)]
        for j in range(4):
            sel = (sel_c == (sel_r >> 2) * MAIN + 4 * j + (sel_r & 3)).astype(F32).astype(BF)
            dst[pl.ds(2 * N_EXP * MAIN, 4 * N_EXP), pl.ds(j * ext, ext)] = dot_nn(sel, extra).astype(BF)

    def ag_copy(c, side):
        return to_frame(rows.at[0, c], rows.at[1 + side, c], ag_s.at[c, side], ag_r.at[c, side],
                        right if side == 0 else left)

    def fw_copy(c, side):
        part = pl.ds(side * half, half)
        return to_frame(rows.at[1 + side, c, part], rows.at[3, c, part], fw_s.at[c, side], fw_r.at[c, side],
                        right if side == 0 else left)

    def add_hidden(b, c):
        hid[b] += dot_nt(rows[b, c], wd[c])

    hid[...] = jnp.zeros_like(hid)
    for copy in w_copies[:4]:
        copy.wait()

    def own_rows(c, carry):
        unpack(c, rows.at[0, c])
        ag_copy(c, 0).start()
        ag_copy(c, 1).start()
        add_hidden(0, c)
        return carry

    lax.fori_loop(0, 4, own_rows, 0)

    def next_rows(c, carry):
        for side in range(2):
            ag_copy(c, side).wait_recv()
            fw_copy(c, side).start()
        add_hidden(1, c)
        add_hidden(2, c)
        return carry

    lax.fori_loop(0, 4, next_rows, 0)

    def own_stored(c, carry):
        unpack(4 + c, sbuf_at(c))
        return carry

    def sbuf_at(c):
        return grads.at[c]

    lax.fori_loop(0, 4, own_stored, 0)
    st_copies = [
        to_frame(grads.at[1], stored.at[0], st_s.at[0], st_r.at[0], right),
        to_frame(grads.at[3], stored.at[1], st_s.at[1], st_r.at[1], left),
        to_frame(grads.at[2], stored.at[2], st_s.at[2], st_r.at[2], opposite),
    ]
    for i in (2, 0, 1):
        st_copies[i].start()

    def far_rows(c, carry):
        for side in range(2):
            fw_copy(c, side).wait_recv()
        add_hidden(3, c)
        return carry

    lax.fori_loop(0, 4, far_rows, 0)

    def hidden_to_grads(b, src):
        h = hid[b]
        g = src[:, pl.ds(0, ff)].astype(F32)
        u = src[:, pl.ds(ff, ff)].astype(F32)
        s = 1.0 / (1.0 + jnp.exp(-g))
        gate = (h * u * s * (1.0 + g * (1.0 - s))).astype(BF)
        up = (h * g * s).astype(BF)
        return gate, up

    for i in (2, 0, 1):
        st_copies[i].wait()
    for b in (3, 2, 1, 0):
        src = grads.at[0] if b == 0 else stored.at[b - 1]
        gate, up = hidden_to_grads(b, src)
        grads[b, :, pl.ds(0, ff)] = gate
        grads[b, :, pl.ds(ff, ff)] = up

    for copy in w_copies[4:]:
        copy.wait()

    def term(b, c):
        at = pl.ds(pl.multiple_of(c * cw, cw), cw)
        return dot_nt(grads[b, :, pl.ds(0, ff)], wg[at, :]) + dot_nt(grads[b, :, pl.ds(ff, ff)], wu[at, :])

    def ha_copy(c, side):
        return to_frame(rows.at[3, c, pl.ds(side * half, half)], half_in.at[side, c],
                        ha_s.at[c, side], ha_r.at[c, side], right if side == 0 else left)

    def fu_copy(c, side):
        return to_frame(rows.at[2 - side, c], full_in.at[side, c], fu_s.at[c, side], fu_r.at[c, side],
                        right if side == 0 else left)

    def far_terms(c, carry):
        rows[3, c] = term(3, c).astype(BF)
        for side in range(2):
            ha_copy(c, side).start()
        return carry

    lax.fori_loop(0, 4, far_terms, 0)

    def near_terms(c, carry):
        for side in range(2):
            fw_copy(c, 1 - side).wait_send()
            part = term(2 - side, c)
            ha_copy(c, side).wait_recv()
            lo = side * half
            rows[2 - side, c, pl.ds(half - lo, half)] = part[half - lo:half - lo + half].astype(BF)
            rows[2 - side, c, pl.ds(lo, half)] = (
                part[lo:lo + half].astype(BF).astype(F32) + half_in[side, c].astype(F32)).astype(BF)
            fu_copy(c, side).start()
        return carry

    lax.fori_loop(0, 4, near_terms, 0)

    def z_copy(c, d):
        return to_expert(
            ysend.at[c, pl.ds(MAIN * d, MAIN)], zrecv.at[c, pl.ds(MAIN * d, MAIN)],
            zs_sem.at[c, d], zr_sem.at[c, d], lax.rem(me + N_EXP - d, N_EXP))

    def own_terms(c, carry):
        part = term(0, c).astype(BF).astype(F32)
        for side in range(2):
            fu_copy(c, side).wait_recv()
        total = (part + full_in[0, c].astype(F32) + full_in[1, c].astype(F32)).astype(BF)
        for d in range(1, N_EXP):
            y_copy(c, d).wait_send()
        ysend[c, :, pl.ds(0, cw)] = total[: N_EXP * MAIN]
        ysend[c, :, pl.ds(cw, cw)] = total[N_EXP * MAIN: 2 * N_EXP * MAIN]
        extra = jnp.zeros((N_EXP * MAIN, ext), F32)
        for j in range(4):
            sel = (selt_c == (selt_r >> 2) * MAIN + 4 * j + (selt_r & 3)).astype(F32).astype(BF)
            extra = extra + dot_nn(sel, total[2 * N_EXP * MAIN:, j * ext:(j + 1) * ext])
        ysend[c, :, pl.ds(2 * cw, ext)] = extra.astype(BF)
        for d in range(1, N_EXP):
            z_copy(c, d).start()
        return carry

    lax.fori_loop(0, 4, own_terms, 0)

    def square_sum(c, acc):
        x = hs_ref[:, pl.ds(pl.multiple_of(c * cw, cw), cw)].astype(F32)
        return acc + jnp.sum(x * x, axis=1, keepdims=True)

    inv = lax.rsqrt(lax.fori_loop(0, 4, square_sum, jnp.zeros((toks, 1), F32)) / width + 1e-6)

    def combine(c, acc):
        for d in range(1, N_EXP):
            z_copy(c, d).wait_recv()
        zrecv[c, pl.ds(0, MAIN)] = ysend[c, pl.ds(0, MAIN)]
        at = pl.ds(pl.multiple_of(c * cw, cw), cw)
        got = dot_nn(atmat[:, pl.ds(0, N_EXP * MAIN)], zrecv[c, :, pl.ds(0, cw)])
        got = got + dot_nn(atmat[:, pl.ds(N_EXP * MAIN, N_EXP * MAIN)], zrecv[c, :, pl.ds(cw, cw)])
        extra = zrecv[c, :, pl.ds(2 * cw, ext)]
        got = got + jnp.concatenate([dot_nn(etmat[j], extra) for j in range(4)], axis=1)
        moe[:, at] = got
        return acc + jnp.sum(got * hs_ref[:, at].astype(F32), axis=1, keepdims=True)

    mean = lax.fori_loop(0, 4, combine, jnp.zeros((toks, 1), F32)) * inv / width

    def residual(c, carry):
        at = pl.ds(pl.multiple_of(c * cw, cw), cw)
        n = hs_ref[:, at].astype(F32) * inv
        resid_ref[:, at] = (og_ref[:, at].astype(F32) + inv * (moe[:, at] - n * mean)).astype(BF)
        return carry

    lax.fori_loop(0, 4, residual, 0)

    hw = gout_ref.shape[1]
    own_at = pl.ds(pl.multiple_of(me * toks, toks), toks)

    def go_copy(d):
        dest = lax.rem(me + d, N_EXP)
        return to_expert(
            resid_ref.at[:, pl.ds(pl.multiple_of(dest * hw, hw), hw)], gout_ref.at[own_at],
            go_s.at[d], go_r.at[d], dest)

    for d in range(1, N_EXP):
        go_copy(d).start()
    gout_ref[own_at, :] = resid_ref[:, pl.ds(pl.multiple_of(me * hw, hw), hw)]

    def drain(c, carry):
        for side in range(2):
            ag_copy(c, side).wait_send()
            ha_copy(c, side).wait_send()
            fu_copy(c, side).wait_send()
        for d in range(1, N_EXP):
            y_copy(4 + c, d).wait_send()
            z_copy(c, d).wait_send()
        return carry

    lax.fori_loop(0, 4, drain, 0)
    for d in range(1, N_EXP):
        go_copy(d).wait()


def moe_call(ids_t, gate_weights, out_grad, stored, hidden_state, wd, wg, wu, att_local):
    toks, width = out_grad.shape
    ff = wd.shape[0]
    cw = width // 4
    n_rows = N_EXP * 36
    pw = 2 * cw + cw // 4
    vm = pl.BlockSpec(memory_space=pltpu.VMEM)
    hbm = pl.BlockSpec(memory_space=pl.ANY)
    dma = pltpu.SemaphoreType.DMA
    return pl.pallas_call(
        moe_kernel,
        out_shape=(
            jax.ShapeDtypeStruct((toks, width), BF),
            jax.ShapeDtypeStruct((toks * N_EXP, att_local), BF),
        ),
        in_specs=[vm] * 5 + [hbm] * 3,
        out_specs=(vm, vm),
        scratch_shapes=[
            pltpu.VMEM((4, ff, cw), BF),
            pltpu.VMEM((width, ff), BF),
            pltpu.VMEM((width, ff), BF),
            pltpu.VMEM((4, 4, n_rows, cw), BF),
            pltpu.VMEM((3, n_rows, 2 * ff), BF),
            pltpu.VMEM((4, n_rows, ff), F32),
            pltpu.VMEM((4, n_rows, 2 * ff), BF),
            pltpu.VMEM((8, N_EXP * MAIN, pw), BF),
            pltpu.VMEM((8, N_EXP * MAIN, pw), BF),
            pltpu.VMEM((4, N_EXP * MAIN, pw), BF),
            pltpu.VMEM((2, 4, n_rows // 2, cw), BF),
            pltpu.VMEM((2, 4, n_rows, cw), BF),
            pltpu.VMEM((toks, width), F32),
            pltpu.VMEM((2 * N_EXP * MAIN, 2 * toks), BF),
            pltpu.VMEM((4, N_EXP * MAIN, 2 * toks), BF),
            pltpu.VMEM((toks, 2 * N_EXP * MAIN), BF),
            pltpu.VMEM((4, toks, N_EXP * MAIN), BF),
            dma((6,)), dma((8, 8)), dma((8, 8)), dma((4, 8)), dma((4, 8)),
            dma((4, 2)), dma((4, 2)), dma((4, 2)), dma((4, 2)), dma((3,)), dma((3,)),
            dma((4, 2)), dma((4, 2)), dma((4, 2)), dma((4, 2)), dma((8,)), dma((8,)),
        ],
        compiler_params=pltpu.CompilerParams(
            collective_id=0, has_side_effects=True, vmem_limit_bytes=VMEM_LIMIT),
        cost_estimate=pl.CostEstimate(flops=15 * 10**9, bytes_accessed=20 * 10**6, transcendentals=0),
        name="moe",
    )(ids_t, gate_weights, out_grad, stored, hidden_state, wd, wg, wu)


def attention_kernel(q_ref, k_ref, v_ref, go_ref, dq_ref, dk_ref, dv_ref, probs):
    fr = lax.axis_index("frame")
    span = q_ref.shape[0]
    qt_w = 512
    scale = HD ** -0.5
    log2e = 1.4426950408889634
    dk_ref[...] = jnp.zeros_like(dk_ref)
    dv_ref[...] = jnp.zeros_like(dv_ref)
    for h in range(2):
        cols = pl.ds(h * HD, HD)
        for qi in range(span // qt_w):
            qrows = pl.ds(qi * qt_w, qt_w)
            q = q_ref[qrows, cols]
            qt = q.astype(F32).T.astype(BF)

            def krows(s):
                return pl.ds(pl.multiple_of(s * span, span), span)

            def largest(s, m):
                sc = dot_nn(k_ref[krows(s), cols], qt) * (scale * log2e)
                return jnp.maximum(m, jnp.max(sc, axis=0, keepdims=True))

            m = lax.fori_loop(0, fr + 1, largest, jnp.full((1, qt_w), -1e30, F32))

            def forward(s, carry):
                l, o = carry
                sc = dot_nn(k_ref[krows(s), cols], qt) * (scale * log2e)
                p = jnp.exp2(sc - m)
                low = p.astype(BF)
                probs[s] = low
                vt = v_ref[krows(s), cols].astype(F32).T.astype(BF)
                return l + jnp.sum(p, axis=0, keepdims=True), o + dot_nn(vt, low)

            l, o = lax.fori_loop(
                0, fr + 1, forward, (jnp.zeros((1, qt_w), F32), jnp.zeros((HD, qt_w), F32)))
            inv = 1.0 / l
            got = go_ref[qrows, cols].astype(F32).T * inv
            go_n = got.astype(BF)
            go_s = (got * scale).astype(BF)
            centre = jnp.sum(go_s.astype(F32) * (o * inv), axis=0, keepdims=True)
            go_rows = go_n.astype(F32).T.astype(BF)

            def backward(s, dq):
                kk = k_ref[krows(s), cols]
                p = probs[s]
                dp = dot_nn(v_ref[krows(s), cols], go_s)
                ds = (p.astype(F32) * (dp - centre)).astype(BF)
                dk_ref[krows(s), cols] += dot_nn(ds, q)
                dv_ref[krows(s), cols] += dot_nn(p, go_rows)
                kt = kk.astype(F32).T.astype(BF)
                return dq + dot_nn(kt, ds)

            dq = lax.fori_loop(0, fr + 1, backward, jnp.zeros((HD, qt_w), F32))
            dq_ref[qrows, cols] = dq.T.astype(BF)


def attention_call(q, k, v, go):
    span, width = q.shape
    vm = pl.BlockSpec(memory_space=pltpu.VMEM)
    return pl.pallas_call(
        attention_kernel,
        out_shape=(
            jax.ShapeDtypeStruct(q.shape, BF),
            jax.ShapeDtypeStruct(k.shape, F32),
            jax.ShapeDtypeStruct(v.shape, F32),
        ),
        in_specs=[vm] * 4,
        out_specs=(vm,) * 3,
        scratch_shapes=[pltpu.VMEM((4, span, 512), BF)],
        compiler_params=pltpu.CompilerParams(vmem_limit_bytes=VMEM_LIMIT),
        cost_estimate=pl.CostEstimate(flops=10 * 10**9, bytes_accessed=20 * 10**6, transcendentals=0),
        name="attention",
    )(q, k, v, go)


def on_device(
    queries, keys, values, hidden_state, out_grad, stored_pre, expert_ids, gate_weights,
    w_gate, w_up, w_down,
):
    toks = out_grad.shape[0]
    key_all, value_all = (
        lax.all_gather(keys, "frame", axis=0, tiled=True),
        lax.all_gather(values, "frame", axis=0, tiled=True),
    )
    resid, go = moe_call(
        expert_ids.T, gate_weights, out_grad, stored_pre.reshape(toks, -1), hidden_state,
        w_down[0], w_gate[0], w_up[0], queries.shape[1])
    dq, dk, dv = attention_call(queries, key_all, value_all, go)
    dk = lax.psum_scatter(dk.astype(BF), "frame", scatter_dimension=0, tiled=True)
    dv = lax.psum_scatter(dv.astype(BF), "frame", scatter_dimension=0, tiled=True)
    return resid, dq, dk, dv


def solution(mesh):
    rows = P(("dp", "frame"), "expert")
    toks = ("dp", "frame", "expert")
    return jax.shard_map(
        on_device,
        mesh=mesh,
        in_specs=(
            rows, rows, rows, P(toks, None), P(toks, None), P(toks, None, None, None),
            P(toks, None), P(toks, None), P("expert", None, "frame"), P("expert", None, "frame"),
            P("expert", "frame", None),
        ),
        out_specs=(P(toks, None), rows, rows, rows),
        check_vma=False,
    )
```

```python
import functools

import jax
import jax.numpy as jnp
from jax import lax
from jax.experimental import pallas as pl
from jax.experimental.pallas import tpu as pltpu
from jax.sharding import PartitionSpec as P

HD = 128
N_EXP = 8
N_FRAME = 4
MAIN = 16
BF = jnp.bfloat16
F32 = jnp.float32
MESH = pl.DeviceIdType.MESH
VMEM_LIMIT = 63 * 1024 * 1024


def dot_nn(a, b):
    return lax.dot_general(a, b, (((1,), (0,)), ((), ())), preferred_element_type=F32)


def dot_nt(a, b):
    return lax.dot_general(a, b, (((1,), (1,)), ((), ())), preferred_element_type=F32)


def moe_kernel(
    ids_ref, gw_ref, og_ref, st_ref, hs_ref, wd_hbm, wg_hbm, wu_hbm,
    resid_ref, gout_ref,
    wd, wg, wu, rows, stored, hid, grads, ysend, yrecv, zrecv,
    half_in, full_in, moe, amat, emat, atmat, etmat,
    w_sem, ys_sem, yr_sem, zs_sem, zr_sem, ag_s, ag_r, fw_s, fw_r, st_s, st_r,
    ha_s, ha_r, fu_s, fu_r, go_s, go_r,
):
    me = lax.axis_index("expert")
    fr = lax.axis_index("frame")
    left = lax.rem(fr + 3, 4)
    right = lax.rem(fr + 1, 4)
    opposite = lax.rem(fr + 2, 4)
    toks, width = og_ref.shape
    cw = width // 4
    ext = cw // 4
    ff = hid.shape[2]
    n_rows = rows.shape[2]
    half = n_rows // 2

    def to_frame(src, dst, ss, rs, dest):
        return pltpu.make_async_remote_copy(
            src_ref=src, dst_ref=dst, send_sem=ss, recv_sem=rs,
            device_id={"frame": dest}, device_id_type=MESH)

    def to_expert(src, dst, ss, rs, dest):
        return pltpu.make_async_remote_copy(
            src_ref=src, dst_ref=dst, send_sem=ss, recv_sem=rs,
            device_id={"expert": dest}, device_id_type=MESH)

    barrier = pltpu.get_barrier_semaphore()
    for d in range(1, N_EXP):
        pl.semaphore_signal(barrier, inc=1, device_id={"expert": lax.rem(me + d, N_EXP)}, device_id_type=MESH)
    for dest in (left, right, opposite):
        pl.semaphore_signal(barrier, inc=1, device_id={"frame": dest}, device_id_type=MESH)

    w_copies = [pltpu.make_async_copy(wd_hbm.at[:, pl.ds(c * cw, cw)], wd.at[c], w_sem.at[c]) for c in range(4)]
    w_copies += [pltpu.make_async_copy(wg_hbm, wg, w_sem.at[4]), pltpu.make_async_copy(wu_hbm, wu, w_sem.at[5])]
    for copy in w_copies:
        copy.start()

    earlier_mask = (
        lax.broadcasted_iota(jnp.int32, (toks, toks), 0) < lax.broadcasted_iota(jnp.int32, (toks, toks), 1)
    ).astype(F32).astype(BF)
    expert_iota = lax.broadcasted_iota(jnp.int32, (N_EXP, toks), 0)
    base = jnp.zeros((N_EXP, 1), F32)
    main_iota = lax.broadcasted_iota(jnp.int32, (2 * N_EXP * MAIN, toks), 0)
    ext_iota = lax.broadcasted_iota(jnp.int32, (N_EXP * MAIN, toks), 0)
    main_sum = jnp.zeros(main_iota.shape, F32)
    ext_sum = [jnp.zeros(ext_iota.shape, F32) for _ in range(4)]
    for k in range(2):
        rel = (ids_ref[pl.ds(k, 1), :] - me + N_EXP) & (N_EXP - 1)
        hit = (expert_iota == rel).astype(F32)
        earlier = dot_nn(hit.astype(BF), earlier_mask) + base
        slot = jnp.sum(hit * earlier, axis=0, keepdims=True).astype(jnp.int32)
        base = base + jnp.sum(hit, axis=1, keepdims=True)
        main_at = jnp.where(slot < 32, (slot >> 4) * (N_EXP * MAIN) + rel * MAIN + (slot & 15), -1)
        ext_at = jnp.where(slot < 32, -1000, rel * MAIN + slot - 32)
        main_k = (main_iota == main_at).astype(F32)
        amat[:, pl.ds(k * toks, toks)] = main_k.astype(BF)
        main_sum = main_sum + main_k
        for j in range(4):
            ext_k = (ext_iota == ext_at + 4 * j).astype(F32)
            emat[j, :, pl.ds(k * toks, toks)] = ext_k.astype(BF)
            ext_sum[j] = ext_sum[j] + ext_k
    atmat[...] = main_sum.T.astype(BF)
    for j in range(4):
        etmat[j] = ext_sum[j].T.astype(BF)

    def pack_pairs(chunk, pairs):
        main = dot_nn(amat[...], pairs).astype(BF)
        ysend[chunk, :, pl.ds(0, cw)] = main[: N_EXP * MAIN]
        ysend[chunk, :, pl.ds(cw, cw)] = main[N_EXP * MAIN:]
        extra = dot_nn(emat[0], pairs[:, :ext])
        for j in range(1, 4):
            extra = extra + dot_nn(emat[j], pairs[:, j * ext:(j + 1) * ext])
        ysend[chunk, :, pl.ds(2 * cw, ext)] = extra.astype(BF)

    def y_copy(chunk, d):
        return to_expert(
            ysend.at[chunk, pl.ds(MAIN * d, MAIN)], yrecv.at[chunk, pl.ds(MAIN * d, MAIN)],
            ys_sem.at[chunk, d], yr_sem.at[chunk, d], lax.rem(me + d, N_EXP))

    pl.semaphore_wait(barrier, N_EXP + 2)

    def build_rows(c, carry):
        x = og_ref[:, pl.ds(pl.multiple_of(c * cw, cw), cw)].astype(F32)
        pairs = jnp.concatenate(
            [(gw_ref[:, 0:1] * x).astype(BF), (gw_ref[:, 1:2] * x).astype(BF)], axis=0)
        pack_pairs(c, pairs)
        for d in range(1, N_EXP):
            y_copy(c, d).start()
        return carry

    lax.fori_loop(0, 4, build_rows, 0)

    def build_stored(c, carry):
        f = lax.rem(fr + c, 4)
        parts = []
        for k in range(2):
            parts.append(jnp.concatenate(
                [st_ref[:, pl.ds(pl.multiple_of((k * 2 + kind) * 4 * ff + f * ff, ff), ff)] for kind in range(2)], axis=1))
        pack_pairs(4 + c, jnp.concatenate(parts, axis=0))
        for d in range(1, N_EXP):
            y_copy(4 + c, d).start()
        return carry

    lax.fori_loop(0, 4, build_stored, 0)

    sel_r = lax.broadcasted_iota(jnp.int32, (4 * N_EXP, N_EXP * MAIN), 0)
    sel_c = lax.broadcasted_iota(jnp.int32, (4 * N_EXP, N_EXP * MAIN), 1)
    selt_r = lax.broadcasted_iota(jnp.int32, (N_EXP * MAIN, 4 * N_EXP), 1)
    selt_c = lax.broadcasted_iota(jnp.int32, (N_EXP * MAIN, 4 * N_EXP), 0)

    def unpack(chunk, dst):
        for d in range(1, N_EXP):
            y_copy(chunk, d).wait_recv()
        yrecv[chunk, pl.ds(0, MAIN)] = ysend[chunk, pl.ds(0, MAIN)]
        dst[pl.ds(0, N_EXP * MAIN), :] = yrecv[chunk, :, pl.ds(0, cw)]
        dst[pl.ds(N_EXP * MAIN, N_EXP * MAIN), :] = yrecv[chunk, :, pl.ds(cw, cw)]
        extra = yrecv[chunk, :, pl.ds(2 * cw, ext)]
        for j in range(4):
            sel = (sel_c == (sel_r >> 2) * MAIN + 4 * j + (sel_r & 3)).astype(F32).astype(BF)
            dst[pl.ds(2 * N_EXP * MAIN, 4 * N_EXP), pl.ds(j * ext, ext)] = dot_nn(sel, extra).astype(BF)

    def ag_copy(c, side):
        return to_frame(rows.at[0, c], rows.at[1 + side, c], ag_s.at[c, side], ag_r.at[c, side],
                        right if side == 0 else left)

    def fw_copy(c, side):
        part = pl.ds(side * half, half)
        return to_frame(rows.at[1 + side, c, part], rows.at[3, c, part], fw_s.at[c, side], fw_r.at[c, side],
                        right if side == 0 else left)

    def add_hidden(b, c):
        hid[b] += dot_nt(rows[b, c], wd[c])

    hid[...] = jnp.zeros_like(hid)
    for copy in w_copies[:4]:
        copy.wait()

    def own_rows(c, carry):
        unpack(c, rows.at[0, c])
        ag_copy(c, 0).start()
        ag_copy(c, 1).start()
        add_hidden(0, c)
        return carry

    lax.fori_loop(0, 4, own_rows, 0)

    def next_rows(c, carry):
        for side in range(2):
            ag_copy(c, side).wait_recv()
            fw_copy(c, side).start()
        add_hidden(1, c)
        add_hidden(2, c)
        return carry

    lax.fori_loop(0, 4, next_rows, 0)

    def own_stored(c, carry):
        unpack(4 + c, sbuf_at(c))
        return carry

    def sbuf_at(c):
        return grads.at[c]

    lax.fori_loop(0, 4, own_stored, 0)
    st_copies = [
        to_frame(grads.at[1], stored.at[0], st_s.at[0], st_r.at[0], right),
        to_frame(grads.at[3], stored.at[1], st_s.at[1], st_r.at[1], left),
        to_frame(grads.at[2], stored.at[2], st_s.at[2], st_r.at[2], opposite),
    ]
    for i in (2, 0, 1):
        st_copies[i].start()

    def far_rows(c, carry):
        for side in range(2):
            fw_copy(c, side).wait_recv()
        add_hidden(3, c)
        return carry

    lax.fori_loop(0, 4, far_rows, 0)

    def hidden_to_grads(b, src):
        h = hid[b]
        g = src[:, pl.ds(0, ff)].astype(F32)
        u = src[:, pl.ds(ff, ff)].astype(F32)
        s = 1.0 / (1.0 + jnp.exp(-g))
        gate = (h * u * s * (1.0 + g * (1.0 - s))).astype(BF)
        up = (h * g * s).astype(BF)
        return gate, up

    for i in (2, 0, 1):
        st_copies[i].wait()
    for b in (3, 2, 1, 0):
        src = grads.at[0] if b == 0 else stored.at[b - 1]
        gate, up = hidden_to_grads(b, src)
        grads[b, :, pl.ds(0, ff)] = gate
        grads[b, :, pl.ds(ff, ff)] = up

    for copy in w_copies[4:]:
        copy.wait()

    def term(b, c):
        at = pl.ds(pl.multiple_of(c * cw, cw), cw)
        return dot_nt(grads[b, :, pl.ds(0, ff)], wg[at, :]) + dot_nt(grads[b, :, pl.ds(ff, ff)], wu[at, :])

    def ha_copy(c, side):
        return to_frame(rows.at[3, c, pl.ds(side * half, half)], half_in.at[side, c],
                        ha_s.at[c, side], ha_r.at[c, side], right if side == 0 else left)

    def fu_copy(c, side):
        return to_frame(rows.at[2 - side, c], full_in.at[side, c], fu_s.at[c, side], fu_r.at[c, side],
                        right if side == 0 else left)

    def far_terms(c, carry):
        rows[3, c] = term(3, c).astype(BF)
        for side in range(2):
            ha_copy(c, side).start()
        return carry

    lax.fori_loop(0, 4, far_terms, 0)

    def near_terms(c, carry):
        for side in range(2):
            fw_copy(c, 1 - side).wait_send()
            part = term(2 - side, c)
            ha_copy(c, side).wait_recv()
            lo = side * half
            rows[2 - side, c, pl.ds(half - lo, half)] = part[half - lo:half - lo + half].astype(BF)
            rows[2 - side, c, pl.ds(lo, half)] = (
                part[lo:lo + half].astype(BF).astype(F32) + half_in[side, c].astype(F32)).astype(BF)
            fu_copy(c, side).start()
        return carry

    lax.fori_loop(0, 4, near_terms, 0)

    def z_copy(c, d):
        return to_expert(
            ysend.at[c, pl.ds(MAIN * d, MAIN)], zrecv.at[c, pl.ds(MAIN * d, MAIN)],
            zs_sem.at[c, d], zr_sem.at[c, d], lax.rem(me + N_EXP - d, N_EXP))

    def own_terms(c, carry):
        part = term(0, c).astype(BF).astype(F32)
        for side in range(2):
            fu_copy(c, side).wait_recv()
        total = (part + full_in[0, c].astype(F32) + full_in[1, c].astype(F32)).astype(BF)
        for d in range(1, N_EXP):
            y_copy(c, d).wait_send()
        ysend[c, :, pl.ds(0, cw)] = total[: N_EXP * MAIN]
        ysend[c, :, pl.ds(cw, cw)] = total[N_EXP * MAIN: 2 * N_EXP * MAIN]
        extra = jnp.zeros((N_EXP * MAIN, ext), F32)
        for j in range(4):
            sel = (selt_c == (selt_r >> 2) * MAIN + 4 * j + (selt_r & 3)).astype(F32).astype(BF)
            extra = extra + dot_nn(sel, total[2 * N_EXP * MAIN:, j * ext:(j + 1) * ext])
        ysend[c, :, pl.ds(2 * cw, ext)] = extra.astype(BF)
        for d in range(1, N_EXP):
            z_copy(c, d).start()
        return carry

    lax.fori_loop(0, 4, own_terms, 0)

    def square_sum(c, acc):
        x = hs_ref[:, pl.ds(pl.multiple_of(c * cw, cw), cw)].astype(F32)
        return acc + jnp.sum(x * x, axis=1, keepdims=True)

    inv = lax.rsqrt(lax.fori_loop(0, 4, square_sum, jnp.zeros((toks, 1), F32)) / width + 1e-6)

    def combine(c, acc):
        for d in range(1, N_EXP):
            z_copy(c, d).wait_recv()
        zrecv[c, pl.ds(0, MAIN)] = ysend[c, pl.ds(0, MAIN)]
        at = pl.ds(pl.multiple_of(c * cw, cw), cw)
        got = dot_nn(atmat[:, pl.ds(0, N_EXP * MAIN)], zrecv[c, :, pl.ds(0, cw)])
        got = got + dot_nn(atmat[:, pl.ds(N_EXP * MAIN, N_EXP * MAIN)], zrecv[c, :, pl.ds(cw, cw)])
        extra = zrecv[c, :, pl.ds(2 * cw, ext)]
        got = got + jnp.concatenate([dot_nn(etmat[j], extra) for j in range(4)], axis=1)
        moe[:, at] = got
        return acc + jnp.sum(got * hs_ref[:, at].astype(F32), axis=1, keepdims=True)

    mean = lax.fori_loop(0, 4, combine, jnp.zeros((toks, 1), F32)) * inv / width

    def residual(c, carry):
        at = pl.ds(pl.multiple_of(c * cw, cw), cw)
        n = hs_ref[:, at].astype(F32) * inv
        resid_ref[:, at] = (og_ref[:, at].astype(F32) + inv * (moe[:, at] - n * mean)).astype(BF)
        return carry

    lax.fori_loop(0, 4, residual, 0)

    hw = gout_ref.shape[1]
    own_at = pl.ds(pl.multiple_of(me * toks, toks), toks)

    def go_copy(d):
        dest = lax.rem(me + d, N_EXP)
        return to_expert(
            resid_ref.at[:, pl.ds(pl.multiple_of(dest * hw, hw), hw)], gout_ref.at[own_at],
            go_s.at[d], go_r.at[d], dest)

    for d in range(1, N_EXP):
        go_copy(d).start()
    gout_ref[own_at, :] = resid_ref[:, pl.ds(pl.multiple_of(me * hw, hw), hw)]

    def drain(c, carry):
        for side in range(2):
            ag_copy(c, side).wait_send()
            ha_copy(c, side).wait_send()
            fu_copy(c, side).wait_send()
        for d in range(1, N_EXP):
            y_copy(4 + c, d).wait_send()
            z_copy(c, d).wait_send()
        return carry

    lax.fori_loop(0, 4, drain, 0)
    for d in range(1, N_EXP):
        go_copy(d).wait()


def moe_call(ids_t, gate_weights, out_grad, stored, hidden_state, wd, wg, wu, att_local):
    toks, width = out_grad.shape
    ff = wd.shape[0]
    cw = width // 4
    n_rows = N_EXP * 36
    pw = 2 * cw + cw // 4
    vm = pl.BlockSpec(memory_space=pltpu.VMEM)
    hbm = pl.BlockSpec(memory_space=pl.ANY)
    dma = pltpu.SemaphoreType.DMA
    return pl.pallas_call(
        moe_kernel,
        out_shape=(
            jax.ShapeDtypeStruct((toks, width), BF),
            jax.ShapeDtypeStruct((toks * N_EXP, att_local), BF),
        ),
        in_specs=[vm] * 5 + [hbm] * 3,
        out_specs=(vm, vm),
        scratch_shapes=[
            pltpu.VMEM((4, ff, cw), BF),
            pltpu.VMEM((width, ff), BF),
            pltpu.VMEM((width, ff), BF),
            pltpu.VMEM((4, 4, n_rows, cw), BF),
            pltpu.VMEM((3, n_rows, 2 * ff), BF),
            pltpu.VMEM((4, n_rows, ff), F32),
            pltpu.VMEM((4, n_rows, 2 * ff), BF),
            pltpu.VMEM((8, N_EXP * MAIN, pw), BF),
            pltpu.VMEM((8, N_EXP * MAIN, pw), BF),
            pltpu.VMEM((4, N_EXP * MAIN, pw), BF),
            pltpu.VMEM((2, 4, n_rows // 2, cw), BF),
            pltpu.VMEM((2, 4, n_rows, cw), BF),
            pltpu.VMEM((toks, width), F32),
            pltpu.VMEM((2 * N_EXP * MAIN, 2 * toks), BF),
            pltpu.VMEM((4, N_EXP * MAIN, 2 * toks), BF),
            pltpu.VMEM((toks, 2 * N_EXP * MAIN), BF),
            pltpu.VMEM((4, toks, N_EXP * MAIN), BF),
            dma((6,)), dma((8, 8)), dma((8, 8)), dma((4, 8)), dma((4, 8)),
            dma((4, 2)), dma((4, 2)), dma((4, 2)), dma((4, 2)), dma((3,)), dma((3,)),
            dma((4, 2)), dma((4, 2)), dma((4, 2)), dma((4, 2)), dma((8,)), dma((8,)),
        ],
        compiler_params=pltpu.CompilerParams(
            collective_id=0, has_side_effects=True, vmem_limit_bytes=VMEM_LIMIT),
        cost_estimate=pl.CostEstimate(flops=15 * 10**9, bytes_accessed=20 * 10**6, transcendentals=0),
        name="moe",
    )(ids_t, gate_weights, out_grad, stored, hidden_state, wd, wg, wu)


def attention_kernel(
    q_ref, k_ref, v_ref, go_ref, dq_ref, dk_ref, dv_ref,
    probs, qt, vt, gs_t, g_rows, dqt, send, half_in, full_in,
    hs, hr, fs, fr_sem,
):
    fr = lax.axis_index("frame")
    left = lax.rem(fr + 3, 4)
    right = lax.rem(fr + 1, 4)
    span = q_ref.shape[0]
    tile = 256
    tiles = span // tile
    scale = HD ** -0.5
    log2e = 1.4426950408889634

    barrier = pltpu.get_barrier_semaphore()
    for dest in (left, right):
        pl.semaphore_signal(barrier, inc=1, device_id={"frame": dest}, device_id_type=MESH)
    pl.semaphore_wait(barrier, 2)

    def to_frame(src, dst, ss, rs, dest):
        return pltpu.make_async_remote_copy(
            src_ref=src, dst_ref=dst, send_sem=ss, recv_sem=rs,
            device_id={"frame": dest}, device_id_type=MESH)

    def half_copy(h):
        return to_frame(send.at[0, h], half_in.at[h], hs.at[h], hr.at[h], left if h == 0 else right)

    def full_copy(side, h):
        return to_frame(send.at[1 + side, h], full_in.at[side, h], fs.at[side, h], fr_sem.at[side, h],
                        left if side == 0 else right)

    def rows_at(s, t):
        return pl.ds(pl.multiple_of(s * span + t * tile, tile), tile)

    def add_half(side, h):
        half_copy(h).wait_recv()
        for j in range(2):
            send[1 + side, h, j] = (send[1 + side, h, j].astype(F32) + half_in[h, j].astype(F32)).astype(BF)

    for h in range(2):
        cols = pl.ds(h * HD, HD)
        qt[...] = q_ref[:, cols].astype(F32).T.astype(BF)

        def largest(i, m):
            sc = dot_nn(k_ref[rows_at(0, i), cols], qt[...])
            return jnp.maximum(m, jnp.max(sc, axis=0, keepdims=True))

        n_tiles = (fr + 1) * tiles
        m = lax.fori_loop(0, n_tiles, largest, jnp.full((1, span), -jnp.inf, F32)) * (scale * log2e)

        def forward(i, carry):
            l, o = carry
            sc = dot_nn(k_ref[rows_at(0, i), cols], qt[...])
            p = jnp.exp2(sc * (scale * log2e) - m)
            low = p.astype(BF)
            probs[rows_at(0, i), :] = low
            v_t = v_ref[rows_at(0, i), cols].astype(F32).T.astype(BF)
            return l + jnp.sum(p, axis=0, keepdims=True), o + dot_nn(v_t, low)

        l, o = lax.fori_loop(
            0, n_tiles, forward, (jnp.zeros((1, span), F32), jnp.zeros((HD, span), F32)))
        inv = 1.0 / l
        got = go_ref[:, cols].astype(F32).T * inv
        gs_t[...] = (got * scale).astype(BF)
        g_rows[...] = got.T.astype(BF)
        centre = jnp.sum(gs_t[...].astype(F32) * (o * inv), axis=0, keepdims=True)
        dqt[...] = jnp.zeros_like(dqt)

        def backward(s, slot):
            def step(t, carry):
                at = rows_at(s, t)
                to = rows_at(0, t)
                kk = k_ref[at, cols]
                p = probs[at, :]
                dp = dot_nn(v_ref[at, cols], gs_t[...])
                ds = (p.astype(F32) * (dp - centre)).astype(BF)
                send[slot, h, 0, to, :] = dot_nn(ds, q_ref[:, cols]).astype(BF)
                send[slot, h, 1, to, :] = dot_nn(p, g_rows[...]).astype(BF)
                dqt[...] += dot_nn(kk.astype(F32).T.astype(BF), ds)
                return carry

            lax.fori_loop(0, tiles, step, 0)

        @pl.when(fr >= 2)
        def _():
            backward(lax.rem(fr + 2, 4), 0)
            half_copy(h).start()

        @pl.when(fr == 3)
        def _():
            backward(0, 2)
            if h == 1:
                add_half(1, 1)
            full_copy(1, h).start()

        @pl.when(fr >= 1)
        def _():
            backward(left, 1)

        if h == 1:
            @pl.when(fr >= 1)
            def _():
                full_copy(0, 1).start()

            @pl.when((fr == 1) | (fr == 2))
            def _():
                add_half(0, 0)
                full_copy(0, 0).start()
        else:
            @pl.when(fr == 3)
            def _():
                full_copy(0, 0).start()

        backward(fr, 3)
        dq_ref[:, cols] = dqt[...].T.astype(BF)

    @pl.when(fr == 0)
    def _():
        half_copy(1).wait_recv()
        send[2, 1] = half_in[1]
        full_copy(1, 1).start()

    def take(side, h):
        full_copy(side, h).wait_recv()
        for j in range(2):
            send[3, h, j] = (send[3, h, j].astype(F32) + full_in[side, h, j].astype(F32)).astype(BF)

    @pl.when(fr <= 2)
    def _():
        take(0, 1)
        take(0, 0)

    @pl.when(fr == 0)
    def _():
        take(1, 0)

    @pl.when(fr <= 1)
    def _():
        take(1, 1)

    for h in range(2):
        cols = pl.ds(h * HD, HD)
        dk_ref[:, cols] = send[3, h, 0]
        dv_ref[:, cols] = send[3, h, 1]

    for h in range(2):
        @pl.when(fr >= 2)
        def _():
            half_copy(h).wait_send()

        @pl.when(fr >= 1)
        def _():
            full_copy(0, h).wait_send()

    @pl.when(fr == 3)
    def _():
        full_copy(1, 0).wait_send()

    @pl.when((fr == 3) | (fr == 0))
    def _():
        full_copy(1, 1).wait_send()


def attention_call(q, k, v, go):
    span, width = q.shape
    vm = pl.BlockSpec(memory_space=pltpu.VMEM)
    dma = pltpu.SemaphoreType.DMA
    return pl.pallas_call(
        attention_kernel,
        out_shape=(jax.ShapeDtypeStruct(q.shape, BF),) * 3,
        in_specs=[vm] * 4,
        out_specs=(vm,) * 3,
        scratch_shapes=[
            pltpu.VMEM((4 * span, span), BF),
            pltpu.VMEM((HD, span), BF),
            pltpu.VMEM((HD, span), BF),
            pltpu.VMEM((HD, span), BF),
            pltpu.VMEM((span, HD), BF),
            pltpu.VMEM((HD, span), F32),
            pltpu.VMEM((4, 2, 2, span, HD), BF),
            pltpu.VMEM((2, 2, span, HD), BF),
            pltpu.VMEM((2, 2, 2, span, HD), BF),
            dma((2,)), dma((2,)), dma((2, 2)), dma((2, 2)),
        ],
        compiler_params=pltpu.CompilerParams(
            collective_id=1, has_side_effects=True, vmem_limit_bytes=VMEM_LIMIT),
        cost_estimate=pl.CostEstimate(flops=10 * 10**9, bytes_accessed=20 * 10**6, transcendentals=0),
        name="attention",
    )(q, k, v, go)


def on_device(
    queries, keys, values, hidden_state, out_grad, stored_pre, expert_ids, gate_weights,
    w_gate, w_up, w_down,
):
    toks = out_grad.shape[0]
    key_all, value_all = (
        lax.all_gather(keys, "frame", axis=0, tiled=True),
        lax.all_gather(values, "frame", axis=0, tiled=True),
    )
    resid, go = moe_call(
        expert_ids.T, gate_weights, out_grad, stored_pre.reshape(toks, -1), hidden_state,
        w_down[0], w_gate[0], w_up[0], queries.shape[1])
    dq, dk, dv = attention_call(queries, key_all, value_all, go)
    return resid, dq, dk, dv


def solution(mesh):
    rows = P(("dp", "frame"), "expert")
    toks = ("dp", "frame", "expert")
    return jax.shard_map(
        on_device,
        mesh=mesh,
        in_specs=(
            rows, rows, rows, P(toks, None), P(toks, None), P(toks, None, None, None),
            P(toks, None), P(toks, None), P("expert", None, "frame"), P("expert", None, "frame"),
            P("expert", "frame", None),
        ),
        out_specs=(P(toks, None), rows, rows, rows),
        check_vma=False,
    )
```

```python
import functools

import jax
import jax.numpy as jnp
from jax import lax
from jax.experimental import pallas as pl
from jax.experimental.pallas import tpu as pltpu
from jax.sharding import PartitionSpec as P

HD = 128
N_EXP = 8
N_FRAME = 4
MAIN = 16
BF = jnp.bfloat16
F32 = jnp.float32
MESH = pl.DeviceIdType.MESH
VMEM_LIMIT = 63 * 1024 * 1024


def dot_nn(a, b):
    return lax.dot_general(a, b, (((1,), (0,)), ((), ())), preferred_element_type=F32)


def dot_nt(a, b):
    return lax.dot_general(a, b, (((1,), (1,)), ((), ())), preferred_element_type=F32)


ZF = 2
RF = 1


def moe_kernel(
    meta_ref, og_ref, st_ref, hs_ref, wd_hbm, wg_hbm, wu_hbm,
    resid_ref, gout_ref,
    wd, wg, wu, rows, stored, hid, grads, ysend, yrecv, zrecv,
    half_in, full_in, dhalf_in, dfull_in, dense, amat, emat, atmat, etmat, raw, meta_in,
    w_sem, ys_sem, yr_sem, zs_sem, zr_sem, ag_s, ag_r, fw_s, fw_r, st_s, st_r,
    ha_s, ha_r, fu_s, fu_r, go_s, go_r, me_s, me_r, ra_s, ra_r, rf_s, rf_r,
    dh_s, dh_r, df_s, df_r,
):
    me = lax.axis_index("expert")
    fr = lax.axis_index("frame")
    left = lax.rem(fr + 3, 4)
    right = lax.rem(fr + 1, 4)
    opposite = lax.rem(fr + 2, 4)
    toks, width = og_ref.shape
    cw = width // 4
    ext = cw // 4
    ff = hid.shape[2]
    n_rows = rows.shape[2]
    half = n_rows // 2
    thalf = toks // 2
    n_blk = N_EXP * MAIN
    n_extra = 3 * ZF

    def chunk_at(c):
        return pl.ds(pl.multiple_of(c * cw, cw), cw)

    def to_frame(src, dst, ss, rs, dest):
        return pltpu.make_async_remote_copy(
            src_ref=src, dst_ref=dst, send_sem=ss, recv_sem=rs,
            device_id={"frame": dest}, device_id_type=MESH)

    def to_side(src, dst, ss, rs, side):
        return to_frame(src, dst, ss, rs, right if side == 0 else left)

    def to_expert(src, dst, ss, rs, dest):
        return pltpu.make_async_remote_copy(
            src_ref=src, dst_ref=dst, send_sem=ss, recv_sem=rs,
            device_id={"expert": dest}, device_id_type=MESH)

    barrier = pltpu.get_barrier_semaphore()
    for d in range(1, N_EXP):
        pl.semaphore_signal(barrier, inc=1, device_id={"expert": lax.rem(me + d, N_EXP)}, device_id_type=MESH)
    for dest in (left, right, opposite):
        pl.semaphore_signal(barrier, inc=1, device_id={"frame": dest}, device_id_type=MESH)

    w_copies = [pltpu.make_async_copy(wd_hbm.at[:, pl.ds(c * cw, cw)], wd.at[c], w_sem.at[c]) for c in range(4)]
    w_copies += [pltpu.make_async_copy(wg_hbm, wg, w_sem.at[4]), pltpu.make_async_copy(wu_hbm, wu, w_sem.at[5])]
    for copy in w_copies:
        copy.start()

    def raw_copy(c, side):
        return to_side(og_ref.at[:, chunk_at(c)], raw.at[side, c], ra_s.at[c, side], ra_r.at[c, side], side)

    def raw_pass(c, side):
        part = pl.ds(side * thalf, thalf)
        return to_side(raw.at[side, c, part], raw.at[2, c, part], rf_s.at[c, side], rf_r.at[c, side], side)

    meta_copies = [
        to_frame(meta_ref, meta_in.at[0], me_s.at[0], me_r.at[0], right),
        to_frame(meta_ref, meta_in.at[1], me_s.at[1], me_r.at[1], left),
        to_frame(meta_ref, meta_in.at[2], me_s.at[2], me_r.at[2], opposite),
    ]
    pl.semaphore_wait(barrier, N_EXP + 2)
    for copy in meta_copies:
        copy.start()
    for c in range(ZF):
        for side in range(2):
            raw_copy(c, side).start()

    earlier_mask = (
        lax.broadcasted_iota(jnp.int32, (toks, toks), 0) < lax.broadcasted_iota(jnp.int32, (toks, toks), 1)
    ).astype(F32).astype(BF)
    expert_iota = lax.broadcasted_iota(jnp.int32, (N_EXP, toks), 0)
    main_iota = lax.broadcasted_iota(jnp.int32, (2 * n_blk, toks), 0)
    ext_iota = lax.broadcasted_iota(jnp.int32, (n_blk, toks), 0)

    def routing(b, meta):
        base = jnp.zeros((N_EXP, 1), F32)
        main_sum = jnp.zeros(main_iota.shape, F32)
        ext_sum = [jnp.zeros(ext_iota.shape, F32) for _ in range(4)]
        for k in range(2):
            rel = (meta[k:k + 1, :].astype(jnp.int32) - me + N_EXP) & (N_EXP - 1)
            hit = (expert_iota == rel).astype(F32)
            earlier = dot_nn(hit.astype(BF), earlier_mask) + base
            slot = jnp.sum(hit * earlier, axis=0, keepdims=True).astype(jnp.int32)
            base = base + jnp.sum(hit, axis=1, keepdims=True)
            main_at = jnp.where(slot < 32, (slot >> 4) * n_blk + rel * MAIN + (slot & 15), -1)
            ext_at = jnp.where(slot < 32, -1000, rel * MAIN + slot - 32)
            main_k = (main_iota == main_at).astype(F32)
            amat[:, pl.ds(k * toks, toks)] = main_k.astype(BF)
            main_sum = main_sum + main_k
            for j in range(4):
                ext_k = (ext_iota == ext_at + 4 * j).astype(F32)
                emat[j, :, pl.ds(k * toks, toks)] = ext_k.astype(BF)
                ext_sum[j] = ext_sum[j] + ext_k
        atmat[b] = main_sum.T.astype(BF)
        for j in range(4):
            etmat[b, j] = ext_sum[j].T.astype(BF)
        return meta.T

    def pack_pairs(slot, at, pairs):
        main = dot_nn(amat[...], pairs).astype(BF)
        extra = dot_nn(emat[0], pairs[:, :ext])
        for j in range(1, 4):
            extra = extra + dot_nn(emat[j], pairs[:, j * ext:(j + 1) * ext])
        extra = extra.astype(BF)
        for lo, w, part in ((0, cw, main[:n_blk]), (cw, cw, main[n_blk:]), (2 * cw, ext, extra)):
            ysend[slot, :, pl.ds(lo, w)] = part
            yrecv[at, pl.ds(0, MAIN), pl.ds(lo, w)] = part[:MAIN]

    def pack_tokens(slot, at, x, weights):
        x = x.astype(F32)
        pack_pairs(slot, at, jnp.concatenate(
            [(weights[:, 2:3] * x).astype(BF), (weights[:, 3:4] * x).astype(BF)], axis=0))

    def y_copy(slot, at, d):
        return to_expert(
            ysend.at[slot, pl.ds(MAIN * d, MAIN)], yrecv.at[at, pl.ds(MAIN * d, MAIN)],
            ys_sem.at[at, d], yr_sem.at[at, d], lax.rem(me + d, N_EXP))

    def y_start(slot, at):
        for d in range(1, N_EXP):
            y_copy(slot, at, d).start()

    def y_sent(slot, at):
        for d in range(1, N_EXP):
            y_copy(slot, at, d).wait_send()

    own_weights = routing(0, meta_ref[...])

    def build_rows(c, carry):
        pack_tokens(c, c, og_ref[:, chunk_at(c)], own_weights)
        y_start(c, c)
        return carry

    def build_stored(c, carry):
        f = lax.rem(fr + c, 4)
        parts = []
        for k in range(2):
            parts.append(jnp.concatenate(
                [st_ref[:, pl.ds(pl.multiple_of((k * 2 + kind) * 4 * ff + f * ff, ff), ff)] for kind in range(2)], axis=1))
        pack_pairs(4 + c, 4 + c, jnp.concatenate(parts, axis=0))
        y_start(4 + c, 4 + c)
        return carry

    lax.fori_loop(ZF, 4, build_rows, 0)
    lax.fori_loop(0, 4, build_stored, 0)
    lax.fori_loop(0, ZF, build_rows, 0)

    sel_r = lax.broadcasted_iota(jnp.int32, (4 * N_EXP, n_blk), 0)
    sel_c = lax.broadcasted_iota(jnp.int32, (4 * N_EXP, n_blk), 1)
    selt_r = lax.broadcasted_iota(jnp.int32, (n_blk, 4 * N_EXP), 1)
    selt_c = lax.broadcasted_iota(jnp.int32, (n_blk, 4 * N_EXP), 0)

    def unpack(slot, at, dst):
        for d in range(1, N_EXP):
            y_copy(slot, at, d).wait_recv()
        dst[pl.ds(0, n_blk), :] = yrecv[at, :, pl.ds(0, cw)]
        dst[pl.ds(n_blk, n_blk), :] = yrecv[at, :, pl.ds(cw, cw)]
        extra = yrecv[at, :, pl.ds(2 * cw, ext)]
        for j in range(4):
            sel = (sel_c == (sel_r >> 2) * MAIN + 4 * j + (sel_r & 3)).astype(F32).astype(BF)
            dst[pl.ds(2 * n_blk, 4 * N_EXP), pl.ds(j * ext, ext)] = dot_nn(sel, extra).astype(BF)

    def ag_copy(c, side):
        return to_side(rows.at[0, c], rows.at[1 + side, c], ag_s.at[c, side], ag_r.at[c, side], side)

    def fw_copy(c, side):
        part = pl.ds(side * half, half)
        return to_side(rows.at[1 + side, c, part], rows.at[3, c, part], fw_s.at[c, side], fw_r.at[c, side], side)

    def add_hidden(b, c):
        hid[b] += dot_nt(rows[b, c], wd[c])

    for c in range(ZF):
        for side in range(2):
            raw_copy(c, side).wait_recv()
            raw_pass(c, side).start()

    def own_rows(c, carry):
        unpack(c, c, rows.at[0, c])
        ag_copy(c, 0).start()
        ag_copy(c, 1).start()
        return carry

    lax.fori_loop(ZF, 4, own_rows, 0)

    for copy in meta_copies:
        copy.wait_recv()
    for b in range(1, 4):
        weights = routing(b, meta_in[b - 1])
        for c in range(ZF):
            i = (b - 1) * ZF + c
            if b == 3:
                for side in range(2):
                    raw_pass(c, side).wait_recv()
            y_sent(i, i)
            pack_tokens(i, 8 + i, raw[b - 1, c], weights)
            y_start(i, 8 + i)

    hid[...] = jnp.zeros_like(hid)
    for copy in w_copies[:4]:
        copy.wait()

    def next_rows(c, carry):
        for side in range(2):
            ag_copy(c, side).wait_recv()
            fw_copy(c, side).start()
        add_hidden(0, c)
        add_hidden(1, c)
        add_hidden(2, c)
        return carry

    lax.fori_loop(ZF, 4, next_rows, 0)

    def own_stored(c, carry):
        unpack(4 + c, 4 + c, grads.at[c])
        return carry

    lax.fori_loop(0, 4, own_stored, 0)
    st_copies = [
        to_frame(grads.at[1], stored.at[0], st_s.at[0], st_r.at[0], right),
        to_frame(grads.at[3], stored.at[1], st_s.at[1], st_r.at[1], left),
        to_frame(grads.at[2], stored.at[2], st_s.at[2], st_r.at[2], opposite),
    ]
    for i in (2, 0, 1):
        st_copies[i].start()

    for c in range(ZF):
        unpack(c, c, rows.at[0, c])
        add_hidden(0, c)

    def far_rows(c, carry):
        for side in range(2):
            fw_copy(c, side).wait_recv()
        add_hidden(3, c)
        return carry

    lax.fori_loop(ZF, 4, far_rows, 0)

    for b in range(1, 4):
        for c in range(ZF):
            i = (b - 1) * ZF + c
            unpack(i, 8 + i, rows.at[b, c])
            add_hidden(b, c)

    def hidden_to_grads(b, src):
        h = hid[b]
        g = src[:, pl.ds(0, ff)].astype(F32)
        u = src[:, pl.ds(ff, ff)].astype(F32)
        s = 1.0 / (1.0 + jnp.exp(-g))
        gate = (h * u * s * (1.0 + g * (1.0 - s))).astype(BF)
        up = (h * g * s).astype(BF)
        grads[b, :, pl.ds(0, ff)] = gate
        grads[b, :, pl.ds(ff, ff)] = up

    for i in (2, 0, 1):
        st_copies[i].wait()
    for b in (3, 2, 1, 0):
        hidden_to_grads(b, grads.at[0] if b == 0 else stored.at[b - 1])

    for copy in w_copies[4:]:
        copy.wait()

    def term(b, c):
        at = chunk_at(c)
        return dot_nt(grads[b, :, pl.ds(0, ff)], wg[at, :]) + dot_nt(grads[b, :, pl.ds(ff, ff)], wu[at, :])

    def ha_copy(c, side):
        return to_side(rows.at[3, c, pl.ds(side * half, half)], half_in.at[side, c - RF],
                       ha_s.at[c, side], ha_r.at[c, side], side)

    def fu_copy(c, side):
        return to_side(rows.at[2 - side, c], full_in.at[side, c - RF], fu_s.at[c, side], fu_r.at[c, side], side)

    def far_terms(c, carry):
        rows[3, c] = term(3, c).astype(BF)
        for side in range(2):
            ha_copy(c, side).start()
        return carry

    lax.fori_loop(RF, 4, far_terms, 0)

    def settle(i, carry):
        y_sent(lax.rem(i, 8), i)
        return carry

    lax.fori_loop(n_extra, 8 + n_extra, settle, 0)

    def z_copy(slot, d):
        return to_expert(
            ysend.at[slot, pl.ds(MAIN * d, MAIN)], zrecv.at[slot, pl.ds(MAIN * d, MAIN)],
            zs_sem.at[slot, d], zr_sem.at[slot, d], lax.rem(me + N_EXP - d, N_EXP))

    def send_back(slot, total):
        extra = jnp.zeros((n_blk, ext), F32)
        for j in range(4):
            sel = (selt_c == (selt_r >> 2) * MAIN + 4 * j + (selt_r & 3)).astype(F32).astype(BF)
            extra = extra + dot_nn(sel, total[2 * n_blk:, j * ext:(j + 1) * ext])
        extra = extra.astype(BF)
        for lo, w, part in ((0, cw, total[:n_blk]), (cw, cw, total[n_blk:2 * n_blk]), (2 * cw, ext, extra)):
            ysend[slot, :, pl.ds(lo, w)] = part
            zrecv[slot, pl.ds(0, MAIN), pl.ds(lo, w)] = part[:MAIN]
        for d in range(1, N_EXP):
            z_copy(slot, d).start()

    def tokens_of(slot, b):
        for d in range(1, N_EXP):
            z_copy(slot, d).wait_recv()
        got = dot_nn(atmat[b, :, pl.ds(0, n_blk)], zrecv[slot, :, pl.ds(0, cw)])
        got = got + dot_nn(atmat[b, :, pl.ds(n_blk, n_blk)], zrecv[slot, :, pl.ds(cw, cw)])
        extra = zrecv[slot, :, pl.ds(2 * cw, ext)]
        return got + jnp.concatenate([dot_nn(etmat[b, j], extra) for j in range(4)], axis=1)

    for c in range(RF):
        for b in (3, 2, 1, 0):
            send_back(4 + 4 * c + b, term(b, c).astype(BF))

    def near_terms(c, carry):
        for side in range(2):
            @pl.when(c >= ZF)
            def _():
                fw_copy(c, 1 - side).wait_send()
            part = term(2 - side, c)
            ha_copy(c, side).wait_recv()
            lo = side * half
            rows[2 - side, c, pl.ds(half - lo, half)] = part[half - lo:half - lo + half].astype(BF)
            rows[2 - side, c, pl.ds(lo, half)] = (
                part[lo:lo + half].astype(BF).astype(F32) + half_in[side, c - RF].astype(F32)).astype(BF)
            fu_copy(c, side).start()
        return carry

    lax.fori_loop(RF, 4, near_terms, 0)

    def put_moe(c, got):
        hid[c, pl.ds(0, toks), :] = got[:, :cw // 2]
        hid[c, pl.ds(toks, toks), :] = got[:, cw // 2:]

    def get_moe(c):
        return jnp.concatenate([hid[c, pl.ds(0, toks), :], hid[c, pl.ds(toks, toks), :]], axis=1)

    def dh_copy(c, side):
        part = pl.ds(side * thalf, thalf)
        return to_side(dense.at[c, 2, part], dhalf_in.at[side, c], dh_s.at[c, side], dh_r.at[c, side], side)

    def df_copy(c, side):
        return to_side(dense.at[c, 1 - side], dfull_in.at[side, c], df_s.at[c, side], df_r.at[c, side], side)

    for c in range(RF):
        dense[c, 2] = tokens_of(4 + 4 * c + 3, 3).astype(BF)
        for side in range(2):
            dh_copy(c, side).start()
        for side in range(2):
            b = 2 - side
            dense[c, b - 1] = tokens_of(4 + 4 * c + b, b).astype(BF)
        for side in range(2):
            b = 2 - side
            part = pl.ds(side * thalf, thalf)
            dh_copy(c, side).wait_recv()
            dense[c, b - 1, part] = (
                dense[c, b - 1, part].astype(F32) + dhalf_in[side, c].astype(F32)).astype(BF)
            df_copy(c, side).start()
        put_moe(c, tokens_of(4 + 4 * c, 0))

    def own_terms(c, carry):
        part = term(0, c).astype(BF).astype(F32)
        for side in range(2):
            fu_copy(c, side).wait_recv()
        send_back(c, (part + full_in[0, c - RF].astype(F32) + full_in[1, c - RF].astype(F32)).astype(BF))
        return carry

    lax.fori_loop(RF, 4, own_terms, 0)

    def square_sum(c, acc):
        x = hs_ref[:, chunk_at(c)].astype(F32)
        return acc + jnp.sum(x * x, axis=1, keepdims=True)

    inv = lax.rsqrt(lax.fori_loop(0, 4, square_sum, jnp.zeros((toks, 1), F32)) / width + 1e-6)

    def combine(c, acc):
        got = tokens_of(c, 0)
        put_moe(c, got)
        return acc + jnp.sum(got * hs_ref[:, chunk_at(c)].astype(F32), axis=1, keepdims=True)

    mean = lax.fori_loop(RF, 4, combine, jnp.zeros((toks, 1), F32))
    for c in range(RF):
        at = pl.ds(c * cw, cw)
        got = get_moe(c)
        for side in range(2):
            df_copy(c, side).wait_recv()
            got = got + dfull_in[side, c].astype(F32)
        put_moe(c, got)
        mean = mean + jnp.sum(got * hs_ref[:, at].astype(F32), axis=1, keepdims=True)
    mean = mean * inv / width

    def residual(c, carry):
        at = chunk_at(c)
        n = hs_ref[:, at].astype(F32) * inv
        resid_ref[:, at] = (og_ref[:, at].astype(F32) + inv * (get_moe(c) - n * mean)).astype(BF)
        return carry

    hw = gout_ref.shape[1]
    own_at = pl.ds(pl.multiple_of(me * toks, toks), toks)

    def go_copy(d):
        dest = lax.rem(me + d, N_EXP)
        return to_expert(
            resid_ref.at[:, pl.ds(pl.multiple_of(dest * hw, hw), hw)], gout_ref.at[own_at],
            go_s.at[d], go_r.at[d], dest)

    lax.fori_loop(0, 2, residual, 0)
    for d in range(1, N_EXP):
        go_copy(d).start()
    gout_ref[own_at, :] = resid_ref[:, pl.ds(pl.multiple_of(me * hw, hw), hw)]
    lax.fori_loop(2, 4, residual, 0)

    for copy in meta_copies:
        copy.wait_send()
    for c in range(ZF):
        for side in range(2):
            raw_copy(c, side).wait_send()
            raw_pass(c, side).wait_send()
    for c in range(RF):
        for side in range(2):
            dh_copy(c, side).wait_send()
            df_copy(c, side).wait_send()

    def drain(c, carry):
        for side in range(2):
            ag_copy(c, side).wait_send()
        return carry

    def drain_back(c, carry):
        for side in range(2):
            ha_copy(c, side).wait_send()
            fu_copy(c, side).wait_send()
        return carry

    def drain_z(slot, carry):
        for d in range(1, N_EXP):
            z_copy(slot, d).wait_send()
        return carry

    lax.fori_loop(ZF, 4, drain, 0)
    lax.fori_loop(RF, 4, drain_back, 0)
    lax.fori_loop(RF, 4 + 4 * RF, drain_z, 0)
    for c in range(ZF, RF):
        for side in range(2):
            fw_copy(c, side).wait_send()
    for d in range(1, N_EXP):
        go_copy(d).wait()


def moe_call(meta, out_grad, stored, hidden_state, wd, wg, wu, att_local):
    toks, width = out_grad.shape
    ff = wd.shape[0]
    cw = width // 4
    n_rows = N_EXP * 36
    n_blk = N_EXP * MAIN
    pw = 2 * cw + cw // 4
    vm = pl.BlockSpec(memory_space=pltpu.VMEM)
    hbm = pl.BlockSpec(memory_space=pl.ANY)
    dma = pltpu.SemaphoreType.DMA
    slots = 8 + 3 * ZF
    back = 4 + 4 * RF
    rf = max(RF, 1)
    zf = max(ZF, 1)
    return pl.pallas_call(
        moe_kernel,
        out_shape=(
            jax.ShapeDtypeStruct((toks, width), BF),
            jax.ShapeDtypeStruct((toks * N_EXP, att_local), BF),
        ),
        in_specs=[vm] * 4 + [hbm] * 3,
        out_specs=(vm, vm),
        scratch_shapes=[
            pltpu.VMEM((4, ff, cw), BF),
            pltpu.VMEM((width, ff), BF),
            pltpu.VMEM((width, ff), BF),
            pltpu.VMEM((4, 4, n_rows, cw), BF),
            pltpu.VMEM((3, n_rows, 2 * ff), BF),
            pltpu.VMEM((4, n_rows, ff), F32),
            pltpu.VMEM((4, n_rows, 2 * ff), BF),
            pltpu.VMEM((8, n_blk, pw), BF),
            pltpu.VMEM((slots, n_blk, pw), BF),
            pltpu.VMEM((back, n_blk, pw), BF),
            pltpu.VMEM((2, 4 - RF, n_rows // 2, cw), BF),
            pltpu.VMEM((2, 4 - RF, n_rows, cw), BF),
            pltpu.VMEM((2, rf, toks // 2, cw), BF),
            pltpu.VMEM((2, rf, toks, cw), BF),
            pltpu.VMEM((rf, 3, toks, cw), BF),
            pltpu.VMEM((2 * n_blk, 2 * toks), BF),
            pltpu.VMEM((4, n_blk, 2 * toks), BF),
            pltpu.VMEM((4, toks, 2 * n_blk), BF),
            pltpu.VMEM((4, 4, toks, n_blk), BF),
            pltpu.VMEM((3, zf, toks, cw), BF),
            pltpu.VMEM((3, 8, toks), F32),
            dma((6,)), dma((slots, 8)), dma((slots, 8)), dma((back, 8)), dma((back, 8)),
            dma((4, 2)), dma((4, 2)), dma((4, 2)), dma((4, 2)), dma((3,)), dma((3,)),
            dma((4, 2)), dma((4, 2)), dma((4, 2)), dma((4, 2)), dma((8,)), dma((8,)),
            dma((3,)), dma((3,)), dma((zf, 2)), dma((zf, 2)), dma((zf, 2)), dma((zf, 2)),
            dma((rf, 2)), dma((rf, 2)), dma((rf, 2)), dma((rf, 2)),
        ],
        compiler_params=pltpu.CompilerParams(
            collective_id=0, has_side_effects=True, vmem_limit_bytes=VMEM_LIMIT),
        cost_estimate=pl.CostEstimate(flops=15 * 10**9, bytes_accessed=20 * 10**6, transcendentals=0),
        name="moe",
    )(meta, out_grad, stored, hidden_state, wd, wg, wu)


def attention_kernel(
    q_ref, k_ref, v_ref, go_ref, dq_ref, dk_ref, dv_ref,
    probs, qt, mx, gs_t, g_rows, dqt, send, half_in, full_in,
    hs, hr, fs, fr_sem,
):
    fr = lax.axis_index("frame")
    left = lax.rem(fr + 3, 4)
    right = lax.rem(fr + 1, 4)
    span = q_ref.shape[0]
    scale = HD ** -0.5
    log2e = 1.4426950408889634

    barrier = pltpu.get_barrier_semaphore()
    for dest in (left, right):
        pl.semaphore_signal(barrier, inc=1, device_id={"frame": dest}, device_id_type=MESH)
    pl.semaphore_wait(barrier, 2)

    def to_frame(src, dst, ss, rs, dest):
        return pltpu.make_async_remote_copy(
            src_ref=src, dst_ref=dst, send_sem=ss, recv_sem=rs,
            device_id={"frame": dest}, device_id_type=MESH)

    def half_copy(h):
        return to_frame(send.at[0, h], half_in.at[h], hs.at[h], hr.at[h], left if h == 0 else right)

    def full_copy(side, h):
        return to_frame(send.at[1 + side, h], full_in.at[side, h], fs.at[side, h], fr_sem.at[side, h],
                        left if side == 0 else right)

    def add_half(side, h):
        half_copy(h).wait_recv()
        for j in range(2):
            send[1 + side, h, j] = (send[1 + side, h, j].astype(F32) + half_in[h, j].astype(F32)).astype(BF)

    def krows(s):
        return pl.ds(pl.multiple_of(s * span, span), span)

    for h in range(2):
        cols = pl.ds(h * HD, HD)
        qt[...] = q_ref[:, cols].astype(F32).T.astype(BF)

        def forward(s, carry):
            m, l, o = carry
            v_t = v_ref[krows(s), cols].astype(F32).T.astype(BF)
            sc = dot_nn(k_ref[krows(s), cols], qt[...])
            m_new = jnp.maximum(m, jnp.max(sc, axis=0, keepdims=True) * (scale * log2e))
            old = jnp.exp2(m - m_new)
            p = jnp.exp2(sc * (scale * log2e) - m_new)
            low = p.astype(BF)
            probs[krows(s), :] = low
            mx[pl.ds(pl.multiple_of(8 * s, 8), 1), :] = m_new
            return m_new, l * old + jnp.sum(p, axis=0, keepdims=True), o * old + dot_nn(v_t, low)

        m, l, o = lax.fori_loop(0, fr + 1, forward, (
            jnp.full((1, span), -jnp.inf, F32), jnp.zeros((1, span), F32), jnp.zeros((HD, span), F32)))
        inv = 1.0 / l
        gs_t[...] = go_ref[:, cols].astype(F32).T * (inv * scale)
        centre = jnp.sum(gs_t[...] * (o * inv), axis=0, keepdims=True)
        dqt[...] = jnp.zeros_like(dqt)

        def backward(s, slot):
            f = jnp.exp2(mx[pl.ds(pl.multiple_of(8 * s, 8), 1), :] - m)
            gt = (gs_t[...] * f).astype(BF)
            g_rows[...] = (gs_t[...] * (f * (1.0 / scale))).T.astype(BF)
            k_t = k_ref[krows(s), cols].astype(F32).T.astype(BF)
            p = probs[krows(s), :]
            dp = dot_nn(v_ref[krows(s), cols], gt)
            ds = (p.astype(F32) * (dp - centre * f)).astype(BF)
            send[slot, h, 0] = dot_nn(ds, q_ref[:, cols]).astype(BF)
            send[slot, h, 1] = dot_nn(p, g_rows[...]).astype(BF)
            dqt[...] += dot_nn(k_t, ds)

        @pl.when(fr >= 2)
        def _():
            backward(lax.rem(fr + 2, 4), 0)
            half_copy(h).start()

        @pl.when(fr == 3)
        def _():
            backward(0, 2)
            if h == 1:
                add_half(1, 1)
            full_copy(1, h).start()

        @pl.when(fr >= 1)
        def _():
            backward(left, 1)

        if h == 1:
            @pl.when(fr >= 1)
            def _():
                full_copy(0, 1).start()

            @pl.when((fr == 1) | (fr == 2))
            def _():
                add_half(0, 0)
                full_copy(0, 0).start()
        else:
            @pl.when(fr == 3)
            def _():
                full_copy(0, 0).start()

        backward(fr, 3)
        dq_ref[:, cols] = dqt[...].T.astype(BF)

    @pl.when(fr == 0)
    def _():
        half_copy(1).wait_recv()
        send[2, 1] = half_in[1]
        full_copy(1, 1).start()

    def take(side, h):
        full_copy(side, h).wait_recv()
        for j in range(2):
            send[3, h, j] = (send[3, h, j].astype(F32) + full_in[side, h, j].astype(F32)).astype(BF)

    @pl.when(fr <= 2)
    def _():
        take(0, 1)
        take(0, 0)

    @pl.when(fr == 0)
    def _():
        take(1, 0)

    @pl.when(fr <= 1)
    def _():
        take(1, 1)

    for h in range(2):
        cols = pl.ds(h * HD, HD)
        dk_ref[:, cols] = send[3, h, 0]
        dv_ref[:, cols] = send[3, h, 1]

    for h in range(2):
        @pl.when(fr >= 2)
        def _():
            half_copy(h).wait_send()

        @pl.when(fr >= 1)
        def _():
            full_copy(0, h).wait_send()

    @pl.when(fr == 3)
    def _():
        full_copy(1, 0).wait_send()

    @pl.when((fr == 3) | (fr == 0))
    def _():
        full_copy(1, 1).wait_send()


def attention_call(q, k, v, go):
    span, width = q.shape
    vm = pl.BlockSpec(memory_space=pltpu.VMEM)
    dma = pltpu.SemaphoreType.DMA
    return pl.pallas_call(
        attention_kernel,
        out_shape=(jax.ShapeDtypeStruct(q.shape, BF),) * 3,
        in_specs=[vm] * 4,
        out_specs=(vm,) * 3,
        scratch_shapes=[
            pltpu.VMEM((4 * span, span), BF),
            pltpu.VMEM((HD, span), BF),
            pltpu.VMEM((32, span), F32),
            pltpu.VMEM((HD, span), F32),
            pltpu.VMEM((span, HD), BF),
            pltpu.VMEM((HD, span), F32),
            pltpu.VMEM((4, 2, 2, span, HD), BF),
            pltpu.VMEM((2, 2, span, HD), BF),
            pltpu.VMEM((2, 2, 2, span, HD), BF),
            dma((2,)), dma((2,)), dma((2, 2)), dma((2, 2)),
        ],
        compiler_params=pltpu.CompilerParams(
            collective_id=1, has_side_effects=True, vmem_limit_bytes=VMEM_LIMIT),
        cost_estimate=pl.CostEstimate(flops=10 * 10**9, bytes_accessed=20 * 10**6, transcendentals=0),
        name="attention",
    )(q, k, v, go)


def on_device(
    queries, keys, values, hidden_state, out_grad, stored_pre, expert_ids, gate_weights,
    w_gate, w_up, w_down,
):
    toks = out_grad.shape[0]
    key_all, value_all = (
        lax.all_gather(keys, "frame", axis=0, tiled=True),
        lax.all_gather(values, "frame", axis=0, tiled=True),
    )
    meta = jnp.concatenate(
        [expert_ids.astype(F32).T, gate_weights.T, jnp.zeros((4, toks), F32)], axis=0)
    resid, go = moe_call(
        meta, out_grad, stored_pre.reshape(toks, -1), hidden_state,
        w_down[0], w_gate[0], w_up[0], queries.shape[1])
    dq, dk, dv = attention_call(queries, key_all, value_all, go)
    return resid, dq, dk, dv


def solution(mesh):
    rows = P(("dp", "frame"), "expert")
    toks = ("dp", "frame", "expert")
    return jax.shard_map(
        on_device,
        mesh=mesh,
        in_specs=(
            rows, rows, rows, P(toks, None), P(toks, None), P(toks, None, None, None),
            P(toks, None), P(toks, None), P("expert", None, "frame"), P("expert", None, "frame"),
            P("expert", "frame", None),
        ),
        out_specs=(P(toks, None), rows, rows, rows),
        check_vma=False,
    )
```

```python
import functools

import jax
import jax.numpy as jnp
from jax import lax
from jax.experimental import pallas as pl
from jax.experimental.pallas import tpu as pltpu
from jax.sharding import PartitionSpec as P

HD = 128
N_EXP = 8
N_FRAME = 4
MAIN = 16
BF = jnp.bfloat16
F32 = jnp.float32
MESH = pl.DeviceIdType.MESH
VMEM_LIMIT = 63 * 1024 * 1024


def dot_nn(a, b):
    return lax.dot_general(a, b, (((1,), (0,)), ((), ())), preferred_element_type=F32)


def dot_nt(a, b):
    return lax.dot_general(a, b, (((1,), (1,)), ((), ())), preferred_element_type=F32)


ZF = 2
RF = 1


def moe_kernel(
    meta_ref, og_ref, st_ref, hs_ref, wd_hbm, wg_hbm, wu_hbm, k_hbm, v_hbm,
    resid_ref, gout_ref, k_far, v_far,
    wd, wg, wu, rows, stored, hid, grads, ysend, yrecv, zrecv,
    half_in, full_in, dhalf_in, dfull_in, dense, amat, emat, atmat, etmat, raw, meta_in,
    w_sem, ys_sem, yr_sem, zs_sem, zr_sem, ag_s, ag_r, fw_s, fw_r, st_s, st_r,
    ha_s, ha_r, fu_s, fu_r, go_s, go_r, me_s, me_r, ra_s, ra_r, rf_s, rf_r,
    dh_s, dh_r, df_s, df_r, kv_s, kv_r,
):
    me = lax.axis_index("expert")
    fr = lax.axis_index("frame")
    left = lax.rem(fr + 3, 4)
    right = lax.rem(fr + 1, 4)
    opposite = lax.rem(fr + 2, 4)
    toks, width = og_ref.shape
    cw = width // 4
    ext = cw // 4
    ff = hid.shape[2]
    n_rows = rows.shape[2]
    half = n_rows // 2
    thalf = toks // 2
    n_blk = N_EXP * MAIN
    n_extra = 3 * ZF

    def chunk_at(c):
        return pl.ds(pl.multiple_of(c * cw, cw), cw)

    def to_frame(src, dst, ss, rs, dest):
        return pltpu.make_async_remote_copy(
            src_ref=src, dst_ref=dst, send_sem=ss, recv_sem=rs,
            device_id={"frame": dest}, device_id_type=MESH)

    def to_side(src, dst, ss, rs, side):
        return to_frame(src, dst, ss, rs, right if side == 0 else left)

    def to_expert(src, dst, ss, rs, dest):
        return pltpu.make_async_remote_copy(
            src_ref=src, dst_ref=dst, send_sem=ss, recv_sem=rs,
            device_id={"expert": dest}, device_id_type=MESH)

    barrier = pltpu.get_barrier_semaphore()
    for d in range(1, N_EXP):
        pl.semaphore_signal(barrier, inc=1, device_id={"expert": lax.rem(me + d, N_EXP)}, device_id_type=MESH)
    for dest in (left, right, opposite):
        pl.semaphore_signal(barrier, inc=1, device_id={"frame": dest}, device_id_type=MESH)

    w_copies = [pltpu.make_async_copy(wd_hbm.at[:, pl.ds(c * cw, cw)], wd.at[c], w_sem.at[c]) for c in range(4)]
    w_copies += [pltpu.make_async_copy(wg_hbm, wg, w_sem.at[4]), pltpu.make_async_copy(wu_hbm, wu, w_sem.at[5])]
    for copy in w_copies:
        copy.start()

    def raw_copy(c, side):
        return to_side(og_ref.at[:, chunk_at(c)], raw.at[side, c], ra_s.at[c, side], ra_r.at[c, side], side)

    def raw_pass(c, side):
        part = pl.ds(side * thalf, thalf)
        return to_side(raw.at[side, c, part], raw.at[2, c, part], rf_s.at[c, side], rf_r.at[c, side], side)

    meta_copies = [
        to_frame(meta_ref, meta_in.at[0], me_s.at[0], me_r.at[0], right),
        to_frame(meta_ref, meta_in.at[1], me_s.at[1], me_r.at[1], left),
        to_frame(meta_ref, meta_in.at[2], me_s.at[2], me_r.at[2], opposite),
    ]
    pl.semaphore_wait(barrier, N_EXP + 2)
    for copy in meta_copies:
        copy.start()
    for c in range(ZF):
        for side in range(2):
            raw_copy(c, side).start()

    earlier_mask = (
        lax.broadcasted_iota(jnp.int32, (toks, toks), 0) < lax.broadcasted_iota(jnp.int32, (toks, toks), 1)
    ).astype(F32).astype(BF)
    expert_iota = lax.broadcasted_iota(jnp.int32, (N_EXP, toks), 0)
    main_iota = lax.broadcasted_iota(jnp.int32, (2 * n_blk, toks), 0)
    ext_iota = lax.broadcasted_iota(jnp.int32, (n_blk, toks), 0)

    def routing(b, meta):
        base = jnp.zeros((N_EXP, 1), F32)
        main_sum = jnp.zeros(main_iota.shape, F32)
        ext_sum = [jnp.zeros(ext_iota.shape, F32) for _ in range(4)]
        for k in range(2):
            rel = (meta[k:k + 1, :].astype(jnp.int32) - me + N_EXP) & (N_EXP - 1)
            hit = (expert_iota == rel).astype(F32)
            earlier = dot_nn(hit.astype(BF), earlier_mask) + base
            slot = jnp.sum(hit * earlier, axis=0, keepdims=True).astype(jnp.int32)
            base = base + jnp.sum(hit, axis=1, keepdims=True)
            main_at = jnp.where(slot < 32, (slot >> 4) * n_blk + rel * MAIN + (slot & 15), -1)
            ext_at = jnp.where(slot < 32, -1000, rel * MAIN + slot - 32)
            main_k = (main_iota == main_at).astype(F32)
            amat[:, pl.ds(k * toks, toks)] = main_k.astype(BF)
            main_sum = main_sum + main_k
            for j in range(4):
                ext_k = (ext_iota == ext_at + 4 * j).astype(F32)
                emat[j, :, pl.ds(k * toks, toks)] = ext_k.astype(BF)
                ext_sum[j] = ext_sum[j] + ext_k
        atmat[b] = main_sum.T.astype(BF)
        for j in range(4):
            etmat[b, j] = ext_sum[j].T.astype(BF)
        return meta.T

    def pack_pairs(slot, at, pairs):
        main = dot_nn(amat[...], pairs).astype(BF)
        extra = dot_nn(emat[0], pairs[:, :ext])
        for j in range(1, 4):
            extra = extra + dot_nn(emat[j], pairs[:, j * ext:(j + 1) * ext])
        extra = extra.astype(BF)
        for lo, w, part in ((0, cw, main[:n_blk]), (cw, cw, main[n_blk:]), (2 * cw, ext, extra)):
            ysend[slot, :, pl.ds(lo, w)] = part
            yrecv[at, pl.ds(0, MAIN), pl.ds(lo, w)] = part[:MAIN]

    def pack_tokens(slot, at, x, weights):
        x = x.astype(F32)
        pack_pairs(slot, at, jnp.concatenate(
            [(weights[:, 2:3] * x).astype(BF), (weights[:, 3:4] * x).astype(BF)], axis=0))

    def y_copy(slot, at, d):
        return to_expert(
            ysend.at[slot, pl.ds(MAIN * d, MAIN)], yrecv.at[at, pl.ds(MAIN * d, MAIN)],
            ys_sem.at[at, d], yr_sem.at[at, d], lax.rem(me + d, N_EXP))

    def y_start(slot, at):
        for d in range(1, N_EXP):
            y_copy(slot, at, d).start()

    def y_sent(slot, at):
        for d in range(1, N_EXP):
            y_copy(slot, at, d).wait_send()

    own_weights = routing(0, meta_ref[...])

    def build_rows(c, carry):
        pack_tokens(c, c, og_ref[:, chunk_at(c)], own_weights)
        y_start(c, c)
        return carry

    def build_stored(c, carry):
        f = lax.rem(fr + c, 4)
        parts = []
        for k in range(2):
            parts.append(jnp.concatenate(
                [st_ref[:, pl.ds(pl.multiple_of((k * 2 + kind) * 4 * ff + f * ff, ff), ff)] for kind in range(2)], axis=1))
        pack_pairs(4 + c, 4 + c, jnp.concatenate(parts, axis=0))
        y_start(4 + c, 4 + c)
        return carry

    lax.fori_loop(ZF, 4, build_rows, 0)
    lax.fori_loop(0, 4, build_stored, 0)
    lax.fori_loop(0, ZF, build_rows, 0)

    sel_r = lax.broadcasted_iota(jnp.int32, (4 * N_EXP, n_blk), 0)
    sel_c = lax.broadcasted_iota(jnp.int32, (4 * N_EXP, n_blk), 1)
    selt_r = lax.broadcasted_iota(jnp.int32, (n_blk, 4 * N_EXP), 1)
    selt_c = lax.broadcasted_iota(jnp.int32, (n_blk, 4 * N_EXP), 0)

    def unpack(slot, at, dst):
        for d in range(1, N_EXP):
            y_copy(slot, at, d).wait_recv()
        dst[pl.ds(0, n_blk), :] = yrecv[at, :, pl.ds(0, cw)]
        dst[pl.ds(n_blk, n_blk), :] = yrecv[at, :, pl.ds(cw, cw)]
        extra = yrecv[at, :, pl.ds(2 * cw, ext)]
        for j in range(4):
            sel = (sel_c == (sel_r >> 2) * MAIN + 4 * j + (sel_r & 3)).astype(F32).astype(BF)
            dst[pl.ds(2 * n_blk, 4 * N_EXP), pl.ds(j * ext, ext)] = dot_nn(sel, extra).astype(BF)

    def ag_copy(c, side):
        return to_side(rows.at[0, c], rows.at[1 + side, c], ag_s.at[c, side], ag_r.at[c, side], side)

    def fw_copy(c, side):
        part = pl.ds(side * half, half)
        return to_side(rows.at[1 + side, c, part], rows.at[3, c, part], fw_s.at[c, side], fw_r.at[c, side], side)

    def add_hidden(b, c):
        hid[b] += dot_nt(rows[b, c], wd[c])

    for c in range(ZF):
        for side in range(2):
            raw_copy(c, side).wait_recv()
            raw_pass(c, side).start()

    def own_rows(c, carry):
        unpack(c, c, rows.at[0, c])
        ag_copy(c, 0).start()
        ag_copy(c, 1).start()
        return carry

    lax.fori_loop(ZF, 4, own_rows, 0)

    for copy in meta_copies:
        copy.wait_recv()
    for b in range(1, 4):
        weights = routing(b, meta_in[b - 1])
        for c in range(ZF):
            i = (b - 1) * ZF + c
            if b == 3:
                for side in range(2):
                    raw_pass(c, side).wait_recv()
            y_sent(i, i)
            pack_tokens(i, 8 + i, raw[b - 1, c], weights)
            y_start(i, 8 + i)

    hid[...] = jnp.zeros_like(hid)
    for copy in w_copies[:4]:
        copy.wait()

    def next_rows(c, carry):
        for side in range(2):
            ag_copy(c, side).wait_recv()
            fw_copy(c, side).start()
        add_hidden(0, c)
        add_hidden(1, c)
        add_hidden(2, c)
        return carry

    lax.fori_loop(ZF, 4, next_rows, 0)

    def own_stored(c, carry):
        unpack(4 + c, 4 + c, grads.at[c])
        return carry

    lax.fori_loop(0, 4, own_stored, 0)
    st_copies = [
        to_frame(grads.at[1], stored.at[0], st_s.at[0], st_r.at[0], right),
        to_frame(grads.at[3], stored.at[1], st_s.at[1], st_r.at[1], left),
        to_frame(grads.at[2], stored.at[2], st_s.at[2], st_r.at[2], opposite),
    ]
    for i in (2, 0, 1):
        st_copies[i].start()

    for c in range(ZF):
        unpack(c, c, rows.at[0, c])
        add_hidden(0, c)

    def far_rows(c, carry):
        for side in range(2):
            fw_copy(c, side).wait_recv()
        add_hidden(3, c)
        return carry

    lax.fori_loop(ZF, 4, far_rows, 0)

    for b in range(1, 4):
        for c in range(ZF):
            i = (b - 1) * ZF + c
            unpack(i, 8 + i, rows.at[b, c])
            add_hidden(b, c)

    def kv_near(i, side):
        src, dst = ((k_hbm, k_far), (v_hbm, v_far))[i]
        return to_side(src, dst.at[2 * side], kv_s.at[i, side], kv_r.at[i, side], side)

    def kv_pass(i):
        dst = (k_far, v_far)[i]
        return to_side(dst.at[2 * i], dst.at[1], kv_s.at[i, 2], kv_r.at[i, 2], i)

    @pl.when(fr <= 2)
    def _():
        kv_near(0, 0).start()

    @pl.when(fr == 0)
    def _():
        kv_near(0, 1).start()

    def hidden_to_grads(b, src):
        h = hid[b]
        g = src[:, pl.ds(0, ff)].astype(F32)
        u = src[:, pl.ds(ff, ff)].astype(F32)
        s = 1.0 / (1.0 + jnp.exp(-g))
        gate = (h * u * s * (1.0 + g * (1.0 - s))).astype(BF)
        up = (h * g * s).astype(BF)
        grads[b, :, pl.ds(0, ff)] = gate
        grads[b, :, pl.ds(ff, ff)] = up

    for i in (2, 0, 1):
        st_copies[i].wait()
    for b in (3, 2, 1, 0):
        hidden_to_grads(b, grads.at[0] if b == 0 else stored.at[b - 1])

    for copy in w_copies[4:]:
        copy.wait()

    def term(b, c):
        at = chunk_at(c)
        return dot_nt(grads[b, :, pl.ds(0, ff)], wg[at, :]) + dot_nt(grads[b, :, pl.ds(ff, ff)], wu[at, :])

    def ha_copy(c, side):
        return to_side(rows.at[3, c, pl.ds(side * half, half)], half_in.at[side, c - RF],
                       ha_s.at[c, side], ha_r.at[c, side], side)

    def fu_copy(c, side):
        return to_side(rows.at[2 - side, c], full_in.at[side, c - RF], fu_s.at[c, side], fu_r.at[c, side], side)

    def far_terms(c, carry):
        rows[3, c] = term(3, c).astype(BF)
        for side in range(2):
            ha_copy(c, side).start()
        return carry

    lax.fori_loop(RF, 4, far_terms, 0)

    def settle(i, carry):
        y_sent(lax.rem(i, 8), i)
        return carry

    lax.fori_loop(n_extra, 8 + n_extra, settle, 0)

    def z_copy(slot, d):
        return to_expert(
            ysend.at[slot, pl.ds(MAIN * d, MAIN)], zrecv.at[slot, pl.ds(MAIN * d, MAIN)],
            zs_sem.at[slot, d], zr_sem.at[slot, d], lax.rem(me + N_EXP - d, N_EXP))

    def send_back(slot, total):
        extra = jnp.zeros((n_blk, ext), F32)
        for j in range(4):
            sel = (selt_c == (selt_r >> 2) * MAIN + 4 * j + (selt_r & 3)).astype(F32).astype(BF)
            extra = extra + dot_nn(sel, total[2 * n_blk:, j * ext:(j + 1) * ext])
        extra = extra.astype(BF)
        for lo, w, part in ((0, cw, total[:n_blk]), (cw, cw, total[n_blk:2 * n_blk]), (2 * cw, ext, extra)):
            ysend[slot, :, pl.ds(lo, w)] = part
            zrecv[slot, pl.ds(0, MAIN), pl.ds(lo, w)] = part[:MAIN]
        for d in range(1, N_EXP):
            z_copy(slot, d).start()

    def tokens_of(slot, b):
        for d in range(1, N_EXP):
            z_copy(slot, d).wait_recv()
        got = dot_nn(atmat[b, :, pl.ds(0, n_blk)], zrecv[slot, :, pl.ds(0, cw)])
        got = got + dot_nn(atmat[b, :, pl.ds(n_blk, n_blk)], zrecv[slot, :, pl.ds(cw, cw)])
        extra = zrecv[slot, :, pl.ds(2 * cw, ext)]
        return got + jnp.concatenate([dot_nn(etmat[b, j], extra) for j in range(4)], axis=1)

    for c in range(RF):
        for b in (3, 2, 1, 0):
            send_back(4 + 4 * c + b, term(b, c).astype(BF))

    def near_terms(c, carry):
        for side in range(2):
            @pl.when(c >= ZF)
            def _():
                fw_copy(c, 1 - side).wait_send()
            part = term(2 - side, c)
            ha_copy(c, side).wait_recv()
            lo = side * half
            rows[2 - side, c, pl.ds(half - lo, half)] = part[half - lo:half - lo + half].astype(BF)
            rows[2 - side, c, pl.ds(lo, half)] = (
                part[lo:lo + half].astype(BF).astype(F32) + half_in[side, c - RF].astype(F32)).astype(BF)
            fu_copy(c, side).start()
        return carry

    lax.fori_loop(RF, 4, near_terms, 0)

    def put_moe(c, got):
        hid[c, pl.ds(0, toks), :] = got[:, :cw // 2]
        hid[c, pl.ds(toks, toks), :] = got[:, cw // 2:]

    def get_moe(c):
        return jnp.concatenate([hid[c, pl.ds(0, toks), :], hid[c, pl.ds(toks, toks), :]], axis=1)

    def dh_copy(c, side):
        part = pl.ds(side * thalf, thalf)
        return to_side(dense.at[c, 2, part], dhalf_in.at[side, c], dh_s.at[c, side], dh_r.at[c, side], side)

    def df_copy(c, side):
        return to_side(dense.at[c, 1 - side], dfull_in.at[side, c], df_s.at[c, side], df_r.at[c, side], side)

    for c in range(RF):
        dense[c, 2] = tokens_of(4 + 4 * c + 3, 3).astype(BF)
        for side in range(2):
            dh_copy(c, side).start()
        for side in range(2):
            b = 2 - side
            dense[c, b - 1] = tokens_of(4 + 4 * c + b, b).astype(BF)
        for side in range(2):
            b = 2 - side
            part = pl.ds(side * thalf, thalf)
            dh_copy(c, side).wait_recv()
            dense[c, b - 1, part] = (
                dense[c, b - 1, part].astype(F32) + dhalf_in[side, c].astype(F32)).astype(BF)
            df_copy(c, side).start()
        put_moe(c, tokens_of(4 + 4 * c, 0))

    @pl.when(fr >= 1)
    def _():
        kv_near(0, 0).wait_recv()

    @pl.when((fr == 1) | (fr == 2))
    def _():
        kv_pass(0).start()

    @pl.when(fr <= 2)
    def _():
        kv_near(1, 0).start()

    @pl.when(fr <= 1)
    def _():
        kv_near(1, 1).start()

    def own_terms(c, carry):
        part = term(0, c).astype(BF).astype(F32)
        for side in range(2):
            fu_copy(c, side).wait_recv()
        send_back(c, (part + full_in[0, c - RF].astype(F32) + full_in[1, c - RF].astype(F32)).astype(BF))
        return carry

    lax.fori_loop(RF, 4, own_terms, 0)

    @pl.when((fr == 3) | (fr == 0))
    def _():
        kv_near(1, 1).wait_recv()
        kv_pass(1).start()

    def square_sum(c, acc):
        x = hs_ref[:, chunk_at(c)].astype(F32)
        return acc + jnp.sum(x * x, axis=1, keepdims=True)

    inv = lax.rsqrt(lax.fori_loop(0, 4, square_sum, jnp.zeros((toks, 1), F32)) / width + 1e-6)

    def combine(c, acc):
        got = tokens_of(c, 0)
        put_moe(c, got)
        return acc + jnp.sum(got * hs_ref[:, chunk_at(c)].astype(F32), axis=1, keepdims=True)

    mean = lax.fori_loop(RF, 4, combine, jnp.zeros((toks, 1), F32))
    for c in range(RF):
        at = pl.ds(c * cw, cw)
        got = get_moe(c)
        for side in range(2):
            df_copy(c, side).wait_recv()
            got = got + dfull_in[side, c].astype(F32)
        put_moe(c, got)
        mean = mean + jnp.sum(got * hs_ref[:, at].astype(F32), axis=1, keepdims=True)
    mean = mean * inv / width

    def residual(c, carry):
        at = chunk_at(c)
        n = hs_ref[:, at].astype(F32) * inv
        resid_ref[:, at] = (og_ref[:, at].astype(F32) + inv * (get_moe(c) - n * mean)).astype(BF)
        return carry

    hw = gout_ref.shape[1]
    own_at = pl.ds(pl.multiple_of(me * toks, toks), toks)

    def go_copy(d):
        dest = lax.rem(me + d, N_EXP)
        return to_expert(
            resid_ref.at[:, pl.ds(pl.multiple_of(dest * hw, hw), hw)], gout_ref.at[own_at],
            go_s.at[d], go_r.at[d], dest)

    lax.fori_loop(0, 2, residual, 0)
    for d in range(1, N_EXP):
        go_copy(d).start()
    gout_ref[own_at, :] = resid_ref[:, pl.ds(pl.multiple_of(me * hw, hw), hw)]
    lax.fori_loop(2, 4, residual, 0)

    @pl.when(fr <= 2)
    def _():
        kv_near(0, 0).wait_send()
        kv_near(1, 0).wait_send()

    @pl.when(fr == 0)
    def _():
        kv_near(0, 1).wait_send()

    @pl.when(fr <= 1)
    def _():
        kv_near(1, 1).wait_send()

    @pl.when((fr == 1) | (fr == 2))
    def _():
        kv_pass(0).wait_send()

    @pl.when((fr == 3) | (fr == 0))
    def _():
        kv_pass(1).wait_send()

    @pl.when(fr >= 1)
    def _():
        kv_near(1, 0).wait_recv()

    @pl.when(fr == 3)
    def _():
        kv_near(0, 1).wait_recv()

    @pl.when(fr >= 2)
    def _():
        kv_pass(0).wait_recv()
        kv_pass(1).wait_recv()

    for copy in meta_copies:
        copy.wait_send()
    for c in range(ZF):
        for side in range(2):
            raw_copy(c, side).wait_send()
            raw_pass(c, side).wait_send()
    for c in range(RF):
        for side in range(2):
            dh_copy(c, side).wait_send()
            df_copy(c, side).wait_send()

    def drain(c, carry):
        for side in range(2):
            ag_copy(c, side).wait_send()
        return carry

    def drain_back(c, carry):
        for side in range(2):
            ha_copy(c, side).wait_send()
            fu_copy(c, side).wait_send()
        return carry

    def drain_z(slot, carry):
        for d in range(1, N_EXP):
            z_copy(slot, d).wait_send()
        return carry

    lax.fori_loop(ZF, 4, drain, 0)
    lax.fori_loop(RF, 4, drain_back, 0)
    lax.fori_loop(RF, 4 + 4 * RF, drain_z, 0)
    for c in range(ZF, RF):
        for side in range(2):
            fw_copy(c, side).wait_send()
    for d in range(1, N_EXP):
        go_copy(d).wait()


def moe_call(meta, out_grad, stored, hidden_state, wd, wg, wu, keys, values):
    toks, width = out_grad.shape
    ff = wd.shape[0]
    cw = width // 4
    n_rows = N_EXP * 36
    n_blk = N_EXP * MAIN
    pw = 2 * cw + cw // 4
    vm = pl.BlockSpec(memory_space=pltpu.VMEM)
    hbm = pl.BlockSpec(memory_space=pl.ANY)
    dma = pltpu.SemaphoreType.DMA
    slots = 8 + 3 * ZF
    back = 4 + 4 * RF
    rf = max(RF, 1)
    zf = max(ZF, 1)
    return pl.pallas_call(
        moe_kernel,
        out_shape=(
            jax.ShapeDtypeStruct((toks, width), BF),
            jax.ShapeDtypeStruct(keys.shape, BF),
            jax.ShapeDtypeStruct((3,) + keys.shape, BF),
            jax.ShapeDtypeStruct((3,) + keys.shape, BF),
        ),
        in_specs=[vm] * 4 + [hbm] * 5,
        out_specs=(vm, vm, hbm, hbm),
        scratch_shapes=[
            pltpu.VMEM((4, ff, cw), BF),
            pltpu.VMEM((width, ff), BF),
            pltpu.VMEM((width, ff), BF),
            pltpu.VMEM((4, 4, n_rows, cw), BF),
            pltpu.VMEM((3, n_rows, 2 * ff), BF),
            pltpu.VMEM((4, n_rows, ff), F32),
            pltpu.VMEM((4, n_rows, 2 * ff), BF),
            pltpu.VMEM((8, n_blk, pw), BF),
            pltpu.VMEM((slots, n_blk, pw), BF),
            pltpu.VMEM((back, n_blk, pw), BF),
            pltpu.VMEM((2, 4 - RF, n_rows // 2, cw), BF),
            pltpu.VMEM((2, 4 - RF, n_rows, cw), BF),
            pltpu.VMEM((2, rf, toks // 2, cw), BF),
            pltpu.VMEM((2, rf, toks, cw), BF),
            pltpu.VMEM((rf, 3, toks, cw), BF),
            pltpu.VMEM((2 * n_blk, 2 * toks), BF),
            pltpu.VMEM((4, n_blk, 2 * toks), BF),
            pltpu.VMEM((4, toks, 2 * n_blk), BF),
            pltpu.VMEM((4, 4, toks, n_blk), BF),
            pltpu.VMEM((3, zf, toks, cw), BF),
            pltpu.VMEM((3, 8, toks), F32),
            dma((6,)), dma((slots, 8)), dma((slots, 8)), dma((back, 8)), dma((back, 8)),
            dma((4, 2)), dma((4, 2)), dma((4, 2)), dma((4, 2)), dma((3,)), dma((3,)),
            dma((4, 2)), dma((4, 2)), dma((4, 2)), dma((4, 2)), dma((8,)), dma((8,)),
            dma((3,)), dma((3,)), dma((zf, 2)), dma((zf, 2)), dma((zf, 2)), dma((zf, 2)),
            dma((rf, 2)), dma((rf, 2)), dma((rf, 2)), dma((rf, 2)), dma((2, 3)), dma((2, 3)),
        ],
        compiler_params=pltpu.CompilerParams(
            collective_id=0, has_side_effects=True, vmem_limit_bytes=VMEM_LIMIT),
        cost_estimate=pl.CostEstimate(flops=15 * 10**9, bytes_accessed=20 * 10**6, transcendentals=0),
        name="moe",
    )(meta, out_grad, stored, hidden_state, wd, wg, wu, keys, values)


def attention_kernel(
    q_ref, go_ref, k_hbm, v_hbm, k_far, v_far, dq_ref, dk_ref, dv_ref,
    kv, probs, qt, mx, gs_t, g_rows, dqt, send, half_in, full_in,
    kv_sem, hs, hr, fs, fr_sem,
):
    fr = lax.axis_index("frame")
    left = lax.rem(fr + 3, 4)
    right = lax.rem(fr + 1, 4)
    span = q_ref.shape[0]
    scale = HD ** -0.5
    log2e = 1.4426950408889634

    def load(i, r):
        src = (k_hbm, v_hbm)[i] if isinstance(r, int) else (k_far, v_far)[i].at[r - 1]
        return pltpu.make_async_copy(src, kv.at[i, r], kv_sem.at[i, r])

    for i in range(2):
        load(i, 0).start()

    def load_far(r, carry):
        for i in range(2):
            load(i, r).start()
        return carry

    lax.fori_loop(1, fr + 1, load_far, 0)

    barrier = pltpu.get_barrier_semaphore()
    for dest in (left, right):
        pl.semaphore_signal(barrier, inc=1, device_id={"frame": dest}, device_id_type=MESH)
    pl.semaphore_wait(barrier, 2)

    def to_frame(src, dst, ss, rs, dest):
        return pltpu.make_async_remote_copy(
            src_ref=src, dst_ref=dst, send_sem=ss, recv_sem=rs,
            device_id={"frame": dest}, device_id_type=MESH)

    def half_copy(h):
        return to_frame(send.at[2, h], half_in.at[h], hs.at[h], hr.at[h], left if h == 0 else right)

    def full_copy(side, h):
        return to_frame(send.at[1 + 2 * side, h], full_in.at[side, h], fs.at[side, h], fr_sem.at[side, h],
                        left if side == 0 else right)

    def add_half(side, h):
        half_copy(h).wait_recv()
        for j in range(2):
            send[1 + 2 * side, h, j] = (
                send[1 + 2 * side, h, j].astype(F32) + half_in[h, j].astype(F32)).astype(BF)

    for i in range(2):
        load(i, 0).wait()

    def head(h, carry):
        cols = pl.ds(pl.multiple_of(h * HD, HD), HD)
        qt[...] = q_ref[:, cols].astype(F32).T.astype(BF)

        def forward(r, carry):
            @pl.when((r >= 1) & (h == 0))
            def _():
                for i in range(2):
                    load(i, r).wait()

            m, l, o = carry
            v_t = kv[1, r, :, cols].astype(F32).T.astype(BF)
            sc = dot_nn(kv[0, r, :, cols], qt[...])
            m_new = jnp.maximum(m, jnp.max(sc, axis=0, keepdims=True) * (scale * log2e))
            old = jnp.exp2(m - m_new)
            p = jnp.exp2(sc * (scale * log2e) - m_new)
            low = p.astype(BF)
            probs[r] = low
            mx[r] = m_new
            return m_new, l * old + jnp.sum(p, axis=0, keepdims=True), o * old + dot_nn(v_t, low)

        m, l, o = lax.fori_loop(0, fr + 1, forward, (
            jnp.full((1, span), -jnp.inf, F32), jnp.zeros((1, span), F32), jnp.zeros((HD, span), F32)))
        inv = 1.0 / l
        gs_t[...] = go_ref[:, cols].astype(F32).T * (inv * scale)
        centre = jnp.sum(gs_t[...] * (o * inv), axis=0, keepdims=True)
        dqt[...] = jnp.zeros_like(dqt)

        def backward(i, carry):
            r = jnp.where(i < 2, i + 2, 3 - i)

            @pl.when(r <= fr)
            def _():
                f = jnp.exp2(mx[r] - m)
                gt = (gs_t[...] * f).astype(BF)
                g_rows[...] = (gs_t[...] * (f * (1.0 / scale))).T.astype(BF)
                k_t = kv[0, r, :, cols].astype(F32).T.astype(BF)
                p = probs[r]
                dp = dot_nn(kv[1, r, :, cols], gt)
                ds = (p.astype(F32) * (dp - centre * f)).astype(BF)
                send[r, h, 0] = dot_nn(ds, q_ref[:, cols]).astype(BF)
                send[r, h, 1] = dot_nn(p, g_rows[...]).astype(BF)
                dqt[...] += dot_nn(k_t, ds)

            for h_at in range(2):
                @pl.when((i == 0) & (fr >= 2) & (h == h_at))
                def _():
                    half_copy(h_at).start()

            @pl.when((i == 1) & (fr == 3) & (h == 0))
            def _():
                full_copy(1, 0).start()

            @pl.when((i == 1) & (fr == 3) & (h == 1))
            def _():
                add_half(1, 1)
                full_copy(1, 1).start()

            @pl.when((i == 2) & (fr == 3) & (h == 0))
            def _():
                full_copy(0, 0).start()

            @pl.when((i == 2) & (fr >= 1) & (h == 1))
            def _():
                full_copy(0, 1).start()

            @pl.when((i == 2) & ((fr == 1) | (fr == 2)) & (h == 1))
            def _():
                add_half(0, 0)
                full_copy(0, 0).start()

            return carry

        lax.fori_loop(0, 4, backward, 0)
        dq_ref[:, cols] = dqt[...].T.astype(BF)
        return carry

    lax.fori_loop(0, 2, head, 0)

    @pl.when(fr == 0)
    def _():
        half_copy(1).wait_recv()
        send[3, 1] = half_in[1]
        full_copy(1, 1).start()

    def take(side, h):
        full_copy(side, h).wait_recv()
        for j in range(2):
            send[0, h, j] = (send[0, h, j].astype(F32) + full_in[side, h, j].astype(F32)).astype(BF)

    @pl.when(fr <= 2)
    def _():
        take(0, 1)
        take(0, 0)

    @pl.when(fr == 0)
    def _():
        take(1, 0)

    @pl.when(fr <= 1)
    def _():
        take(1, 1)

    for h in range(2):
        cols = pl.ds(h * HD, HD)
        dk_ref[:, cols] = send[0, h, 0]
        dv_ref[:, cols] = send[0, h, 1]

    for h in range(2):
        @pl.when(fr >= 2)
        def _():
            half_copy(h).wait_send()

        @pl.when(fr >= 1)
        def _():
            full_copy(0, h).wait_send()

    @pl.when(fr == 3)
    def _():
        full_copy(1, 0).wait_send()

    @pl.when((fr == 3) | (fr == 0))
    def _():
        full_copy(1, 1).wait_send()


def attention_call(q, go, k, v, k_far, v_far):
    span, width = q.shape
    vm = pl.BlockSpec(memory_space=pltpu.VMEM)
    hbm = pl.BlockSpec(memory_space=pl.ANY)
    dma = pltpu.SemaphoreType.DMA
    return pl.pallas_call(
        attention_kernel,
        out_shape=(jax.ShapeDtypeStruct(q.shape, BF),) * 3,
        in_specs=[vm] * 2 + [hbm] * 4,
        out_specs=(vm,) * 3,
        scratch_shapes=[
            pltpu.VMEM((2, 4, span, width), BF),
            pltpu.VMEM((4, span, span), BF),
            pltpu.VMEM((HD, span), BF),
            pltpu.VMEM((4, 1, span), F32),
            pltpu.VMEM((HD, span), F32),
            pltpu.VMEM((span, HD), BF),
            pltpu.VMEM((HD, span), F32),
            pltpu.VMEM((4, 2, 2, span, HD), BF),
            pltpu.VMEM((2, 2, span, HD), BF),
            pltpu.VMEM((2, 2, 2, span, HD), BF),
            dma((2, 4)), dma((2,)), dma((2,)), dma((2, 2)), dma((2, 2)),
        ],
        compiler_params=pltpu.CompilerParams(
            collective_id=1, has_side_effects=True, vmem_limit_bytes=VMEM_LIMIT),
        cost_estimate=pl.CostEstimate(flops=10 * 10**9, bytes_accessed=20 * 10**6, transcendentals=0),
        name="attention",
    )(q, go, k, v, k_far, v_far)


def on_device(
    queries, keys, values, hidden_state, out_grad, stored_pre, expert_ids, gate_weights,
    w_gate, w_up, w_down,
):
    toks = out_grad.shape[0]
    meta = jnp.concatenate(
        [expert_ids.astype(F32).T, gate_weights.T, jnp.zeros((4, toks), F32)], axis=0)
    resid, go, k_far, v_far = moe_call(
        meta, out_grad, stored_pre.reshape(toks, -1), hidden_state,
        w_down[0], w_gate[0], w_up[0], keys, values)
    dq, dk, dv = attention_call(queries, go, keys, values, k_far, v_far)
    return resid, dq, dk, dv


def solution(mesh):
    rows = P(("dp", "frame"), "expert")
    toks = ("dp", "frame", "expert")
    return jax.shard_map(
        on_device,
        mesh=mesh,
        in_specs=(
            rows, rows, rows, P(toks, None), P(toks, None), P(toks, None, None, None),
            P(toks, None), P(toks, None), P("expert", None, "frame"), P("expert", None, "frame"),
            P("expert", "frame", None),
        ),
        out_specs=(P(toks, None), rows, rows, rows),
        check_vma=False,
    )
```

```python
import functools

import jax
import jax.numpy as jnp
from jax import lax
from jax.experimental import pallas as pl
from jax.experimental.pallas import tpu as pltpu
from jax.sharding import PartitionSpec as P

HD = 128
N_EXP = 8
N_FRAME = 4
MAIN = 16
BF = jnp.bfloat16
F32 = jnp.float32
MESH = pl.DeviceIdType.MESH
VMEM_LIMIT = 63 * 1024 * 1024


def dot_nn(a, b):
    return lax.dot_general(a, b, (((1,), (0,)), ((), ())), preferred_element_type=F32)


def dot_nt(a, b):
    return lax.dot_general(a, b, (((1,), (1,)), ((), ())), preferred_element_type=F32)


ZF = 2
RF = 1


def moe_kernel(
    meta_ref, og_ref, st_ref, hs_ref, wd_hbm, wg_hbm, wu_hbm, k_hbm, v_hbm,
    resid_ref, gout_ref, k_far, v_far,
    wd, wg, wu, rows, stored, hid, grads, ysend, yrecv, zrecv,
    half_in, full_in, dhalf_in, dfull_in, dense, amat, emat, atmat, etmat, raw, meta_in,
    w_sem, ys_sem, yr_sem, zs_sem, zr_sem, ag_s, ag_r, fw_s, fw_r, st_s, st_r,
    ha_s, ha_r, fu_s, fu_r, go_s, go_r, me_s, me_r, ra_s, ra_r, rf_s, rf_r,
    dh_s, dh_r, df_s, df_r, kv_s, kv_r,
):
    me = lax.axis_index("expert")
    fr = lax.axis_index("frame")
    left = lax.rem(fr + 3, 4)
    right = lax.rem(fr + 1, 4)
    opposite = lax.rem(fr + 2, 4)
    toks, width = og_ref.shape
    cw = width // 4
    ext = cw // 4
    ff = hid.shape[2]
    n_rows = rows.shape[2]
    half = n_rows // 2
    thalf = toks // 2
    n_blk = N_EXP * MAIN
    n_extra = 3 * ZF

    def chunk_at(c):
        return pl.ds(pl.multiple_of(c * cw, cw), cw)

    def to_frame(src, dst, ss, rs, dest):
        return pltpu.make_async_remote_copy(
            src_ref=src, dst_ref=dst, send_sem=ss, recv_sem=rs,
            device_id={"frame": dest}, device_id_type=MESH)

    def to_side(src, dst, ss, rs, side):
        return to_frame(src, dst, ss, rs, right if side == 0 else left)

    def to_expert(src, dst, ss, rs, dest):
        return pltpu.make_async_remote_copy(
            src_ref=src, dst_ref=dst, send_sem=ss, recv_sem=rs,
            device_id={"expert": dest}, device_id_type=MESH)

    barrier = pltpu.get_barrier_semaphore()
    for d in range(1, N_EXP):
        pl.semaphore_signal(barrier, inc=1, device_id={"expert": lax.rem(me + d, N_EXP)}, device_id_type=MESH)
    for dest in (left, right, opposite):
        pl.semaphore_signal(barrier, inc=1, device_id={"frame": dest}, device_id_type=MESH)

    w_copies = [pltpu.make_async_copy(wd_hbm.at[:, pl.ds(c * cw, cw)], wd.at[c], w_sem.at[c]) for c in range(4)]
    w_copies += [pltpu.make_async_copy(wg_hbm, wg, w_sem.at[4]), pltpu.make_async_copy(wu_hbm, wu, w_sem.at[5])]
    for copy in w_copies:
        copy.start()

    def raw_copy(c, side):
        return to_side(og_ref.at[:, chunk_at(c)], raw.at[side, c], ra_s.at[c, side], ra_r.at[c, side], side)

    def raw_pass(c, side):
        part = pl.ds(side * thalf, thalf)
        return to_side(raw.at[side, c, part], raw.at[2, c, part], rf_s.at[c, side], rf_r.at[c, side], side)

    meta_copies = [
        to_frame(meta_ref, meta_in.at[0], me_s.at[0], me_r.at[0], right),
        to_frame(meta_ref, meta_in.at[1], me_s.at[1], me_r.at[1], left),
        to_frame(meta_ref, meta_in.at[2], me_s.at[2], me_r.at[2], opposite),
    ]
    pl.semaphore_wait(barrier, N_EXP + 2)
    for copy in meta_copies:
        copy.start()
    for c in range(ZF):
        for side in range(2):
            raw_copy(c, side).start()

    earlier_mask = (
        lax.broadcasted_iota(jnp.int32, (toks, toks), 0) < lax.broadcasted_iota(jnp.int32, (toks, toks), 1)
    ).astype(F32).astype(BF)
    expert_iota = lax.broadcasted_iota(jnp.int32, (N_EXP, toks), 0)
    main_iota = lax.broadcasted_iota(jnp.int32, (2 * n_blk, toks), 0)
    ext_iota = lax.broadcasted_iota(jnp.int32, (n_blk, toks), 0)

    def routing(b, meta):
        base = jnp.zeros((N_EXP, 1), F32)
        main_sum = jnp.zeros(main_iota.shape, F32)
        ext_sum = [jnp.zeros(ext_iota.shape, F32) for _ in range(4)]
        for k in range(2):
            rel = (meta[k:k + 1, :].astype(jnp.int32) - me + N_EXP) & (N_EXP - 1)
            hit = (expert_iota == rel).astype(F32)
            earlier = dot_nn(hit.astype(BF), earlier_mask) + base
            slot = jnp.sum(hit * earlier, axis=0, keepdims=True).astype(jnp.int32)
            base = base + jnp.sum(hit, axis=1, keepdims=True)
            main_at = jnp.where(slot < 32, (slot >> 4) * n_blk + rel * MAIN + (slot & 15), -1)
            ext_at = jnp.where(slot < 32, -1000, rel * MAIN + slot - 32)
            main_k = (main_iota == main_at).astype(F32)
            amat[:, pl.ds(k * toks, toks)] = main_k.astype(BF)
            main_sum = main_sum + main_k
            for j in range(4):
                ext_k = (ext_iota == ext_at + 4 * j).astype(F32)
                emat[j, :, pl.ds(k * toks, toks)] = ext_k.astype(BF)
                ext_sum[j] = ext_sum[j] + ext_k
        atmat[b] = main_sum.T.astype(BF)
        for j in range(4):
            etmat[b, j] = ext_sum[j].T.astype(BF)
        return meta.T

    def pack_pairs(slot, at, pairs):
        main = dot_nn(amat[...], pairs).astype(BF)
        extra = dot_nn(emat[0], pairs[:, :ext])
        for j in range(1, 4):
            extra = extra + dot_nn(emat[j], pairs[:, j * ext:(j + 1) * ext])
        extra = extra.astype(BF)
        for lo, w, part in ((0, cw, main[:n_blk]), (cw, cw, main[n_blk:]), (2 * cw, ext, extra)):
            ysend[slot, :, pl.ds(lo, w)] = part
            yrecv[at, pl.ds(0, MAIN), pl.ds(lo, w)] = part[:MAIN]

    def pack_tokens(slot, at, x, weights):
        x = x.astype(F32)
        pack_pairs(slot, at, jnp.concatenate(
            [(weights[:, 2:3] * x).astype(BF), (weights[:, 3:4] * x).astype(BF)], axis=0))

    def y_copy(slot, at, d):
        return to_expert(
            ysend.at[slot, pl.ds(MAIN * d, MAIN)], yrecv.at[at, pl.ds(MAIN * d, MAIN)],
            ys_sem.at[at, d], yr_sem.at[at, d], lax.rem(me + d, N_EXP))

    def y_start(slot, at):
        for d in range(1, N_EXP):
            y_copy(slot, at, d).start()

    def y_sent(slot, at):
        for d in range(1, N_EXP):
            y_copy(slot, at, d).wait_send()

    own_weights = routing(0, meta_ref[...])

    def build_rows(i, carry):
        c = lax.rem(i + ZF, 4)
        pack_tokens(c, c, og_ref[:, chunk_at(c)], own_weights)
        y_start(c, c)
        return carry

    def build_stored(c, carry):
        f = lax.rem(fr + c, 4)
        parts = []
        for k in range(2):
            parts.append(jnp.concatenate(
                [st_ref[:, pl.ds(pl.multiple_of((k * 2 + kind) * 4 * ff + f * ff, ff), ff)] for kind in range(2)], axis=1))
        pack_pairs(4 + c, 4 + c, jnp.concatenate(parts, axis=0))
        y_start(4 + c, 4 + c)
        return carry

    lax.fori_loop(0, 4 - ZF, build_rows, 0)
    lax.fori_loop(0, 4, build_stored, 0)
    lax.fori_loop(4 - ZF, 4, build_rows, 0)

    sel_r = lax.broadcasted_iota(jnp.int32, (4 * N_EXP, n_blk), 0)
    sel_c = lax.broadcasted_iota(jnp.int32, (4 * N_EXP, n_blk), 1)
    selt_r = lax.broadcasted_iota(jnp.int32, (n_blk, 4 * N_EXP), 1)
    selt_c = lax.broadcasted_iota(jnp.int32, (n_blk, 4 * N_EXP), 0)

    def unpack(slot, at, dst):
        for d in range(1, N_EXP):
            y_copy(slot, at, d).wait_recv()
        dst[pl.ds(0, n_blk), :] = yrecv[at, :, pl.ds(0, cw)]
        dst[pl.ds(n_blk, n_blk), :] = yrecv[at, :, pl.ds(cw, cw)]
        extra = yrecv[at, :, pl.ds(2 * cw, ext)]
        for j in range(4):
            sel = (sel_c == (sel_r >> 2) * MAIN + 4 * j + (sel_r & 3)).astype(F32).astype(BF)
            dst[pl.ds(2 * n_blk, 4 * N_EXP), pl.ds(j * ext, ext)] = dot_nn(sel, extra).astype(BF)

    def ag_copy(c, side):
        return to_side(rows.at[0, c], rows.at[1 + side, c], ag_s.at[c, side], ag_r.at[c, side], side)

    def fw_copy(c, side):
        part = pl.ds(side * half, half)
        return to_side(rows.at[1 + side, c, part], rows.at[3, c, part], fw_s.at[c, side], fw_r.at[c, side], side)

    def add_hidden(b, c):
        hid[b] += dot_nt(rows[b, c], wd[c])

    for c in range(ZF):
        for side in range(2):
            raw_copy(c, side).wait_recv()
            raw_pass(c, side).start()

    def own_rows(c, carry):
        unpack(c, c, rows.at[0, c])
        ag_copy(c, 0).start()
        ag_copy(c, 1).start()
        return carry

    lax.fori_loop(ZF, 4, own_rows, 0)

    def extra_block(n):
        return lax.rem(n + 2, 3) + 1

    def extra_slot(i):
        return 2 + lax.rem(i, 6)

    for copy in meta_copies:
        copy.wait_recv()

    def dispatch(n, carry):
        b = extra_block(n)
        weights = routing(b, meta_in[b - 1])

        def one(c, carry):
            i = n * ZF + c

            @pl.when(n == 0)
            def _():
                for side in range(2):
                    raw_pass(c, side).wait_recv()

            slot = extra_slot(i)
            y_sent(slot, jnp.where(i < 6, slot, i + 2))
            pack_tokens(slot, 8 + i, raw[b - 1, c], weights)
            y_start(slot, 8 + i)
            return carry

        return lax.fori_loop(0, ZF, one, carry)

    lax.fori_loop(0, 1, dispatch, 0)

    hid[...] = jnp.zeros_like(hid)
    for copy in w_copies[:4]:
        copy.wait()

    def next_rows(c, carry):
        for side in range(2):
            ag_copy(c, side).wait_recv()
            fw_copy(c, side).start()

        def near(b, carry):
            add_hidden(b, c)
            return carry

        return lax.fori_loop(0, 3, near, carry)

    lax.fori_loop(ZF, 4, next_rows, 0)

    def own_stored(c, carry):
        unpack(4 + c, 4 + c, grads.at[c])
        return carry

    lax.fori_loop(0, 4, own_stored, 0)
    st_copies = [
        to_frame(grads.at[1], stored.at[0], st_s.at[0], st_r.at[0], right),
        to_frame(grads.at[3], stored.at[1], st_s.at[1], st_r.at[1], left),
        to_frame(grads.at[2], stored.at[2], st_s.at[2], st_r.at[2], opposite),
    ]
    for i in (2, 0, 1):
        st_copies[i].start()

    lax.fori_loop(1, 3, dispatch, 0)

    def far_rows(c, carry):
        for side in range(2):
            fw_copy(c, side).wait_recv()
        add_hidden(3, c)
        return carry

    lax.fori_loop(ZF, 4, far_rows, 0)

    def dispatched(i, carry):
        b = extra_block(i // ZF)
        c = lax.rem(i, ZF)
        unpack(extra_slot(i), 8 + i, rows.at[b, c])
        add_hidden(b, c)
        return carry

    lax.fori_loop(0, ZF, dispatched, 0)

    def kv_near(i, side):
        src, dst = ((k_hbm, k_far), (v_hbm, v_far))[i]
        return to_side(src, dst.at[2 * side], kv_s.at[i, side], kv_r.at[i, side], side)

    def kv_pass(i):
        dst = (k_far, v_far)[i]
        return to_side(dst.at[2 * i], dst.at[1], kv_s.at[i, 2], kv_r.at[i, 2], i)

    def hidden_to_grads(b, src):
        def some_rows(i, carry):
            at = pl.ds(pl.multiple_of(i * 32, 32), 32)
            h = hid[b, at, :]
            g = src[at, pl.ds(0, ff)].astype(F32)
            u = src[at, pl.ds(ff, ff)].astype(F32)
            s = 1.0 / (1.0 + jnp.exp(-g))
            gate = (h * u * s * (1.0 + g * (1.0 - s))).astype(BF)
            up = (h * g * s).astype(BF)
            grads[b, at, pl.ds(0, ff)] = gate
            grads[b, at, pl.ds(ff, ff)] = up
            return carry

        lax.fori_loop(0, n_rows // 32, some_rows, 0)

    st_copies[2].wait()
    st_copies[1].wait_send()
    hidden_to_grads(3, stored.at[2])
    for copy in w_copies[4:]:
        copy.wait()

    def term(b, c):
        at = chunk_at(c)
        return dot_nt(grads[b, :, pl.ds(0, ff)], wg[at, :]) + dot_nt(grads[b, :, pl.ds(ff, ff)], wu[at, :])

    def ha_copy(c, side):
        return to_side(rows.at[3, c, pl.ds(side * half, half)], half_in.at[side, c - RF],
                       ha_s.at[c, side], ha_r.at[c, side], side)

    def fu_copy(c, side):
        return to_side(rows.at[2 - side, c], full_in.at[side, c - RF], fu_s.at[c, side], fu_r.at[c, side], side)

    def z_copy(slot, d):
        return to_expert(
            ysend.at[slot, pl.ds(MAIN * d, MAIN)], zrecv.at[slot, pl.ds(MAIN * d, MAIN)],
            zs_sem.at[slot, d], zr_sem.at[slot, d], lax.rem(me + N_EXP - d, N_EXP))

    def send_back(slot, total):
        extra = jnp.zeros((n_blk, ext), F32)
        for j in range(4):
            sel = (selt_c == (selt_r >> 2) * MAIN + 4 * j + (selt_r & 3)).astype(F32).astype(BF)
            extra = extra + dot_nn(sel, total[2 * n_blk:, j * ext:(j + 1) * ext])
        extra = extra.astype(BF)
        for lo, w, part in ((0, cw, total[:n_blk]), (cw, cw, total[n_blk:2 * n_blk]), (2 * cw, ext, extra)):
            ysend[slot, :, pl.ds(lo, w)] = part
            zrecv[slot, pl.ds(0, MAIN), pl.ds(lo, w)] = part[:MAIN]
        for d in range(1, N_EXP):
            z_copy(slot, d).start()

    def far_terms(c, carry):
        rows[3, c] = term(3, c).astype(BF)
        for side in range(2):
            ha_copy(c, side).start()
        return carry

    lax.fori_loop(RF, 4, far_terms, 0)
    y_sent(0, 0)
    send_back(0, term(3, 0).astype(BF))

    @pl.when(fr <= 2)
    def _():
        kv_near(0, 0).start()

    @pl.when(fr == 0)
    def _():
        kv_near(0, 1).start()

    def own_dispatched(c, carry):
        unpack(c, c, rows.at[0, c])
        add_hidden(0, c)
        return carry

    lax.fori_loop(0, ZF, own_dispatched, 0)
    lax.fori_loop(ZF, n_extra, dispatched, 0)
    st_copies[0].wait()
    st_copies[1].wait_recv()

    def near_grads(i, carry):
        hidden_to_grads(2 - i, stored.at[1 - i])
        return carry

    lax.fori_loop(0, 2, near_grads, 0)
    hidden_to_grads(0, grads.at[0])

    def settle(i, carry):
        y_sent(i, i)
        return carry

    def settle_extra(i, carry):
        y_sent(extra_slot(i), 8 + i)
        return carry

    lax.fori_loop(1, 2, settle, 0)
    lax.fori_loop(2 + min(n_extra, 6), 8, settle, 0)
    lax.fori_loop(max(n_extra - 6, 0), n_extra, settle_extra, 0)

    def tokens_of(slot, b):
        for d in range(1, N_EXP):
            z_copy(slot, d).wait_recv()
        got = dot_nn(atmat[b, :, pl.ds(0, n_blk)], zrecv[slot, :, pl.ds(0, cw)])
        got = got + dot_nn(atmat[b, :, pl.ds(n_blk, n_blk)], zrecv[slot, :, pl.ds(cw, cw)])
        extra = zrecv[slot, :, pl.ds(2 * cw, ext)]
        return got + jnp.concatenate([dot_nn(etmat[b, j], extra) for j in range(4)], axis=1)

    def near_terms(i, carry):
        c = RF + i // 2
        side = lax.rem(i, 2)

        def block(side):
            @pl.when(c >= ZF)
            def _():
                fw_copy(c, 1 - side).wait_send()

        for side_at in range(2):
            @pl.when(side == side_at)
            def _():
                block(side_at)

        rows[2 - side, c] = term(2 - side, c).astype(BF)
        for side_at in range(2):
            @pl.when(side == side_at)
            def _():
                part = pl.ds(side_at * half, half)
                ha_copy(c, side_at).wait_recv()
                rows[2 - side_at, c, part] = (
                    rows[2 - side_at, c, part].astype(F32) + half_in[side_at, c - RF].astype(F32)).astype(BF)
                fu_copy(c, side_at).start()
        return carry

    def near_and_back(j, carry):
        lax.fori_loop(2 * j, 2 * j + 2, near_terms, 0)
        send_back(6 - j, term(2 - j, 0).astype(BF))
        return carry

    lax.fori_loop(0, 3, near_and_back, 0)

    def put_moe(c, got):
        hid[c, pl.ds(0, toks), :] = got[:, :cw // 2]
        hid[c, pl.ds(toks, toks), :] = got[:, cw // 2:]

    def get_moe(c):
        return jnp.concatenate([hid[c, pl.ds(0, toks), :], hid[c, pl.ds(toks, toks), :]], axis=1)

    def dh_copy(c, side):
        part = pl.ds(side * thalf, thalf)
        return to_side(dense.at[c, 2, part], dhalf_in.at[side, c], dh_s.at[c, side], dh_r.at[c, side], side)

    def df_copy(c, side):
        return to_side(dense.at[c, 1 - side], dfull_in.at[side, c], df_s.at[c, side], df_r.at[c, side], side)

    for c in range(RF):
        dense[c, 2] = tokens_of(0, 3).astype(BF)
        for side in range(2):
            dh_copy(c, side).start()
        for side in range(2):
            b = 2 - side
            dense[c, b - 1] = tokens_of(4 + 4 * c + b, b).astype(BF)
        for side in range(2):
            b = 2 - side
            part = pl.ds(side * thalf, thalf)
            dh_copy(c, side).wait_recv()
            dense[c, b - 1, part] = (
                dense[c, b - 1, part].astype(F32) + dhalf_in[side, c].astype(F32)).astype(BF)
            df_copy(c, side).start()
        put_moe(c, tokens_of(4 + 4 * c, 0))

    @pl.when(fr >= 1)
    def _():
        kv_near(0, 0).wait_recv()

    @pl.when((fr == 1) | (fr == 2))
    def _():
        kv_pass(0).start()

    @pl.when(fr <= 2)
    def _():
        kv_near(1, 0).start()

    @pl.when(fr <= 1)
    def _():
        kv_near(1, 1).start()

    def own_terms(c, carry):
        part = term(0, c).astype(BF).astype(F32)
        for side in range(2):
            fu_copy(c, side).wait_recv()
        send_back(c, (part + full_in[0, c - RF].astype(F32) + full_in[1, c - RF].astype(F32)).astype(BF))
        return carry

    lax.fori_loop(RF, 4, own_terms, 0)

    @pl.when((fr == 3) | (fr == 0))
    def _():
        kv_near(1, 1).wait_recv()
        kv_pass(1).start()

    def square_sum(c, acc):
        x = hs_ref[:, chunk_at(c)].astype(F32)
        return acc + jnp.sum(x * x, axis=1, keepdims=True)

    inv = lax.rsqrt(lax.fori_loop(0, 4, square_sum, jnp.zeros((toks, 1), F32)) / width + 1e-6)

    def combine(c, acc):
        got = tokens_of(c, 0)
        put_moe(c, got)
        return acc + jnp.sum(got * hs_ref[:, chunk_at(c)].astype(F32), axis=1, keepdims=True)

    mean = lax.fori_loop(RF, 4, combine, jnp.zeros((toks, 1), F32))
    for c in range(RF):
        at = pl.ds(c * cw, cw)
        got = get_moe(c)
        for side in range(2):
            df_copy(c, side).wait_recv()
            got = got + dfull_in[side, c].astype(F32)
        put_moe(c, got)
        mean = mean + jnp.sum(got * hs_ref[:, at].astype(F32), axis=1, keepdims=True)
    mean = mean * inv / width

    def residual(c, carry):
        at = chunk_at(c)
        n = hs_ref[:, at].astype(F32) * inv
        resid_ref[:, at] = (og_ref[:, at].astype(F32) + inv * (get_moe(c) - n * mean)).astype(BF)
        return carry

    hw = gout_ref.shape[1]
    own_at = pl.ds(pl.multiple_of(me * toks, toks), toks)

    def go_copy(d):
        dest = lax.rem(me + d, N_EXP)
        return to_expert(
            resid_ref.at[:, pl.ds(pl.multiple_of(dest * hw, hw), hw)], gout_ref.at[own_at],
            go_s.at[d], go_r.at[d], dest)

    lax.fori_loop(0, 2, residual, 0)
    for d in range(1, N_EXP):
        go_copy(d).start()
    gout_ref[own_at, :] = resid_ref[:, pl.ds(pl.multiple_of(me * hw, hw), hw)]
    lax.fori_loop(2, 4, residual, 0)

    @pl.when(fr <= 2)
    def _():
        kv_near(0, 0).wait_send()
        kv_near(1, 0).wait_send()

    @pl.when(fr == 0)
    def _():
        kv_near(0, 1).wait_send()

    @pl.when(fr <= 1)
    def _():
        kv_near(1, 1).wait_send()

    @pl.when((fr == 1) | (fr == 2))
    def _():
        kv_pass(0).wait_send()

    @pl.when((fr == 3) | (fr == 0))
    def _():
        kv_pass(1).wait_send()

    @pl.when(fr >= 1)
    def _():
        kv_near(1, 0).wait_recv()

    @pl.when(fr == 3)
    def _():
        kv_near(0, 1).wait_recv()

    @pl.when(fr >= 2)
    def _():
        kv_pass(0).wait_recv()
        kv_pass(1).wait_recv()

    for copy in meta_copies:
        copy.wait_send()
    for c in range(ZF):
        for side in range(2):
            raw_copy(c, side).wait_send()
            raw_pass(c, side).wait_send()
    for c in range(RF):
        for side in range(2):
            dh_copy(c, side).wait_send()
            df_copy(c, side).wait_send()

    def drain(c, carry):
        for side in range(2):
            ag_copy(c, side).wait_send()
        return carry

    def drain_back(c, carry):
        for side in range(2):
            ha_copy(c, side).wait_send()
            fu_copy(c, side).wait_send()
        return carry

    def drain_z(slot, carry):
        for d in range(1, N_EXP):
            z_copy(slot, d).wait_send()
        return carry

    lax.fori_loop(ZF, 4, drain, 0)
    lax.fori_loop(RF, 4, drain_back, 0)
    lax.fori_loop(0, 7, drain_z, 0)
    for c in range(ZF, RF):
        for side in range(2):
            fw_copy(c, side).wait_send()
    for d in range(1, N_EXP):
        go_copy(d).wait()


def moe_call(meta, out_grad, stored, hidden_state, wd, wg, wu, keys, values):
    toks, width = out_grad.shape
    ff = wd.shape[0]
    cw = width // 4
    n_rows = N_EXP * 36
    n_blk = N_EXP * MAIN
    pw = 2 * cw + cw // 4
    vm = pl.BlockSpec(memory_space=pltpu.VMEM)
    hbm = pl.BlockSpec(memory_space=pl.ANY)
    dma = pltpu.SemaphoreType.DMA
    slots = 8 + 3 * ZF
    back = 7
    rf = max(RF, 1)
    zf = max(ZF, 1)
    return pl.pallas_call(
        moe_kernel,
        out_shape=(
            jax.ShapeDtypeStruct((toks, width), BF),
            jax.ShapeDtypeStruct(keys.shape, BF),
            jax.ShapeDtypeStruct((3,) + keys.shape, BF),
            jax.ShapeDtypeStruct((3,) + keys.shape, BF),
        ),
        in_specs=[vm] * 4 + [hbm] * 5,
        out_specs=(vm, vm, hbm, hbm),
        scratch_shapes=[
            pltpu.VMEM((4, ff, cw), BF),
            pltpu.VMEM((width, ff), BF),
            pltpu.VMEM((width, ff), BF),
            pltpu.VMEM((4, 4, n_rows, cw), BF),
            pltpu.VMEM((3, n_rows, 2 * ff), BF),
            pltpu.VMEM((4, n_rows, ff), F32),
            pltpu.VMEM((4, n_rows, 2 * ff), BF),
            pltpu.VMEM((8, n_blk, pw), BF),
            pltpu.VMEM((slots, n_blk, pw), BF),
            pltpu.VMEM((back, n_blk, pw), BF),
            pltpu.VMEM((2, 4 - RF, n_rows // 2, cw), BF),
            pltpu.VMEM((2, 4 - RF, n_rows, cw), BF),
            pltpu.VMEM((2, rf, toks // 2, cw), BF),
            pltpu.VMEM((2, rf, toks, cw), BF),
            pltpu.VMEM((rf, 3, toks, cw), BF),
            pltpu.VMEM((2 * n_blk, 2 * toks), BF),
            pltpu.VMEM((4, n_blk, 2 * toks), BF),
            pltpu.VMEM((4, toks, 2 * n_blk), BF),
            pltpu.VMEM((4, 4, toks, n_blk), BF),
            pltpu.VMEM((3, zf, toks, cw), BF),
            pltpu.VMEM((3, 8, toks), F32),
            dma((6,)), dma((slots, 8)), dma((slots, 8)), dma((back, 8)), dma((back, 8)),
            dma((4, 2)), dma((4, 2)), dma((4, 2)), dma((4, 2)), dma((3,)), dma((3,)),
            dma((4, 2)), dma((4, 2)), dma((4, 2)), dma((4, 2)), dma((8,)), dma((8,)),
            dma((3,)), dma((3,)), dma((zf, 2)), dma((zf, 2)), dma((zf, 2)), dma((zf, 2)),
            dma((rf, 2)), dma((rf, 2)), dma((rf, 2)), dma((rf, 2)), dma((2, 3)), dma((2, 3)),
        ],
        compiler_params=pltpu.CompilerParams(
            collective_id=0, has_side_effects=True, vmem_limit_bytes=VMEM_LIMIT),
        cost_estimate=pl.CostEstimate(flops=15 * 10**9, bytes_accessed=20 * 10**6, transcendentals=0),
        name="moe",
    )(meta, out_grad, stored, hidden_state, wd, wg, wu, keys, values)


def attention_kernel(
    q_ref, go_ref, k_hbm, v_hbm, k_far, v_far, dq_ref, dk_ref, dv_ref,
    kv, probs, qt, mx, gs_t, g_rows, dqt, send, half_in, full_in,
    kv_sem, hs, hr, fs, fr_sem,
):
    fr = lax.axis_index("frame")
    left = lax.rem(fr + 3, 4)
    right = lax.rem(fr + 1, 4)
    span = q_ref.shape[0]
    scale = HD ** -0.5
    log2e = 1.4426950408889634

    def load(i, r):
        src = (k_hbm, v_hbm)[i] if isinstance(r, int) else (k_far, v_far)[i].at[r - 1]
        return pltpu.make_async_copy(src, kv.at[i, r], kv_sem.at[i, r])

    for i in range(2):
        load(i, 0).start()

    def load_far(r, carry):
        for i in range(2):
            load(i, r).start()
        return carry

    lax.fori_loop(1, fr + 1, load_far, 0)

    barrier = pltpu.get_barrier_semaphore()
    for dest in (left, right):
        pl.semaphore_signal(barrier, inc=1, device_id={"frame": dest}, device_id_type=MESH)
    pl.semaphore_wait(barrier, 2)

    def to_frame(src, dst, ss, rs, dest):
        return pltpu.make_async_remote_copy(
            src_ref=src, dst_ref=dst, send_sem=ss, recv_sem=rs,
            device_id={"frame": dest}, device_id_type=MESH)

    def half_copy(h):
        return to_frame(send.at[2, h], half_in.at[h], hs.at[h], hr.at[h], left if h == 0 else right)

    def full_copy(side, h):
        return to_frame(send.at[1 + 2 * side, h], full_in.at[side, h], fs.at[side, h], fr_sem.at[side, h],
                        left if side == 0 else right)

    def add_half(side, h):
        half_copy(h).wait_recv()
        for j in range(2):
            send[1 + 2 * side, h, j] = (
                send[1 + 2 * side, h, j].astype(F32) + half_in[h, j].astype(F32)).astype(BF)

    for i in range(2):
        load(i, 0).wait()

    def head(h, carry):
        cols = pl.ds(pl.multiple_of(h * HD, HD), HD)
        qt[...] = q_ref[:, cols].astype(F32).T.astype(BF)

        def forward(r, carry):
            @pl.when((r >= 1) & (h == 0))
            def _():
                for i in range(2):
                    load(i, r).wait()

            m, l, o = carry
            v_t = kv[1, r, :, cols].astype(F32).T.astype(BF)
            sc = dot_nn(kv[0, r, :, cols], qt[...])
            m_new = jnp.maximum(m, jnp.max(sc, axis=0, keepdims=True) * (scale * log2e))
            old = jnp.exp2(m - m_new)
            p = jnp.exp2(sc * (scale * log2e) - m_new)
            low = p.astype(BF)
            probs[r] = low
            mx[r] = m_new
            return m_new, l * old + jnp.sum(p, axis=0, keepdims=True), o * old + dot_nn(v_t, low)

        m, l, o = lax.fori_loop(0, fr + 1, forward, (
            jnp.full((1, span), -jnp.inf, F32), jnp.zeros((1, span), F32), jnp.zeros((HD, span), F32)))
        inv = 1.0 / l
        gs_t[...] = go_ref[:, cols].astype(F32).T * (inv * scale)
        centre = jnp.sum(gs_t[...] * (o * inv), axis=0, keepdims=True)
        dqt[...] = jnp.zeros_like(dqt)

        def backward(i, carry):
            r = jnp.where(i < 2, i + 2, 3 - i)

            @pl.when(r <= fr)
            def _():
                f = jnp.exp2(mx[r] - m)
                gt = (gs_t[...] * f).astype(BF)
                g_rows[...] = (gs_t[...] * (f * (1.0 / scale))).T.astype(BF)
                k_t = kv[0, r, :, cols].astype(F32).T.astype(BF)
                p = probs[r]
                dp = dot_nn(kv[1, r, :, cols], gt)
                ds = (p.astype(F32) * (dp - centre * f)).astype(BF)
                send[r, h, 0] = dot_nn(ds, q_ref[:, cols]).astype(BF)
                send[r, h, 1] = dot_nn(p, g_rows[...]).astype(BF)
                dqt[...] += dot_nn(k_t, ds)

            for h_at in range(2):
                @pl.when((i == 0) & (fr >= 2) & (h == h_at))
                def _():
                    half_copy(h_at).start()

            @pl.when((i == 1) & (fr == 3) & (h == 0))
            def _():
                full_copy(1, 0).start()

            @pl.when((i == 1) & (fr == 3) & (h == 1))
            def _():
                add_half(1, 1)
                full_copy(1, 1).start()

            @pl.when((i == 2) & (fr == 3) & (h == 0))
            def _():
                full_copy(0, 0).start()

            @pl.when((i == 2) & (fr >= 1) & (h == 1))
            def _():
                full_copy(0, 1).start()

            @pl.when((i == 2) & ((fr == 1) | (fr == 2)) & (h == 1))
            def _():
                add_half(0, 0)
                full_copy(0, 0).start()

            return carry

        lax.fori_loop(0, 4, backward, 0)
        dq_ref[:, cols] = dqt[...].T.astype(BF)
        return carry

    lax.fori_loop(0, 2, head, 0)

    @pl.when(fr == 0)
    def _():
        half_copy(1).wait_recv()
        send[3, 1] = half_in[1]
        full_copy(1, 1).start()

    def take(side, h):
        full_copy(side, h).wait_recv()
        for j in range(2):
            send[0, h, j] = (send[0, h, j].astype(F32) + full_in[side, h, j].astype(F32)).astype(BF)

    @pl.when(fr <= 2)
    def _():
        take(0, 1)
        take(0, 0)

    @pl.when(fr == 0)
    def _():
        take(1, 0)

    @pl.when(fr <= 1)
    def _():
        take(1, 1)

    for h in range(2):
        cols = pl.ds(h * HD, HD)
        dk_ref[:, cols] = send[0, h, 0]
        dv_ref[:, cols] = send[0, h, 1]

    for h in range(2):
        @pl.when(fr >= 2)
        def _():
            half_copy(h).wait_send()

        @pl.when(fr >= 1)
        def _():
            full_copy(0, h).wait_send()

    @pl.when(fr == 3)
    def _():
        full_copy(1, 0).wait_send()

    @pl.when((fr == 3) | (fr == 0))
    def _():
        full_copy(1, 1).wait_send()


def attention_call(q, go, k, v, k_far, v_far):
    span, width = q.shape
    vm = pl.BlockSpec(memory_space=pltpu.VMEM)
    hbm = pl.BlockSpec(memory_space=pl.ANY)
    dma = pltpu.SemaphoreType.DMA
    return pl.pallas_call(
        attention_kernel,
        out_shape=(jax.ShapeDtypeStruct(q.shape, BF),) * 3,
        in_specs=[vm] * 2 + [hbm] * 4,
        out_specs=(vm,) * 3,
        scratch_shapes=[
            pltpu.VMEM((2, 4, span, width), BF),
            pltpu.VMEM((4, span, span), BF),
            pltpu.VMEM((HD, span), BF),
            pltpu.VMEM((4, 1, span), F32),
            pltpu.VMEM((HD, span), F32),
            pltpu.VMEM((span, HD), BF),
            pltpu.VMEM((HD, span), F32),
            pltpu.VMEM((4, 2, 2, span, HD), BF),
            pltpu.VMEM((2, 2, span, HD), BF),
            pltpu.VMEM((2, 2, 2, span, HD), BF),
            dma((2, 4)), dma((2,)), dma((2,)), dma((2, 2)), dma((2, 2)),
        ],
        compiler_params=pltpu.CompilerParams(
            collective_id=1, has_side_effects=True, vmem_limit_bytes=VMEM_LIMIT),
        cost_estimate=pl.CostEstimate(flops=10 * 10**9, bytes_accessed=20 * 10**6, transcendentals=0),
        name="attention",
    )(q, go, k, v, k_far, v_far)


def on_device(
    queries, keys, values, hidden_state, out_grad, stored_pre, expert_ids, gate_weights,
    w_gate, w_up, w_down,
):
    toks = out_grad.shape[0]
    meta = jnp.concatenate(
        [expert_ids.astype(F32).T, gate_weights.T, jnp.zeros((4, toks), F32)], axis=0)
    resid, go, k_far, v_far = moe_call(
        meta, out_grad, stored_pre.reshape(toks, -1), hidden_state,
        w_down[0], w_gate[0], w_up[0], keys, values)
    dq, dk, dv = attention_call(queries, go, keys, values, k_far, v_far)
    return resid, dq, dk, dv


def solution(mesh):
    rows = P(("dp", "frame"), "expert")
    toks = ("dp", "frame", "expert")
    return jax.shard_map(
        on_device,
        mesh=mesh,
        in_specs=(
            rows, rows, rows, P(toks, None), P(toks, None), P(toks, None, None, None),
            P(toks, None), P(toks, None), P("expert", None, "frame"), P("expert", None, "frame"),
            P("expert", "frame", None),
        ),
        out_specs=(P(toks, None), rows, rows, rows),
        check_vma=False,
    )
```

```python
import functools

import jax
import jax.numpy as jnp
from jax import lax
from jax.experimental import pallas as pl
from jax.experimental.pallas import tpu as pltpu
from jax.sharding import PartitionSpec as P

HD = 128
N_EXP = 8
N_FRAME = 4
MAIN = 16
BF = jnp.bfloat16
F32 = jnp.float32
MESH = pl.DeviceIdType.MESH
VMEM_LIMIT = 63 * 1024 * 1024


def dot_nn(a, b):
    return lax.dot_general(a, b, (((1,), (0,)), ((), ())), preferred_element_type=F32)


def dot_nt(a, b):
    return lax.dot_general(a, b, (((1,), (1,)), ((), ())), preferred_element_type=F32)


ZF = 2
RF = 1


def moe_kernel(
    meta_ref, og_ref, st_ref, hs_ref, wd_hbm, wg_hbm, wu_hbm, k_ref, v_ref,
    resid_ref, gout_ref, k_far, v_far,
    wd, wg, wu, rows, stored, hid, grads, ysend, yrecv, zrecv,
    half_in, full_in, dhalf_in, dfull_in, dense, amat, emat, atmat, etmat, raw, meta_in,
    w_sem, ys_sem, yr_sem, zs_sem, zr_sem, ag_s, ag_r, fw_s, fw_r, st_s, st_r,
    ha_s, ha_r, fu_s, fu_r, go_s, go_r, me_s, me_r, ra_s, ra_r, rf_s, rf_r,
    dh_s, dh_r, df_s, df_r, kv_s, kv_r,
):
    me = lax.axis_index("expert")
    fr = lax.axis_index("frame")
    left = lax.rem(fr + 3, 4)
    right = lax.rem(fr + 1, 4)
    opposite = lax.rem(fr + 2, 4)
    toks, width = og_ref.shape
    cw = width // 4
    ext = cw // 4
    ff = hid.shape[2]
    n_rows = rows.shape[2]
    half = n_rows // 2
    thalf = toks // 2
    n_blk = N_EXP * MAIN
    n_extra = 3 * ZF

    def chunk_at(c):
        return pl.ds(pl.multiple_of(c * cw, cw), cw)

    def to_frame(src, dst, ss, rs, dest):
        return pltpu.make_async_remote_copy(
            src_ref=src, dst_ref=dst, send_sem=ss, recv_sem=rs,
            device_id={"frame": dest}, device_id_type=MESH)

    def to_side(src, dst, ss, rs, side):
        return to_frame(src, dst, ss, rs, right if side == 0 else left)

    def to_expert(src, dst, ss, rs, dest):
        return pltpu.make_async_remote_copy(
            src_ref=src, dst_ref=dst, send_sem=ss, recv_sem=rs,
            device_id={"expert": dest}, device_id_type=MESH)

    barrier = pltpu.get_barrier_semaphore()
    for d in range(1, N_EXP):
        pl.semaphore_signal(barrier, inc=1, device_id={"expert": lax.rem(me + d, N_EXP)}, device_id_type=MESH)
    for dest in (left, right, opposite):
        pl.semaphore_signal(barrier, inc=1, device_id={"frame": dest}, device_id_type=MESH)

    w_copies = [pltpu.make_async_copy(wd_hbm.at[:, pl.ds(c * cw, cw)], wd.at[c], w_sem.at[c]) for c in range(4)]
    w_copies += [pltpu.make_async_copy(wg_hbm, wg, w_sem.at[4]), pltpu.make_async_copy(wu_hbm, wu, w_sem.at[5])]
    for copy in w_copies:
        copy.start()

    def raw_copy(c, side):
        return to_side(og_ref.at[:, chunk_at(c)], raw.at[side, c], ra_s.at[c, side], ra_r.at[c, side], side)

    def raw_pass(c, side):
        part = pl.ds(side * thalf, thalf)
        return to_side(raw.at[side, c, part], raw.at[2, c, part], rf_s.at[c, side], rf_r.at[c, side], side)

    meta_copies = [
        to_frame(meta_ref, meta_in.at[0], me_s.at[0], me_r.at[0], right),
        to_frame(meta_ref, meta_in.at[1], me_s.at[1], me_r.at[1], left),
        to_frame(meta_ref, meta_in.at[2], me_s.at[2], me_r.at[2], opposite),
    ]
    pl.semaphore_wait(barrier, N_EXP + 2)
    for copy in meta_copies:
        copy.start()
    for c in range(ZF):
        for side in range(2):
            raw_copy(c, side).start()

    earlier_mask = (
        lax.broadcasted_iota(jnp.int32, (toks, toks), 0) < lax.broadcasted_iota(jnp.int32, (toks, toks), 1)
    ).astype(F32).astype(BF)
    expert_iota = lax.broadcasted_iota(jnp.int32, (N_EXP, toks), 0)
    main_iota = lax.broadcasted_iota(jnp.int32, (2 * n_blk, toks), 0)
    ext_iota = lax.broadcasted_iota(jnp.int32, (n_blk, toks), 0)

    def routing(b, meta):
        base = jnp.zeros((N_EXP, 1), F32)
        main_sum = jnp.zeros(main_iota.shape, F32)
        ext_sum = [jnp.zeros(ext_iota.shape, F32) for _ in range(4)]
        for k in range(2):
            rel = (meta[k:k + 1, :].astype(jnp.int32) - me + N_EXP) & (N_EXP - 1)
            hit = (expert_iota == rel).astype(F32)
            earlier = dot_nn(hit.astype(BF), earlier_mask) + base
            slot = jnp.sum(hit * earlier, axis=0, keepdims=True).astype(jnp.int32)
            base = base + jnp.sum(hit, axis=1, keepdims=True)
            main_at = jnp.where(slot < 32, (slot >> 4) * n_blk + rel * MAIN + (slot & 15), -1)
            ext_at = jnp.where(slot < 32, -1000, rel * MAIN + slot - 32)
            main_k = (main_iota == main_at).astype(F32)
            amat[:, pl.ds(k * toks, toks)] = main_k.astype(BF)
            main_sum = main_sum + main_k
            for j in range(4):
                ext_k = (ext_iota == ext_at + 4 * j).astype(F32)
                emat[j, :, pl.ds(k * toks, toks)] = ext_k.astype(BF)
                ext_sum[j] = ext_sum[j] + ext_k
        atmat[b] = main_sum.T.astype(BF)
        for j in range(4):
            etmat[b, j] = ext_sum[j].T.astype(BF)
        return meta.T

    def pack_pairs(slot, at, pairs):
        main = dot_nn(amat[...], pairs).astype(BF)
        extra = dot_nn(emat[0], pairs[:, :ext])
        for j in range(1, 4):
            extra = extra + dot_nn(emat[j], pairs[:, j * ext:(j + 1) * ext])
        extra = extra.astype(BF)
        for lo, w, part in ((0, cw, main[:n_blk]), (cw, cw, main[n_blk:]), (2 * cw, ext, extra)):
            ysend[slot, :, pl.ds(lo, w)] = part
            yrecv[at, pl.ds(0, MAIN), pl.ds(lo, w)] = part[:MAIN]

    def pack_tokens(slot, at, x, weights):
        x = x.astype(F32)
        pack_pairs(slot, at, jnp.concatenate(
            [(weights[:, 2:3] * x).astype(BF), (weights[:, 3:4] * x).astype(BF)], axis=0))

    def y_copy(slot, at, d):
        return to_expert(
            ysend.at[slot, pl.ds(MAIN * d, MAIN)], yrecv.at[at, pl.ds(MAIN * d, MAIN)],
            ys_sem.at[at, d], yr_sem.at[at, d], lax.rem(me + d, N_EXP))

    def y_start(slot, at):
        for d in range(1, N_EXP):
            y_copy(slot, at, d).start()

    def y_sent(slot, at):
        for d in range(1, N_EXP):
            y_copy(slot, at, d).wait_send()

    own_weights = routing(0, meta_ref[...])

    def build_rows(i, carry):
        c = lax.rem(i + ZF, 4)
        pack_tokens(c, c, og_ref[:, chunk_at(c)], own_weights)
        y_start(c, c)
        return carry

    def build_stored(c, carry):
        f = lax.rem(fr + c, 4)
        parts = []
        for k in range(2):
            parts.append(jnp.concatenate(
                [st_ref[:, pl.ds(pl.multiple_of((k * 2 + kind) * 4 * ff + f * ff, ff), ff)] for kind in range(2)], axis=1))
        pack_pairs(4 + c, 4 + c, jnp.concatenate(parts, axis=0))
        y_start(4 + c, 4 + c)
        return carry

    lax.fori_loop(0, 4 - ZF, build_rows, 0)
    lax.fori_loop(0, 4, build_stored, 0)
    lax.fori_loop(4 - ZF, 4, build_rows, 0)

    sel_r = lax.broadcasted_iota(jnp.int32, (4 * N_EXP, n_blk), 0)
    sel_c = lax.broadcasted_iota(jnp.int32, (4 * N_EXP, n_blk), 1)
    selt_r = lax.broadcasted_iota(jnp.int32, (n_blk, 4 * N_EXP), 1)
    selt_c = lax.broadcasted_iota(jnp.int32, (n_blk, 4 * N_EXP), 0)

    def unpack(slot, at, dst):
        for d in range(1, N_EXP):
            y_copy(slot, at, d).wait_recv()
        dst[pl.ds(0, n_blk), :] = yrecv[at, :, pl.ds(0, cw)]
        dst[pl.ds(n_blk, n_blk), :] = yrecv[at, :, pl.ds(cw, cw)]
        extra = yrecv[at, :, pl.ds(2 * cw, ext)]
        for j in range(4):
            sel = (sel_c == (sel_r >> 2) * MAIN + 4 * j + (sel_r & 3)).astype(F32).astype(BF)
            dst[pl.ds(2 * n_blk, 4 * N_EXP), pl.ds(j * ext, ext)] = dot_nn(sel, extra).astype(BF)

    def ag_copy(c, side):
        return to_side(rows.at[0, c], rows.at[1 + side, c], ag_s.at[c, side], ag_r.at[c, side], side)

    def fw_copy(c, side):
        part = pl.ds(side * half, half)
        return to_side(rows.at[1 + side, c, part], rows.at[3, c, part], fw_s.at[c, side], fw_r.at[c, side], side)

    def add_hidden(b, c):
        hid[b] += dot_nt(rows[b, c], wd[c])

    for c in range(ZF):
        for side in range(2):
            raw_copy(c, side).wait_recv()
            raw_pass(c, side).start()

    def own_rows(c, carry):
        unpack(c, c, rows.at[0, c])
        ag_copy(c, 0).start()
        ag_copy(c, 1).start()
        return carry

    lax.fori_loop(ZF, 4, own_rows, 0)

    def extra_block(n):
        return lax.rem(n + 2, 3) + 1

    def extra_slot(i):
        return 2 + lax.rem(i, 6)

    for copy in meta_copies:
        copy.wait_recv()

    def dispatch(n, carry):
        b = extra_block(n)
        weights = routing(b, meta_in[b - 1])

        def one(c, carry):
            i = n * ZF + c

            @pl.when(n == 0)
            def _():
                for side in range(2):
                    raw_pass(c, side).wait_recv()

            slot = extra_slot(i)
            y_sent(slot, jnp.where(i < 6, slot, i + 2))
            pack_tokens(slot, 8 + i, raw[b - 1, c], weights)
            y_start(slot, 8 + i)
            return carry

        return lax.fori_loop(0, ZF, one, carry)

    lax.fori_loop(0, 1, dispatch, 0)

    hid[...] = jnp.zeros_like(hid)
    for copy in w_copies[:4]:
        copy.wait()

    def next_rows(c, carry):
        for side in range(2):
            ag_copy(c, side).wait_recv()
            fw_copy(c, side).start()

        def near(b, carry):
            add_hidden(b, c)
            return carry

        return lax.fori_loop(0, 3, near, carry)

    lax.fori_loop(ZF, 4, next_rows, 0)

    def own_stored(c, carry):
        unpack(4 + c, 4 + c, grads.at[c])
        return carry

    lax.fori_loop(0, 4, own_stored, 0)
    st_copies = [
        to_frame(grads.at[1], stored.at[0], st_s.at[0], st_r.at[0], right),
        to_frame(grads.at[3], stored.at[1], st_s.at[1], st_r.at[1], left),
        to_frame(grads.at[2], stored.at[2], st_s.at[2], st_r.at[2], opposite),
    ]
    for i in (2, 0, 1):
        st_copies[i].start()

    lax.fori_loop(1, 3, dispatch, 0)

    def far_rows(c, carry):
        for side in range(2):
            fw_copy(c, side).wait_recv()
        add_hidden(3, c)
        return carry

    lax.fori_loop(ZF, 4, far_rows, 0)

    def dispatched(i, carry):
        b = extra_block(i // ZF)
        c = lax.rem(i, ZF)
        unpack(extra_slot(i), 8 + i, rows.at[b, c])
        add_hidden(b, c)
        return carry

    lax.fori_loop(0, ZF, dispatched, 0)

    def kv_near(i, side):
        src, dst = ((k_ref, k_far), (v_ref, v_far))[i]
        return to_side(src, dst.at[2 * side], kv_s.at[i, side], kv_r.at[i, side], side)

    def kv_pass(i):
        dst = (k_far, v_far)[i]
        return to_side(dst.at[2 * i], dst.at[1], kv_s.at[i, 2], kv_r.at[i, 2], i)

    def hidden_to_grads(b, src):
        def some_rows(i, carry):
            at = pl.ds(pl.multiple_of(i * 32, 32), 32)
            h = hid[b, at, :]
            g = src[at, pl.ds(0, ff)].astype(F32)
            u = src[at, pl.ds(ff, ff)].astype(F32)
            s = 1.0 / (1.0 + jnp.exp(-g))
            gate = (h * u * s * (1.0 + g * (1.0 - s))).astype(BF)
            up = (h * g * s).astype(BF)
            grads[b, at, pl.ds(0, ff)] = gate
            grads[b, at, pl.ds(ff, ff)] = up
            return carry

        lax.fori_loop(0, n_rows // 32, some_rows, 0)

    st_copies[2].wait()
    st_copies[1].wait_send()
    hidden_to_grads(3, stored.at[2])
    for copy in w_copies[4:]:
        copy.wait()

    def term(b, c):
        at = chunk_at(c)
        return dot_nt(grads[b, :, pl.ds(0, ff)], wg[at, :]) + dot_nt(grads[b, :, pl.ds(ff, ff)], wu[at, :])

    def ha_copy(c, side):
        return to_side(rows.at[3, c, pl.ds(side * half, half)], half_in.at[side, c - RF],
                       ha_s.at[c, side], ha_r.at[c, side], side)

    def fu_copy(c, side):
        return to_side(rows.at[2 - side, c], full_in.at[side, c - RF], fu_s.at[c, side], fu_r.at[c, side], side)

    def z_copy(slot, d):
        return to_expert(
            ysend.at[slot, pl.ds(MAIN * d, MAIN)], zrecv.at[slot, pl.ds(MAIN * d, MAIN)],
            zs_sem.at[slot, d], zr_sem.at[slot, d], lax.rem(me + N_EXP - d, N_EXP))

    def send_back(slot, total):
        extra = jnp.zeros((n_blk, ext), F32)
        for j in range(4):
            sel = (selt_c == (selt_r >> 2) * MAIN + 4 * j + (selt_r & 3)).astype(F32).astype(BF)
            extra = extra + dot_nn(sel, total[2 * n_blk:, j * ext:(j + 1) * ext])
        extra = extra.astype(BF)
        for lo, w, part in ((0, cw, total[:n_blk]), (cw, cw, total[n_blk:2 * n_blk]), (2 * cw, ext, extra)):
            ysend[slot, :, pl.ds(lo, w)] = part
            zrecv[slot, pl.ds(0, MAIN), pl.ds(lo, w)] = part[:MAIN]
        for d in range(1, N_EXP):
            z_copy(slot, d).start()

    def far_terms(c, carry):
        rows[3, c] = term(3, c).astype(BF)
        for side in range(2):
            ha_copy(c, side).start()
        return carry

    lax.fori_loop(RF, 4, far_terms, 0)
    y_sent(0, 0)
    send_back(0, term(3, 0).astype(BF))

    @pl.when(fr <= 2)
    def _():
        kv_near(0, 0).start()

    @pl.when(fr == 0)
    def _():
        kv_near(0, 1).start()

    def own_dispatched(c, carry):
        unpack(c, c, rows.at[0, c])
        add_hidden(0, c)
        return carry

    lax.fori_loop(0, ZF, own_dispatched, 0)
    lax.fori_loop(ZF, n_extra, dispatched, 0)
    st_copies[0].wait()
    st_copies[1].wait_recv()

    def near_grads(i, carry):
        hidden_to_grads(2 - i, stored.at[1 - i])
        return carry

    lax.fori_loop(0, 2, near_grads, 0)
    hidden_to_grads(0, grads.at[0])

    def settle(i, carry):
        y_sent(i, i)
        return carry

    def settle_extra(i, carry):
        y_sent(extra_slot(i), 8 + i)
        return carry

    lax.fori_loop(1, 2, settle, 0)
    lax.fori_loop(2 + min(n_extra, 6), 8, settle, 0)
    lax.fori_loop(max(n_extra - 6, 0), n_extra, settle_extra, 0)

    def tokens_of(slot, b):
        for d in range(1, N_EXP):
            z_copy(slot, d).wait_recv()
        got = dot_nn(atmat[b, :, pl.ds(0, n_blk)], zrecv[slot, :, pl.ds(0, cw)])
        got = got + dot_nn(atmat[b, :, pl.ds(n_blk, n_blk)], zrecv[slot, :, pl.ds(cw, cw)])
        extra = zrecv[slot, :, pl.ds(2 * cw, ext)]
        return got + jnp.concatenate([dot_nn(etmat[b, j], extra) for j in range(4)], axis=1)

    def near_terms(i, carry):
        c = RF + i // 2
        side = lax.rem(i, 2)

        def block(side):
            @pl.when(c >= ZF)
            def _():
                fw_copy(c, 1 - side).wait_send()

        for side_at in range(2):
            @pl.when(side == side_at)
            def _():
                block(side_at)

        rows[2 - side, c] = term(2 - side, c).astype(BF)
        for side_at in range(2):
            @pl.when(side == side_at)
            def _():
                part = pl.ds(side_at * half, half)
                ha_copy(c, side_at).wait_recv()
                rows[2 - side_at, c, part] = (
                    rows[2 - side_at, c, part].astype(F32) + half_in[side_at, c - RF].astype(F32)).astype(BF)
                fu_copy(c, side_at).start()
        return carry

    def near_and_back(j, carry):
        lax.fori_loop(2 * j, 2 * j + 2, near_terms, 0)
        send_back(6 - j, term(2 - j, 0).astype(BF))
        return carry

    lax.fori_loop(0, 3, near_and_back, 0)

    def put_moe(c, got):
        hid[c, pl.ds(0, toks), :] = got[:, :cw // 2]
        hid[c, pl.ds(toks, toks), :] = got[:, cw // 2:]

    def get_moe(c):
        return jnp.concatenate([hid[c, pl.ds(0, toks), :], hid[c, pl.ds(toks, toks), :]], axis=1)

    def dh_copy(c, side):
        part = pl.ds(side * thalf, thalf)
        return to_side(dense.at[c, 2, part], dhalf_in.at[side, c], dh_s.at[c, side], dh_r.at[c, side], side)

    def df_copy(c, side):
        return to_side(dense.at[c, 1 - side], dfull_in.at[side, c], df_s.at[c, side], df_r.at[c, side], side)

    for c in range(RF):
        dense[c, 2] = tokens_of(0, 3).astype(BF)
        for side in range(2):
            dh_copy(c, side).start()
        for side in range(2):
            b = 2 - side
            dense[c, b - 1] = tokens_of(4 + 4 * c + b, b).astype(BF)
        for side in range(2):
            b = 2 - side
            part = pl.ds(side * thalf, thalf)
            dh_copy(c, side).wait_recv()
            dense[c, b - 1, part] = (
                dense[c, b - 1, part].astype(F32) + dhalf_in[side, c].astype(F32)).astype(BF)
            df_copy(c, side).start()
        put_moe(c, tokens_of(4 + 4 * c, 0))

    @pl.when(fr >= 1)
    def _():
        kv_near(0, 0).wait_recv()

    @pl.when((fr == 1) | (fr == 2))
    def _():
        kv_pass(0).start()

    @pl.when(fr <= 2)
    def _():
        kv_near(1, 0).start()

    @pl.when(fr <= 1)
    def _():
        kv_near(1, 1).start()

    def own_terms(c, carry):
        part = term(0, c).astype(BF).astype(F32)
        for side in range(2):
            fu_copy(c, side).wait_recv()
        send_back(c, (part + full_in[0, c - RF].astype(F32) + full_in[1, c - RF].astype(F32)).astype(BF))
        return carry

    lax.fori_loop(RF, 4, own_terms, 0)

    @pl.when((fr == 3) | (fr == 0))
    def _():
        kv_near(1, 1).wait_recv()
        kv_pass(1).start()

    def square_sum(c, acc):
        x = hs_ref[:, chunk_at(c)].astype(F32)
        return acc + jnp.sum(x * x, axis=1, keepdims=True)

    inv = lax.rsqrt(lax.fori_loop(0, 4, square_sum, jnp.zeros((toks, 1), F32)) / width + 1e-6)

    def combine(c, acc):
        got = tokens_of(c, 0)
        put_moe(c, got)
        return acc + jnp.sum(got * hs_ref[:, chunk_at(c)].astype(F32), axis=1, keepdims=True)

    mean = lax.fori_loop(RF, 4, combine, jnp.zeros((toks, 1), F32))
    for c in range(RF):
        at = pl.ds(c * cw, cw)
        got = get_moe(c)
        for side in range(2):
            df_copy(c, side).wait_recv()
            got = got + dfull_in[side, c].astype(F32)
        put_moe(c, got)
        mean = mean + jnp.sum(got * hs_ref[:, at].astype(F32), axis=1, keepdims=True)
    mean = mean * inv / width

    def residual(c, carry):
        at = chunk_at(c)
        n = hs_ref[:, at].astype(F32) * inv
        resid_ref[:, at] = (og_ref[:, at].astype(F32) + inv * (get_moe(c) - n * mean)).astype(BF)
        return carry

    hw = gout_ref.shape[1]
    own_at = pl.ds(pl.multiple_of(me * toks, toks), toks)

    def go_copy(d):
        dest = lax.rem(me + d, N_EXP)
        return to_expert(
            resid_ref.at[:, pl.ds(pl.multiple_of(dest * hw, hw), hw)], gout_ref.at[own_at],
            go_s.at[d], go_r.at[d], dest)

    lax.fori_loop(0, 2, residual, 0)
    for d in range(1, N_EXP):
        go_copy(d).start()
    gout_ref[own_at, :] = resid_ref[:, pl.ds(pl.multiple_of(me * hw, hw), hw)]
    lax.fori_loop(2, 4, residual, 0)

    @pl.when(fr <= 2)
    def _():
        kv_near(0, 0).wait_send()
        kv_near(1, 0).wait_send()

    @pl.when(fr == 0)
    def _():
        kv_near(0, 1).wait_send()

    @pl.when(fr <= 1)
    def _():
        kv_near(1, 1).wait_send()

    @pl.when((fr == 1) | (fr == 2))
    def _():
        kv_pass(0).wait_send()

    @pl.when((fr == 3) | (fr == 0))
    def _():
        kv_pass(1).wait_send()

    @pl.when(fr >= 1)
    def _():
        kv_near(1, 0).wait_recv()

    @pl.when(fr == 3)
    def _():
        kv_near(0, 1).wait_recv()

    @pl.when(fr >= 2)
    def _():
        kv_pass(0).wait_recv()
        kv_pass(1).wait_recv()

    for copy in meta_copies:
        copy.wait_send()
    for c in range(ZF):
        for side in range(2):
            raw_copy(c, side).wait_send()
            raw_pass(c, side).wait_send()
    for c in range(RF):
        for side in range(2):
            dh_copy(c, side).wait_send()
            df_copy(c, side).wait_send()

    def drain(c, carry):
        for side in range(2):
            ag_copy(c, side).wait_send()
        return carry

    def drain_back(c, carry):
        for side in range(2):
            ha_copy(c, side).wait_send()
            fu_copy(c, side).wait_send()
        return carry

    def drain_z(slot, carry):
        for d in range(1, N_EXP):
            z_copy(slot, d).wait_send()
        return carry

    lax.fori_loop(ZF, 4, drain, 0)
    lax.fori_loop(RF, 4, drain_back, 0)
    lax.fori_loop(0, 7, drain_z, 0)
    for c in range(ZF, RF):
        for side in range(2):
            fw_copy(c, side).wait_send()
    for d in range(1, N_EXP):
        go_copy(d).wait()


def moe_call(meta, out_grad, stored, hidden_state, wd, wg, wu, keys, values):
    toks, width = out_grad.shape
    ff = wd.shape[0]
    cw = width // 4
    n_rows = N_EXP * 36
    n_blk = N_EXP * MAIN
    pw = 2 * cw + cw // 4
    vm = pl.BlockSpec(memory_space=pltpu.VMEM)
    hbm = pl.BlockSpec(memory_space=pl.ANY)
    dma = pltpu.SemaphoreType.DMA
    slots = 8 + 3 * ZF
    back = 7
    rf = max(RF, 1)
    zf = max(ZF, 1)
    return pl.pallas_call(
        moe_kernel,
        out_shape=(
            jax.ShapeDtypeStruct((toks, width), BF),
            jax.ShapeDtypeStruct(keys.shape, BF),
            jax.ShapeDtypeStruct((3,) + keys.shape, BF),
            jax.ShapeDtypeStruct((3,) + keys.shape, BF),
        ),
        in_specs=[vm] * 4 + [hbm] * 3 + [vm] * 2,
        out_specs=(vm, vm, hbm, hbm),
        scratch_shapes=[
            pltpu.VMEM((4, ff, cw), BF),
            pltpu.VMEM((width, ff), BF),
            pltpu.VMEM((width, ff), BF),
            pltpu.VMEM((4, 4, n_rows, cw), BF),
            pltpu.VMEM((3, n_rows, 2 * ff), BF),
            pltpu.VMEM((4, n_rows, ff), F32),
            pltpu.VMEM((4, n_rows, 2 * ff), BF),
            pltpu.VMEM((8, n_blk, pw), BF),
            pltpu.VMEM((slots, n_blk, pw), BF),
            pltpu.VMEM((back, n_blk, pw), BF),
            pltpu.VMEM((2, 4 - RF, n_rows // 2, cw), BF),
            pltpu.VMEM((2, 4 - RF, n_rows, cw), BF),
            pltpu.VMEM((2, rf, toks // 2, cw), BF),
            pltpu.VMEM((2, rf, toks, cw), BF),
            pltpu.VMEM((rf, 3, toks, cw), BF),
            pltpu.VMEM((2 * n_blk, 2 * toks), BF),
            pltpu.VMEM((4, n_blk, 2 * toks), BF),
            pltpu.VMEM((4, toks, 2 * n_blk), BF),
            pltpu.VMEM((4, 4, toks, n_blk), BF),
            pltpu.VMEM((3, zf, toks, cw), BF),
            pltpu.VMEM((3, 8, toks), F32),
            dma((6,)), dma((slots, 8)), dma((slots, 8)), dma((back, 8)), dma((back, 8)),
            dma((4, 2)), dma((4, 2)), dma((4, 2)), dma((4, 2)), dma((3,)), dma((3,)),
            dma((4, 2)), dma((4, 2)), dma((4, 2)), dma((4, 2)), dma((8,)), dma((8,)),
            dma((3,)), dma((3,)), dma((zf, 2)), dma((zf, 2)), dma((zf, 2)), dma((zf, 2)),
            dma((rf, 2)), dma((rf, 2)), dma((rf, 2)), dma((rf, 2)), dma((2, 3)), dma((2, 3)),
        ],
        compiler_params=pltpu.CompilerParams(
            collective_id=0, has_side_effects=True, vmem_limit_bytes=VMEM_LIMIT),
        cost_estimate=pl.CostEstimate(flops=15 * 10**9, bytes_accessed=20 * 10**6, transcendentals=0),
        name="moe",
    )(meta, out_grad, stored, hidden_state, wd, wg, wu, keys, values)


def attention_kernel(
    q_ref, go_ref, k_hbm, v_hbm, k_far, v_far, dq_ref, dk_ref, dv_ref,
    kv, probs, qt, mx, gs_t, g_rows, dqt, send, half_in, full_in,
    kv_sem, hs, hr, fs, fr_sem,
):
    fr = lax.axis_index("frame")
    left = lax.rem(fr + 3, 4)
    right = lax.rem(fr + 1, 4)
    span = q_ref.shape[0]
    scale = HD ** -0.5
    log2e = 1.4426950408889634

    def load(i, r):
        src = (k_hbm, v_hbm)[i] if isinstance(r, int) else (k_far, v_far)[i].at[r - 1]
        return pltpu.make_async_copy(src, kv.at[i, r], kv_sem.at[i, r])

    for i in range(2):
        load(i, 0).start()

    def load_far(r, carry):
        for i in range(2):
            load(i, r).start()
        return carry

    lax.fori_loop(1, fr + 1, load_far, 0)

    barrier = pltpu.get_barrier_semaphore()
    for dest in (left, right):
        pl.semaphore_signal(barrier, inc=1, device_id={"frame": dest}, device_id_type=MESH)
    pl.semaphore_wait(barrier, 2)

    def to_frame(src, dst, ss, rs, dest):
        return pltpu.make_async_remote_copy(
            src_ref=src, dst_ref=dst, send_sem=ss, recv_sem=rs,
            device_id={"frame": dest}, device_id_type=MESH)

    def half_copy(h):
        return to_frame(send.at[2, h], half_in.at[h], hs.at[h], hr.at[h], left if h == 0 else right)

    def full_copy(side, h):
        return to_frame(send.at[1 + 2 * side, h], full_in.at[side, h], fs.at[side, h], fr_sem.at[side, h],
                        left if side == 0 else right)

    def add_half(side, h):
        half_copy(h).wait_recv()
        for j in range(2):
            send[1 + 2 * side, h, j] = (
                send[1 + 2 * side, h, j].astype(F32) + half_in[h, j].astype(F32)).astype(BF)

    for i in range(2):
        load(i, 0).wait()

    def head(h, carry):
        cols = pl.ds(pl.multiple_of(h * HD, HD), HD)
        qt[...] = q_ref[:, cols].astype(F32).T.astype(BF)

        def forward(r, carry):
            @pl.when((r >= 1) & (h == 0))
            def _():
                for i in range(2):
                    load(i, r).wait()

            m, l, o = carry
            v_t = kv[1, r, :, cols].astype(F32).T.astype(BF)
            sc = dot_nn(kv[0, r, :, cols], qt[...])
            m_new = jnp.maximum(m, jnp.max(sc, axis=0, keepdims=True) * (scale * log2e))
            old = jnp.exp2(m - m_new)
            p = jnp.exp2(sc * (scale * log2e) - m_new)
            low = p.astype(BF)
            probs[r] = low
            mx[r] = m_new
            return m_new, l * old + jnp.sum(p, axis=0, keepdims=True), o * old + dot_nn(v_t, low)

        m, l, o = lax.fori_loop(0, fr + 1, forward, (
            jnp.full((1, span), -jnp.inf, F32), jnp.zeros((1, span), F32), jnp.zeros((HD, span), F32)))
        inv = 1.0 / l
        gs_t[...] = go_ref[:, cols].astype(F32).T * (inv * scale)
        centre = jnp.sum(gs_t[...] * (o * inv), axis=0, keepdims=True)
        dqt[...] = jnp.zeros_like(dqt)

        def backward(i, carry):
            r = jnp.where(i < 2, i + 2, 3 - i)

            @pl.when(r <= fr)
            def _():
                f = jnp.exp2(mx[r] - m)
                gt = (gs_t[...] * f).astype(BF)
                g_rows[...] = (gs_t[...] * (f * (1.0 / scale))).T.astype(BF)
                k_t = kv[0, r, :, cols].astype(F32).T.astype(BF)
                p = probs[r]
                dp = dot_nn(kv[1, r, :, cols], gt)
                ds = (p.astype(F32) * (dp - centre * f)).astype(BF)
                send[r, h, 0] = dot_nn(ds, q_ref[:, cols]).astype(BF)
                send[r, h, 1] = dot_nn(p, g_rows[...]).astype(BF)
                dqt[...] += dot_nn(k_t, ds)

            for h_at in range(2):
                @pl.when((i == 0) & (fr >= 2) & (h == h_at))
                def _():
                    half_copy(h_at).start()

            @pl.when((i == 1) & (fr == 3) & (h == 0))
            def _():
                full_copy(1, 0).start()

            @pl.when((i == 1) & (fr == 3) & (h == 1))
            def _():
                add_half(1, 1)
                full_copy(1, 1).start()

            @pl.when((i == 2) & (fr == 3) & (h == 0))
            def _():
                full_copy(0, 0).start()

            @pl.when((i == 2) & (fr >= 1) & (h == 1))
            def _():
                full_copy(0, 1).start()

            @pl.when((i == 2) & ((fr == 1) | (fr == 2)) & (h == 1))
            def _():
                add_half(0, 0)
                full_copy(0, 0).start()

            return carry

        lax.fori_loop(0, 4, backward, 0)
        dq_ref[:, cols] = dqt[...].T.astype(BF)
        return carry

    lax.fori_loop(0, 2, head, 0)

    @pl.when(fr == 0)
    def _():
        half_copy(1).wait_recv()
        send[3, 1] = half_in[1]
        full_copy(1, 1).start()

    def take(side, h):
        full_copy(side, h).wait_recv()
        for j in range(2):
            send[0, h, j] = (send[0, h, j].astype(F32) + full_in[side, h, j].astype(F32)).astype(BF)

    @pl.when(fr <= 2)
    def _():
        take(0, 1)
        take(0, 0)

    @pl.when(fr == 0)
    def _():
        take(1, 0)

    @pl.when(fr <= 1)
    def _():
        take(1, 1)

    for h in range(2):
        cols = pl.ds(h * HD, HD)
        dk_ref[:, cols] = send[0, h, 0]
        dv_ref[:, cols] = send[0, h, 1]

    for h in range(2):
        @pl.when(fr >= 2)
        def _():
            half_copy(h).wait_send()

        @pl.when(fr >= 1)
        def _():
            full_copy(0, h).wait_send()

    @pl.when(fr == 3)
    def _():
        full_copy(1, 0).wait_send()

    @pl.when((fr == 3) | (fr == 0))
    def _():
        full_copy(1, 1).wait_send()


def attention_call(q, go, k, v, k_far, v_far):
    span, width = q.shape
    vm = pl.BlockSpec(memory_space=pltpu.VMEM)
    hbm = pl.BlockSpec(memory_space=pl.ANY)
    dma = pltpu.SemaphoreType.DMA
    return pl.pallas_call(
        attention_kernel,
        out_shape=(jax.ShapeDtypeStruct(q.shape, BF),) * 3,
        in_specs=[vm] * 2 + [hbm] * 4,
        out_specs=(vm,) * 3,
        scratch_shapes=[
            pltpu.VMEM((2, 4, span, width), BF),
            pltpu.VMEM((4, span, span), BF),
            pltpu.VMEM((HD, span), BF),
            pltpu.VMEM((4, 1, span), F32),
            pltpu.VMEM((HD, span), F32),
            pltpu.VMEM((span, HD), BF),
            pltpu.VMEM((HD, span), F32),
            pltpu.VMEM((4, 2, 2, span, HD), BF),
            pltpu.VMEM((2, 2, span, HD), BF),
            pltpu.VMEM((2, 2, 2, span, HD), BF),
            dma((2, 4)), dma((2,)), dma((2,)), dma((2, 2)), dma((2, 2)),
        ],
        compiler_params=pltpu.CompilerParams(
            collective_id=1, has_side_effects=True, vmem_limit_bytes=VMEM_LIMIT),
        cost_estimate=pl.CostEstimate(flops=10 * 10**9, bytes_accessed=20 * 10**6, transcendentals=0),
        name="attention",
    )(q, go, k, v, k_far, v_far)


def on_device(
    queries, keys, values, hidden_state, out_grad, stored_pre, expert_ids, gate_weights,
    w_gate, w_up, w_down,
):
    toks = out_grad.shape[0]
    meta = jnp.concatenate(
        [expert_ids.astype(F32).T, gate_weights.T, jnp.zeros((4, toks), F32)], axis=0)
    resid, go, k_far, v_far = moe_call(
        meta, out_grad, stored_pre.reshape(toks, -1), hidden_state,
        w_down[0], w_gate[0], w_up[0], keys, values)
    dq, dk, dv = attention_call(queries, go, keys, values, k_far, v_far)
    return resid, dq, dk, dv


def solution(mesh):
    rows = P(("dp", "frame"), "expert")
    toks = ("dp", "frame", "expert")
    return jax.shard_map(
        on_device,
        mesh=mesh,
        in_specs=(
            rows, rows, rows, P(toks, None), P(toks, None), P(toks, None, None, None),
            P(toks, None), P(toks, None), P("expert", None, "frame"), P("expert", None, "frame"),
            P("expert", "frame", None),
        ),
        out_specs=(P(toks, None), rows, rows, rows),
        check_vma=False,
    )
```
